32 devices in a mesh: rep: 8 (over y, x, core), exp: 4 (over z).
Axes of the slice: x: 2, y: 2, z: 4, core: 2. Of those that a mesh axis runs over, the one named last changes fastest.
Arguments:
- activations: bfloat16 [8192, 3072], P('rep', 'exp'), may hold values from -6 to 6
- kv_grad: bfloat16 [8192, 1024], P('rep'), may hold values from -0.1875 to 0.1875
- errors: bfloat16 [8, 3072, 1024], P('rep', 'exp'), may hold values from -6 to 6
- right_factor: float32 [1024, 64], replicated, may hold values from -6 to 6
- hidden: bfloat16 [8, 512, 768], P('rep', 'exp'), may hold values from -6 to 6
- out_grad: bfloat16 [8, 512, 2048], P('rep', 'exp'), may hold values from -0.25 to 0.25
- moment_one: float32 [8, 768, 2048], P('rep', 'exp'), may hold values from -4 to 4
- moment_two: float32 [8, 768, 2048], P('rep', 'exp'), may hold values from 0.05 to 1
Outputs:
- new_error: bfloat16 [8, 3072, 1024], P('rep', 'exp')
- new_right: float32 [1024, 64], replicated
- new_moment_one: float32 [8, 768, 2048], P('rep', 'exp')
- new_moment_two: float32 [8, 768, 2048], P('rep', 'exp')
- update: bfloat16 [8, 768, 2048], P('rep', 'exp')
The draws below stay inside these ranges and needn't reach their ends.
All inputs are finite; a program needn't handle non-finite values.
Results may differ from the reference program's by a relative error of at most 0.006.
Values may be sent and summed in bfloat16 or wider, within the bound.
No kernel may reach another device: no remote copies, remote signals or barrier semaphores. Data moves between devices by JAX's collectives and lax.ppermute only.
A program may use at most 64 MiB of HBM per device.

```python
import math
import jax
import jax.numpy as jnp
from jax import lax

DD = 3072
KV = 1024
RANK = 64
TOK_DEV = 1024
REPLICAS = 8
TOKENS = 8192
FFE = 768
DW = 2048
TOK_EXP = 128
GROUP = 4
EXPERTS = 8


def shard_levels(rng, shape, cuts, least, largest):
    def one(dim, parts):
        draws = jax.random.uniform(jax.random.fold_in(jax.random.fold_in(rng, 6), dim), (parts,), jnp.float32, least / len(cuts), largest / len(cuts))
        return jnp.repeat(jnp.exp(draws), shape[dim] // parts).reshape((-1,) + (1,) * (len(shape) - dim - 1))

    gain = one(*cuts[0])
    for cut in cuts[1:]:
        gain = gain * one(*cut)
    return gain


def centred(key, shape, scale, bound, cuts=(), held_as=jnp.bfloat16):
    array = scale * jax.random.normal(key, shape, jnp.float32)
    if cuts:
        array = array * shard_levels(key, shape, cuts, -0.22, 0.18)
    return jnp.clip(array, -bound, bound).astype(held_as)


def setup_inputs(seed: int = 0) -> dict:
    seeds = jax.random.split(jax.random.key(seed), 9)
    activations = centred(seeds[0], (TOKENS, DD), 1.0, 6.0, ((0, 8), (1, 4)))
    kv_grad = centred(seeds[1], (TOKENS, KV), TOK_DEV ** -0.5, 0.1875, ((0, 8),))
    errors = centred(seeds[2], (REPLICAS, DD, KV), 1.0, 6.0, ((0, 8), (1, 4)))
    right_factor = centred(seeds[3], (KV, RANK), 1.0, 6.0, (), jnp.float32)
    hidden = centred(seeds[4], (EXPERTS, TOK_EXP * GROUP, FFE), 1.0, 6.0, ((0, 8), (1, 4)))
    out_grad = centred(seeds[5], (EXPERTS, TOK_EXP * GROUP, DW), (TOK_EXP * GROUP) ** -0.5, 0.25, ((0, 8), (1, 4)))
    moment_one = centred(seeds[6], (EXPERTS, FFE, DW), 0.3, 4.0, ((0, 8), (1, 4)), jnp.float32)
    moment_two = jnp.clip(jnp.exp(math.log(1.0) - 2.9957323 * jax.random.uniform(seeds[7], (EXPERTS, FFE, DW), jnp.float32) ** shard_levels(seeds[7], (EXPERTS, FFE, DW), ((0, 8), (1, 4)), -0.2, 0.2)), 0.05, 1.0)
    return dict(activations=activations, kv_grad=kv_grad, errors=errors, right_factor=right_factor, hidden=hidden, out_grad=out_grad, moment_one=moment_one, moment_two=moment_two)


HIGHEST = lax.Precision.HIGHEST
beta_one = 0.9
beta_two = 0.99
correction_one = 1.0 - 0.9 ** 10
correction_two = 1.0 - 0.99 ** 10
epsilon = 1e-08

def apply_inverse(lower, matrix):
    return lax.linalg.triangular_solve(lower, matrix, left_side=False, lower=True, transpose_a=True)

def form_merged(pieces):
    acts_block, grad_block, error_block = pieces
    product = lax.dot_general(acts_block.astype(jnp.float32), grad_block.astype(jnp.float32), (((0,), (0,)), ((), ())), preferred_element_type=jnp.float32)
    return product + error_block.astype(jnp.float32)

def expert_step(pieces):
    hidden_block, grad_block, first, second = pieces
    hidden_split = hidden_block.reshape(GROUP, TOK_EXP, FFE).astype(jnp.float32)
    grad_split = grad_block.reshape(GROUP, TOK_EXP, DW).astype(jnp.float32)
    expert_partial = jnp.einsum('gtf,gtd->gfd', hidden_split, grad_split, precision=HIGHEST).astype(jnp.bfloat16)
    expert_grad = lax.optimization_barrier(jnp.sum(expert_partial.astype(jnp.float32), axis=0))
    first_new = beta_one * first + (1.0 - beta_one) * expert_grad
    second_new = beta_two * second + (1.0 - beta_two) * expert_grad * expert_grad
    step_dir = first_new / correction_one / (jnp.sqrt(second_new / correction_two) + epsilon)
    return (first_new, second_new, step_dir.astype(jnp.bfloat16))

def reference(activations, kv_grad, errors, right_factor, hidden, out_grad, moment_one, moment_two):
    acts_split = activations.reshape(REPLICAS, TOK_DEV, DD)
    grad_split = kv_grad.reshape(REPLICAS, TOK_DEV, KV)
    merged = lax.map(form_merged, (acts_split, grad_split, errors))
    summed = lax.optimization_barrier(jnp.sum(merged, axis=0))
    left_factor = jnp.dot(summed, right_factor, precision=HIGHEST)
    gram_matrix = jnp.dot(left_factor.T, left_factor, precision=HIGHEST)
    lower_factor = jnp.linalg.cholesky(gram_matrix)
    basis_left = apply_inverse(lower_factor, left_factor)
    new_right = jnp.dot(summed.T, basis_left, precision=HIGHEST) / REPLICAS
    approx = jnp.dot(basis_left, new_right.T, precision=HIGHEST)
    new_error = (merged - approx[None]).astype(jnp.bfloat16)
    new_moment_one, new_moment_two, update = lax.map(expert_step, (hidden, out_grad, moment_one, moment_two))
    return (new_error, new_right, new_moment_one, new_moment_two, update)
```

```python
import functools

import jax
import jax.numpy as jnp
from jax import lax
from jax.experimental import pallas as pl
from jax.experimental.pallas import tpu as pltpu
from jax.sharding import PartitionSpec as P

HIGHEST = lax.Precision.HIGHEST
F32 = jnp.float32
BF16 = jnp.bfloat16
beta_one = 0.9
beta_two = 0.99
correction_one = 1.0 - 0.9**10
correction_two = 1.0 - 0.99**10
epsilon = 1e-08

ROWS_FIRST = (((0,), (0,)), ((), ()))
COLS_LAST = (((1,), (1,)), ((), ()))
TILE_R, TILE_C = 16, 128
VMEM_LIMIT = 40 * 1024 * 1024


def params():
    return pltpu.CompilerParams(vmem_limit_bytes=VMEM_LIMIT)


def cost(flops, nbytes):
    return pl.CostEstimate(flops=int(flops), bytes_accessed=int(nbytes), transcendentals=0)


def split_two(x):
    hi = x.astype(BF16)
    return hi, (x - hi.astype(F32)).astype(BF16)


def left_times(left, right_bf16, dims):
    rows = left.shape[0]
    hi, lo = split_two(left)
    both = jnp.concatenate([hi, lo], axis=0)
    out = lax.dot_general(both, right_bf16, dims, preferred_element_type=F32)
    return out[:rows] + out[rows:]


def merge_kernel(acts_ref, kv_ref, err_ref, vt_ref, merged_ref, lt_ref):
    merged = lax.dot_general(acts_ref[...], kv_ref[...], ROWS_FIRST, preferred_element_type=F32)
    merged = merged + err_ref[0].astype(F32)
    merged_ref[...] = merged
    lt_ref[...] = left_times(vt_ref[...], merged.astype(BF16), COLS_LAST)


def merge(acts, kv, err, vt):
    tokens, rows = acts.shape
    cols = kv.shape[1]
    rank = vt.shape[0]
    block = 256
    return pl.pallas_call(
        merge_kernel,
        grid=(rows // block,),
        in_specs=[
            pl.BlockSpec((tokens, block), lambda i: (0, i)),
            pl.BlockSpec((tokens, cols), lambda i: (0, 0)),
            pl.BlockSpec((1, block, cols), lambda i: (0, i, 0)),
            pl.BlockSpec((rank, cols), lambda i: (0, 0)),
        ],
        out_specs=[
            pl.BlockSpec((block, cols), lambda i: (i, 0)),
            pl.BlockSpec((rank, block), lambda i: (0, i)),
        ],
        out_shape=[
            jax.ShapeDtypeStruct((rows, cols), F32),
            jax.ShapeDtypeStruct((rank, rows), F32),
        ],
        compiler_params=params(),
        cost_estimate=cost(2 * tokens * rows * cols, 2 * tokens * (rows + cols) + 6 * rows * cols),
        name="merge",
    )(acts, kv, err, vt)


def right_kernel(parts_ref, merged_ref, lt_ref, gram_ref, chunk_ref):
    parts = [parts_ref[i].astype(F32) for i in range(parts_ref.shape[0])]
    while len(parts) > 1:
        parts = [a + b for a, b in zip(parts[0::2], parts[1::2])]
    lt = parts[0]
    rank = lt.shape[0]
    lt_ref[...] = lt
    gram = lax.dot_general(lt, lt, COLS_LAST, precision=HIGHEST, preferred_element_type=F32)
    gram_ref[...] = jnp.concatenate([gram, jnp.zeros_like(gram)], axis=1)
    product = left_times(lt, merged_ref[...].astype(BF16), (((1,), (0,)), ((), ()))).astype(BF16)
    across = product.shape[1] // TILE_C
    for a in range(rank // TILE_R):
        for b in range(across):
            chunk_ref[a * across + b] = product[
                a * TILE_R : (a + 1) * TILE_R, b * TILE_C : (b + 1) * TILE_C
            ]


def right_product(parts, merged):
    _, rank, rows = parts.shape
    cols = merged.shape[1]
    chunks = rank * cols // (TILE_R * TILE_C)
    return pl.pallas_call(
        right_kernel,
        out_shape=[
            jax.ShapeDtypeStruct((rank, rows), F32),
            jax.ShapeDtypeStruct((rank, 2 * rank), F32),
            jax.ShapeDtypeStruct((chunks, TILE_R, TILE_C), BF16),
        ],
        compiler_params=params(),
        cost_estimate=cost(2 * rows * cols * 128, 4 * rows * cols),
        name="right_product",
    )(parts, merged)


def inverse_kernel(gram_ref, w_ref):
    parts = [gram_ref[i] for i in range(gram_ref.shape[0])]
    while len(parts) > 1:
        parts = [a + b for a, b in zip(parts[0::2], parts[1::2])]
    rank, width = parts[0].shape
    row = lax.broadcasted_iota(jnp.int32, (rank, width), 0)
    col = lax.broadcasted_iota(jnp.int32, (rank, width), 1)
    a = parts[0] + jnp.where(col == row + rank, 1.0, 0.0).astype(F32)
    row_ids = lax.broadcasted_iota(jnp.int32, (rank, 1), 0)
    for k in range(rank):
        pivot_row = a[k : k + 1, :]
        pivot = pivot_row[:, k : k + 1]
        w_ref[k : k + 1, :] = pivot_row[:, rank:] * lax.rsqrt(pivot)
        if k + 1 < rank:
            factor = jnp.where(row_ids > k, a[:, k : k + 1] / pivot, 0.0)
            a = a - factor * pivot_row


def inverse_factor(gram_parts):
    rank = gram_parts.shape[1]
    return pl.pallas_call(
        inverse_kernel,
        out_shape=jax.ShapeDtypeStruct((rank, rank), F32),
        compiler_params=params(),
        cost_estimate=cost(4e9, 1e5),
        name="inverse_factor",
    )(gram_parts)


def finish_kernel(replicas, w_ref, chunk_ref, lt_ref, merged_ref, right_ref, err_ref, nr_ref):
    @pl.when(pl.program_id(0) == 0)
    def _():
        cols = right_ref.shape[1]
        across = cols // TILE_C
        pieces = []
        for a in range(right_ref.shape[0] // TILE_R):
            pieces.append(
                jnp.concatenate([chunk_ref[a * across + b] for b in range(across)], axis=1)
            )
        product = jnp.concatenate(pieces, axis=0)
        new_right = left_times(w_ref[...], product, (((1,), (0,)), ((), ()))) * (1.0 / replicas)
        right_ref[...] = new_right
        nr_ref[...] = new_right.astype(BF16)

    basis = jnp.dot(w_ref[...], lt_ref[...], precision=HIGHEST, preferred_element_type=F32)
    approx = lax.dot_general(basis.astype(BF16), nr_ref[...], ROWS_FIRST, preferred_element_type=F32)
    err_ref[0] = (merged_ref[...] - approx).astype(BF16)


def finish(replicas, w, chunks, lt, merged):
    rank, rows = lt.shape
    cols = merged.shape[1]
    block = 256
    return pl.pallas_call(
        functools.partial(finish_kernel, replicas),
        grid=(rows // block,),
        in_specs=[
            pl.BlockSpec(w.shape, lambda i: (0, 0)),
            pl.BlockSpec(chunks.shape, lambda i: (0, 0, 0)),
            pl.BlockSpec((rank, block), lambda i: (0, i)),
            pl.BlockSpec((block, cols), lambda i: (i, 0)),
        ],
        out_specs=[
            pl.BlockSpec((rank, cols), lambda i: (0, 0)),
            pl.BlockSpec((1, block, cols), lambda i: (0, i, 0)),
        ],
        out_shape=[
            jax.ShapeDtypeStruct((rank, cols), F32),
            jax.ShapeDtypeStruct((1, rows, cols), BF16),
        ],
        scratch_shapes=[pltpu.VMEM((rank, cols), BF16)],
        compiler_params=params(),
        cost_estimate=cost(2 * rows * cols * 128, 6 * rows * cols),
        name="finish",
    )(w, chunks, lt, merged)


def expert_kernel(n_hid, n_grad, *refs):
    hid_refs, grad_refs = refs[:n_hid], refs[n_hid : n_hid + sum(n_grad)]
    one_ref, two_ref, first_ref, second_ref, step_ref = refs[n_hid + sum(n_grad) :]
    grad = None
    at = 0
    for h_ref, count in zip(hid_refs, n_grad):
        rows = grad_refs[at][0]
        if count == 2:
            rows = rows + grad_refs[at + 1][0]
        at += count
        part = jnp.dot(h_ref[...], rows, preferred_element_type=F32).astype(BF16).astype(F32)
        grad = part if grad is None else grad + part
    first_new = beta_one * one_ref[0] + (1.0 - beta_one) * grad
    second_new = beta_two * two_ref[0] + (1.0 - beta_two) * grad * grad
    first_ref[0] = first_new
    second_ref[0] = second_new
    step = first_new / correction_one / (jnp.sqrt(second_new / correction_two) + epsilon)
    step_ref[0] = step.astype(BF16)


def expert_step(hids, grads, moment_one, moment_two):
    _, units, width = moment_one.shape
    block = 512
    n_grad = tuple(len(g) for g in grads)
    flat = [g for group in grads for g in group]
    tokens = flat[0].shape[1]
    wide = pl.BlockSpec((1, units, block), lambda i: (0, 0, i))
    return pl.pallas_call(
        functools.partial(expert_kernel, len(hids), n_grad),
        grid=(width // block,),
        in_specs=[pl.BlockSpec((units, tokens), lambda i: (0, 0))] * len(hids)
        + [pl.BlockSpec((1, tokens, block), lambda i: (0, 0, i))] * len(flat)
        + [wide, wide],
        out_specs=[wide, wide, wide],
        out_shape=[
            jax.ShapeDtypeStruct((1, units, width), F32),
            jax.ShapeDtypeStruct((1, units, width), F32),
            jax.ShapeDtypeStruct((1, units, width), BF16),
        ],
        compiler_params=params(),
        cost_estimate=cost(2 * units * width * tokens * len(hids), 20 * units * width),
        name="expert_step",
    )(*hids, *flat, moment_one, moment_two)


def power_of_two(n):
    return n & (n - 1) == 0


def swap(x, axis, size, mask):
    return lax.ppermute(x, axis, [(i, i ^ mask) for i in range(size)])


def gather_line(x, axis, size):
    right, left = [x], [x]
    for k in range(1, size):
        right.append(lax.ppermute(right[-1], axis, [(i, i + 1) for i in range(k - 1, size - 1)]))
        left.append(lax.ppermute(left[-1], axis, [(i, i - 1) for i in range(1, size - k + 1)]))
    return [(right[k], left[size - k]) for k in range(1, size)]


def body(n_rep, n_exp, activations, kv_grad, errors, right_factor, hidden, out_grad, moment_one, moment_two):
    others = gather_line(out_grad, "exp", n_exp)

    merged, lt = merge(activations, kv_grad, errors, right_factor.T)

    place = lax.axis_index("exp")
    tokens, units = hidden.shape[1], hidden.shape[2] // n_exp
    slabs = hidden[0].T.reshape(n_exp, units, tokens)
    hids = [lax.dynamic_index_in_dim(slabs, place, 0, keepdims=False)]
    for k in range(1, n_exp):
        piece = lax.dynamic_index_in_dim(slabs, lax.rem(place + k, n_exp), 0, keepdims=False)
        hids.append(lax.ppermute(piece, "exp", [(i, (i + k) % n_exp) for i in range(n_exp)]))

    lt = lt + swap(lt, "rep", n_rep, 1)
    bit = 2
    parts = lt.astype(BF16)[None]
    while bit < n_rep:
        if bit > 2:
            total = parts.astype(F32)
            while total.shape[0] > 1:
                total = total[0::2] + total[1::2]
            parts = total.astype(BF16)
        own = parts[0]
        masks = [bit] if 2 * bit >= n_rep else [bit, 2 * bit, 3 * bit]
        parts = jnp.stack([own] + [swap(own, "rep", n_rep, m) for m in masks])
        bit *= 2 * len(masks) if len(masks) == 1 else 4
    lt, gram, chunks = right_product(parts, merged)

    if power_of_two(n_exp):
        gram_parts = jnp.stack([gram] + [swap(gram, "exp", n_exp, m) for m in range(1, n_exp)])
    else:
        gram_parts = lax.psum(gram, "exp")[None]
    w = inverse_factor(gram_parts)

    n_chunks = chunks.shape[0]
    if n_chunks == n_rep * n_exp:
        both = ("rep", "exp")
        shares = lax.all_to_all(chunks, both, 0, 0, tiled=True)
        share = jnp.sum(shares.astype(F32), axis=0).astype(BF16)
        chunks = lax.all_to_all(jnp.broadcast_to(share[None], chunks.shape), both, 0, 0, tiled=True)
    else:
        chunks = lax.psum(chunks.astype(F32), ("rep", "exp")).astype(BF16)

    new_right, new_error = finish(n_rep, w, chunks, lt, merged)
    first_new, second_new, step = expert_step(hids, [(out_grad,)] + others, moment_one, moment_two)
    return new_error, new_right.T, first_new, second_new, step


def solution(mesh):
    placed = (
        P("rep", "exp"),
        P("rep", None),
        P("rep", "exp", None),
        P(),
        P("rep", "exp", None),
        P("rep", "exp", None),
        P("rep", "exp", None),
        P("rep", "exp", None),
    )
    return jax.shard_map(
        functools.partial(body, mesh.shape["rep"], mesh.shape["exp"]),
        mesh=mesh,
        in_specs=placed,
        out_specs=(
            P("rep", "exp", None),
            P(),
            P("rep", "exp", None),
            P("rep", "exp", None),
            P("rep", "exp", None),
        ),
        check_vma=False,
    )
```

```python
import functools

import jax
import jax.numpy as jnp
from jax import lax
from jax.experimental import pallas as pl
from jax.experimental.pallas import tpu as pltpu
from jax.sharding import PartitionSpec as P

HIGHEST = lax.Precision.HIGHEST
F32 = jnp.float32
BF16 = jnp.bfloat16
beta_one = 0.9
beta_two = 0.99
correction_one = 1.0 - 0.9**10
correction_two = 1.0 - 0.99**10
epsilon = 1e-08

ROWS_FIRST = (((0,), (0,)), ((), ()))
COLS_LAST = (((1,), (1,)), ((), ()))
TILE_R, TILE_C = 16, 128
VMEM_LIMIT = 40 * 1024 * 1024


def params():
    return pltpu.CompilerParams(vmem_limit_bytes=VMEM_LIMIT)


def cost(flops, nbytes):
    return pl.CostEstimate(flops=int(flops), bytes_accessed=int(nbytes), transcendentals=0)


def split_two(x):
    hi = x.astype(BF16)
    return hi, (x - hi.astype(F32)).astype(BF16)


def left_times(left, right_bf16, dims):
    rows = left.shape[0]
    hi, lo = split_two(left)
    both = jnp.concatenate([hi, lo], axis=0)
    out = lax.dot_general(both, right_bf16, dims, preferred_element_type=F32)
    return out[:rows] + out[rows:]


def merge_kernel(acts_ref, kv_ref, err_ref, vt_ref, merged_ref, lt_ref):
    merged = lax.dot_general(acts_ref[...], kv_ref[...], ROWS_FIRST, preferred_element_type=F32)
    merged = merged + err_ref[0].astype(F32)
    merged_ref[...] = merged
    lt_ref[...] = left_times(vt_ref[...], merged.astype(BF16), COLS_LAST)


def merge(acts, kv, err, vt):
    tokens, rows = acts.shape
    cols = kv.shape[1]
    rank = vt.shape[0]
    block = 256
    return pl.pallas_call(
        merge_kernel,
        grid=(rows // block,),
        in_specs=[
            pl.BlockSpec((tokens, block), lambda i: (0, i)),
            pl.BlockSpec((tokens, cols), lambda i: (0, 0)),
            pl.BlockSpec((1, block, cols), lambda i: (0, i, 0)),
            pl.BlockSpec((rank, cols), lambda i: (0, 0)),
        ],
        out_specs=[
            pl.BlockSpec((block, cols), lambda i: (i, 0)),
            pl.BlockSpec((rank, block), lambda i: (0, i)),
        ],
        out_shape=[
            jax.ShapeDtypeStruct((rows, cols), F32),
            jax.ShapeDtypeStruct((rank, rows), F32),
        ],
        compiler_params=params(),
        cost_estimate=cost(2 * tokens * rows * cols, 2 * tokens * (rows + cols) + 6 * rows * cols),
        name="merge",
    )(*[pltpu.with_memory_space_constraint(x, pltpu.HBM) for x in (acts, kv, err, vt)])


def slab_kernel(hidden_ref, slab_ref):
    slab_ref[...] = hidden_ref[0].T.reshape(slab_ref.shape)


def unit_slabs(hidden, parts):
    _, tokens, units = hidden.shape
    return pl.pallas_call(
        slab_kernel,
        out_shape=jax.ShapeDtypeStruct((parts, units // parts, tokens), BF16),
        compiler_params=params(),
        cost_estimate=cost(0, 4 * tokens * units),
        name="unit_slabs",
    )(hidden)


def right_kernel(n_parts, n_exp, *refs):
    part_refs, merged_ref, slab_ref = refs[:n_parts], refs[n_parts], refs[n_parts + 1]
    lt_ref, gram_ref, chunk_ref = refs[n_parts + 2 : n_parts + 5]
    load_refs = refs[n_parts + 5 :]
    parts = [ref[...].astype(F32) for ref in part_refs]
    while len(parts) > 1:
        parts = [a + b for a, b in zip(parts[0::2], parts[1::2])]
    lt = parts[0]
    rank = lt.shape[0]
    lt_ref[...] = lt
    product = left_times(lt, merged_ref[...].astype(BF16), (((1,), (0,)), ((), ()))).astype(BF16)
    across = product.shape[1] // TILE_C
    for a in range(rank // TILE_R):
        for b in range(across):
            chunk_ref[a * across + b] = product[
                a * TILE_R : (a + 1) * TILE_R, b * TILE_C : (b + 1) * TILE_C
            ]
    gram = lax.dot_general(lt, lt, COLS_LAST, precision=HIGHEST, preferred_element_type=F32)
    half = rank // 2
    packed = jnp.concatenate([gram[:half], gram[half:]], axis=1)
    high = packed.astype(BF16)
    rest = packed - high.astype(F32)
    middle = rest.astype(BF16)
    low = (rest - middle.astype(F32)).astype(BF16)
    gram_ref[...] = high.astype(F32) + middle.astype(F32) + low.astype(F32)
    place = lax.axis_index("exp")
    units = slab_ref.shape[1]
    for k in range(n_exp):
        load_ref = load_refs[k]
        load_ref[0:units] = slab_ref[lax.rem(place + k, n_exp)]
        if k:
            load_ref[units : units + half] = high
            load_ref[units + half : units + 2 * half] = middle
            load_ref[units + 2 * half : units + 3 * half] = low


def right_product(parts, merged, slabs):
    rank, rows = parts[0].shape
    cols = merged.shape[1]
    chunks = rank * cols // (TILE_R * TILE_C)
    n_exp, units, tokens = slabs.shape
    assert tokens == 2 * rank
    load = jax.ShapeDtypeStruct((units + 3 * (rank // 2), tokens), BF16)
    out = pl.pallas_call(
        functools.partial(right_kernel, len(parts), n_exp),
        out_shape=[
            jax.ShapeDtypeStruct((rank, rows), F32),
            jax.ShapeDtypeStruct((rank // 2, 2 * rank), F32),
            jax.ShapeDtypeStruct((chunks, TILE_R, TILE_C), BF16),
        ]
        + [jax.ShapeDtypeStruct((units, tokens), BF16)]
        + [load] * (n_exp - 1),
        compiler_params=params(),
        cost_estimate=cost(2 * rows * cols * 128, 4 * rows * cols),
        name="right_product",
    )(*parts, merged, slabs)
    return out[0], out[1], out[2], out[3:]


def inverse_kernel(n_exp, *refs):
    gram_ref, load_refs = refs[0], refs[1:n_exp]
    lt_ref, w_ref, basis_ref, parts_ref = refs[n_exp:]
    rank = lt_ref.shape[0]
    half = rank // 2
    parts_ref[0] = gram_ref[...]
    for k in range(1, n_exp):
        terms = load_refs[k - 1][load_refs[k - 1].shape[0] - 3 * half :].astype(F32)
        parts_ref[k] = terms[:half] + terms[half : 2 * half] + terms[2 * half :]
    place = lax.axis_index("exp")
    packed = None
    for j in range(n_exp):
        part = parts_ref[lax.rem(place + n_exp - j, n_exp)]
        packed = part if packed is None else packed + part
    gram = jnp.concatenate([packed[:, :rank], packed[:, rank:]], axis=0)
    row = lax.broadcasted_iota(jnp.int32, (rank, rank), 0)
    col = lax.broadcasted_iota(jnp.int32, (rank, rank), 1)
    a = jnp.concatenate([gram, jnp.where(row == col, 1.0, 0.0).astype(F32)], axis=1)
    row_ids = lax.broadcasted_iota(jnp.int32, (rank, 1), 0)
    for k in range(rank):
        pivot_row = a[k : k + 1, :]
        pivot = pivot_row[:, k : k + 1]
        w_ref[k : k + 1, :] = pivot_row[:, rank:] * lax.rsqrt(pivot)
        if k + 1 < rank:
            factor = jnp.where(row_ids > k, a[:, k : k + 1] / pivot, 0.0)
            a = a - factor * pivot_row
    basis = jnp.dot(w_ref[...], lt_ref[...], precision=HIGHEST, preferred_element_type=F32)
    basis_ref[...] = basis.T.astype(BF16)


def inverse_factor(gram, loads, lt):
    rank, rows = lt.shape
    n_exp = len(loads) + 1
    return pl.pallas_call(
        functools.partial(inverse_kernel, n_exp),
        out_shape=[
            jax.ShapeDtypeStruct((rank, rank), F32),
            jax.ShapeDtypeStruct((rows, rank), BF16),
        ],
        scratch_shapes=[pltpu.VMEM((n_exp, rank // 2, 2 * rank), F32)],
        compiler_params=params(),
        cost_estimate=cost(4e9, 1e5),
        name="inverse_factor",
    )(gram, *loads, lt)


def finish_kernel(replicas, w_ref, chunk_ref, basis_ref, merged_ref, right_hbm, err_hbm, right_ref, err_ref, sems):
    rank, cols = right_ref.shape
    across = cols // TILE_C
    pieces = []
    for a in range(rank // TILE_R):
        pieces.append(jnp.concatenate([chunk_ref[a * across + b] for b in range(across)], axis=1))
    product = jnp.concatenate(pieces, axis=0)
    new_right = left_times(w_ref[...], product, (((1,), (0,)), ((), ()))) * (1.0 / replicas)
    right_ref[...] = new_right
    copies = [pltpu.make_async_copy(right_ref, right_hbm, sems.at[0])]
    copies[0].start()
    rounded = new_right.astype(BF16)
    rows, block = err_ref.shape[0], 128
    for i in range(rows // block):
        here = slice(i * block, (i + 1) * block)
        approx = jnp.dot(basis_ref[here, :], rounded, preferred_element_type=F32)
        err_ref[here, :] = (merged_ref[here, :] - approx).astype(BF16)
        copies.append(
            pltpu.make_async_copy(err_ref.at[here, :], err_hbm.at[0, here, :], sems.at[i + 1])
        )
        copies[-1].start()
    for copy in copies:
        copy.wait()


def finish(replicas, w, chunks, basis, merged):
    rows, rank = basis.shape
    cols = merged.shape[1]
    return pl.pallas_call(
        functools.partial(finish_kernel, replicas),
        out_specs=[pl.BlockSpec(memory_space=pltpu.HBM)] * 2,
        out_shape=[
            jax.ShapeDtypeStruct((rank, cols), F32),
            jax.ShapeDtypeStruct((1, rows, cols), BF16),
        ],
        scratch_shapes=[
            pltpu.VMEM((rank, cols), F32),
            pltpu.VMEM((rows, cols), BF16),
            pltpu.SemaphoreType.DMA((rows // 128 + 1,)),
        ],
        compiler_params=params(),
        cost_estimate=cost(2 * rows * cols * 128, 6 * rows * cols),
        name="finish",
    )(w, chunks, basis, merged)


def expert_kernel(n_exp, *refs):
    hid_refs, grad_refs = refs[:n_exp], refs[n_exp : 2 * n_exp]
    one_ref, two_ref, first_ref, second_ref, step_ref = refs[2 * n_exp :]
    units = one_ref.shape[1]
    hid = jnp.concatenate([ref[0:units, :] for ref in hid_refs], axis=1)
    rows = jnp.concatenate([ref[0] for ref in grad_refs], axis=0)
    grad = jnp.dot(hid, rows, preferred_element_type=F32)
    first_new = beta_one * one_ref[0] + (1.0 - beta_one) * grad
    second_new = beta_two * two_ref[0] + (1.0 - beta_two) * grad * grad
    first_ref[0] = first_new
    second_ref[0] = second_new
    scaled = second_new * (1.0 / correction_two)
    bottom = scaled * lax.rsqrt(scaled) + epsilon
    step = first_new * (1.0 / correction_one) * pl.reciprocal(bottom, approx=True)
    step_ref[0] = step.astype(BF16)


def expert_step(hids, grads, moment_one, moment_two):
    _, units, width = moment_one.shape
    block = 512
    n_exp = len(hids)
    tokens = grads[0].shape[1]
    wide = pl.BlockSpec((1, units, block), lambda i: (0, 0, i))
    return pl.pallas_call(
        functools.partial(expert_kernel, n_exp),
        grid=(width // block,),
        in_specs=[pl.BlockSpec(h.shape, lambda i: (0, 0)) for h in hids]
        + [pl.BlockSpec((1, tokens, block), lambda i: (0, 0, i))] * n_exp
        + [wide, wide],
        out_specs=[wide, wide, wide],
        out_shape=[
            jax.ShapeDtypeStruct((1, units, width), F32),
            jax.ShapeDtypeStruct((1, units, width), F32),
            jax.ShapeDtypeStruct((1, units, width), BF16),
        ],
        compiler_params=params(),
        cost_estimate=cost(2 * units * width * tokens * n_exp, 20 * units * width),
        name="expert_step",
    )(*hids, pltpu.with_memory_space_constraint(grads[0], pltpu.HBM), *grads[1:], moment_one, moment_two)


def swap(x, axis, size, mask):
    return lax.ppermute(x, axis, [(i, i ^ mask) for i in range(size)])


def shift(x, size, k):
    return lax.ppermute(x, "exp", [(i, (i + k) % size) for i in range(size)])


def after(x, y):
    return lax.optimization_barrier((x, y))[0]


def body(n_rep, n_exp, activations, kv_grad, errors, right_factor, hidden, out_grad, moment_one, moment_two):
    grads = {0: out_grad}
    if n_exp > 1:
        grads[1] = shift(out_grad, n_exp, 1)
    merged, lt = merge(activations, kv_grad, errors, right_factor.T)
    if n_exp > 2:
        grads[n_exp - 1] = shift(after(out_grad, lt), n_exp, -1)

    lt = (lt + swap(lt, "rep", n_rep, 1)).astype(BF16)
    slabs = unit_slabs(after(hidden, lt), n_exp)
    bit = 2
    parts = [lt]
    while bit < n_rep:
        while len(parts) > 1:
            parts = [a.astype(F32) + b.astype(F32) for a, b in zip(parts[0::2], parts[1::2])]
        own = parts[0].astype(BF16)
        masks = [bit] if 2 * bit >= n_rep else [bit, 2 * bit, 3 * bit]
        parts = [own] + [swap(own, "rep", n_rep, m) for m in masks]
        bit *= len(parts)
    lt, gram, chunks, loads = right_product(parts, merged, slabs)

    left, right = 1, n_exp - 1
    while right - left > 1:
        if left <= n_exp - right:
            grads[left + 1] = shift(after(grads[left], chunks), n_exp, 1)
            left += 1
        else:
            grads[right - 1] = shift(after(grads[right], chunks), n_exp, -1)
            right -= 1

    loads = [loads[0]] + [shift(loads[k], n_exp, k) for k in range(1, n_exp)]
    w, basis = inverse_factor(gram, loads[1:], lt)

    n_chunks = chunks.shape[0]
    if n_chunks == n_rep * n_exp:
        both = ("rep", "exp")
        shares = lax.all_to_all(chunks, both, 0, 0, tiled=True)
        share = jnp.sum(shares.astype(F32), axis=0).astype(BF16)
        chunks = lax.all_to_all(jnp.broadcast_to(share[None], chunks.shape), both, 0, 0, tiled=True)
    else:
        chunks = lax.psum(chunks.astype(F32), ("rep", "exp")).astype(BF16)

    new_right, new_error = finish(n_rep, w, chunks, basis, merged)
    first_new, second_new, step = expert_step(
        loads, [grads[k] for k in range(n_exp)], moment_one, moment_two
    )
    return new_error, new_right.T, first_new, second_new, step


def solution(mesh):
    placed = (
        P("rep", "exp"),
        P("rep", None),
        P("rep", "exp", None),
        P(),
        P("rep", "exp", None),
        P("rep", "exp", None),
        P("rep", "exp", None),
        P("rep", "exp", None),
    )
    return jax.shard_map(
        functools.partial(body, mesh.shape["rep"], mesh.shape["exp"]),
        mesh=mesh,
        in_specs=placed,
        out_specs=(
            P("rep", "exp", None),
            P(),
            P("rep", "exp", None),
            P("rep", "exp", None),
            P("rep", "exp", None),
        ),
        check_vma=False,
    )
```

```python
import functools

import jax
import jax.numpy as jnp
from jax import lax
from jax.experimental import pallas as pl
from jax.experimental.pallas import tpu as pltpu
from jax.sharding import PartitionSpec as P

HIGHEST = lax.Precision.HIGHEST
F32 = jnp.float32
BF16 = jnp.bfloat16
beta_one = 0.9
beta_two = 0.99
correction_one = 1.0 - 0.9**10
correction_two = 1.0 - 0.99**10
epsilon = 1e-08

ROWS_FIRST = (((0,), (0,)), ((), ()))
COLS_LAST = (((1,), (1,)), ((), ()))
TILE_R, TILE_C = 16, 128
HBM = pl.BlockSpec(memory_space=pltpu.HBM)
VMEM = pl.BlockSpec(memory_space=pltpu.VMEM)


def params(mebibytes):
    return pltpu.CompilerParams(vmem_limit_bytes=mebibytes * 1024 * 1024)


def in_hbm(*arrays):
    return [pltpu.with_memory_space_constraint(x, pltpu.HBM) for x in arrays]


def cost(flops, nbytes):
    return pl.CostEstimate(flops=int(flops), bytes_accessed=int(nbytes), transcendentals=0)


def split_two(x):
    hi = x.astype(BF16)
    return hi, (x - hi.astype(F32)).astype(BF16)


def left_times(left, right_bf16, dims):
    rows = left.shape[0]
    hi, lo = split_two(left)
    both = jnp.concatenate([hi, lo], axis=0)
    out = lax.dot_general(both, right_bf16, dims, preferred_element_type=F32)
    return out[:rows] + out[rows:]


def merge_kernel(block, acts_hbm, kv_hbm, err_hbm, vt_hbm, merged_ref, lt_ref, acts, kv, err, vt, sems):
    tokens, rows = acts.shape
    half = tokens // 2
    count = rows // block

    def acts_copy(i):
        here = slice(i * block, (i + 1) * block)
        return pltpu.make_async_copy(acts_hbm.at[:, here], acts.at[:, here], sems.at[3 + i])

    def err_copy(i):
        here = slice(i * block, (i + 1) * block)
        return pltpu.make_async_copy(err_hbm.at[0, here, :], err.at[here, :], sems.at[3 + count + i])

    def kv_copy(i):
        here = slice(i * half, (i + 1) * half)
        return pltpu.make_async_copy(kv_hbm.at[here, :], kv.at[here, :], sems.at[i])

    vt_copy = pltpu.make_async_copy(vt_hbm, vt, sems.at[2])
    acts_copy(0).start()
    kv_copy(0).start()
    kv_copy(1).start()
    err_copy(0).start()
    vt_copy.start()
    for i in range(count):
        here = slice(i * block, (i + 1) * block)
        acts_copy(i).wait()
        if i == 0:
            kv_copy(0).wait()
            for later in range(1, count):
                acts_copy(later).start()
                err_copy(later).start()
            merged = lax.dot_general(
                acts[:half, here], kv[:half, :], ROWS_FIRST, preferred_element_type=F32
            )
            kv_copy(1).wait()
            merged = merged + lax.dot_general(
                acts[half:, here], kv[half:, :], ROWS_FIRST, preferred_element_type=F32
            )
        else:
            merged = lax.dot_general(acts[:, here], kv[...], ROWS_FIRST, preferred_element_type=F32)
        err_copy(i).wait()
        merged = merged + err[here, :].astype(F32)
        merged_ref[here, :] = merged
        if i == 0:
            vt_copy.wait()
        lt_ref[:, here] = left_times(vt[...], merged.astype(BF16), COLS_LAST)


def merge(acts, kv, err, vt):
    tokens, rows = acts.shape
    cols = kv.shape[1]
    rank = vt.shape[0]
    block = 256
    return pl.pallas_call(
        functools.partial(merge_kernel, block),
        in_specs=[HBM] * 4,
        out_specs=[VMEM] * 2,
        out_shape=[
            jax.ShapeDtypeStruct((rows, cols), F32),
            jax.ShapeDtypeStruct((rank, rows), F32),
        ],
        scratch_shapes=[
            pltpu.VMEM((tokens, rows), BF16),
            pltpu.VMEM((tokens, cols), BF16),
            pltpu.VMEM((rows, cols), BF16),
            pltpu.VMEM((rank, cols), F32),
            pltpu.SemaphoreType.DMA((3 + 2 * (rows // block),)),
        ],
        compiler_params=params(24),
        cost_estimate=cost(2 * tokens * rows * cols, 2 * tokens * (rows + cols) + 6 * rows * cols),
        name="merge",
    )(*in_hbm(acts, kv, err, vt))


def slab_kernel(hidden_ref, slab_ref):
    slab_ref[...] = hidden_ref[0].T.reshape(slab_ref.shape)


def unit_slabs(hidden, parts):
    _, tokens, units = hidden.shape
    return pl.pallas_call(
        slab_kernel,
        out_shape=jax.ShapeDtypeStruct((parts, units // parts, tokens), BF16),
        compiler_params=params(8),
        cost_estimate=cost(0, 4 * tokens * units),
        name="unit_slabs",
    )(hidden)


def right_kernel(n_parts, *refs):
    part_refs, merged_ref = refs[:n_parts], refs[n_parts]
    lt_ref, gram_ref, chunk_ref = refs[n_parts + 1 :]
    parts = [ref[...].astype(F32) for ref in part_refs]
    while len(parts) > 1:
        parts = [a + b for a, b in zip(parts[0::2], parts[1::2])]
    lt = parts[0]
    rank = lt.shape[0]
    lt_ref[...] = lt
    product = left_times(lt, merged_ref[...].astype(BF16), (((1,), (0,)), ((), ()))).astype(BF16)
    across = product.shape[1] // TILE_C
    for a in range(rank // TILE_R):
        for b in range(across):
            chunk_ref[a * across + b] = product[
                a * TILE_R : (a + 1) * TILE_R, b * TILE_C : (b + 1) * TILE_C
            ]
    gram = lax.dot_general(lt, lt, COLS_LAST, precision=HIGHEST, preferred_element_type=F32)
    half = rank // 2
    packed = jnp.concatenate([gram[:half], gram[half:]], axis=1)
    high = packed.astype(BF16)
    rest = packed - high.astype(F32)
    middle = rest.astype(BF16)
    low = (rest - middle.astype(F32)).astype(BF16)
    gram_ref[0:half] = high
    gram_ref[half : 2 * half] = middle
    gram_ref[2 * half : 3 * half] = low


def right_product(parts, merged):
    rank, rows = parts[0].shape
    cols = merged.shape[1]
    chunks = rank * cols // (TILE_R * TILE_C)
    return pl.pallas_call(
        functools.partial(right_kernel, len(parts)),
        out_shape=[
            jax.ShapeDtypeStruct((rank, rows), F32),
            jax.ShapeDtypeStruct((3 * (rank // 2), 2 * rank), BF16),
            jax.ShapeDtypeStruct((chunks, TILE_R, TILE_C), BF16),
        ],
        compiler_params=params(16),
        cost_estimate=cost(2 * rows * cols * 128, 4 * rows * cols),
        name="right_product",
    )(*parts, merged)


def load_kernel(share_ref, gram_ref, load_ref):
    total = share_ref[0].astype(F32)
    for i in range(1, share_ref.shape[0]):
        total = total + share_ref[i].astype(F32)
    terms, rows = gram_ref.shape[0], load_ref.shape[1] - gram_ref.shape[0]
    if rows > total.shape[0]:
        total = jnp.concatenate([total, jnp.zeros((rows - total.shape[0], TILE_C), F32)], axis=0)
    total = total.astype(BF16)
    for k in range(load_ref.shape[0]):
        load_ref[k, 0:terms] = gram_ref[...]
        load_ref[k, terms : terms + rows] = total


def line_load(shares, gram, n_exp):
    rows = -(-shares.shape[1] // TILE_R) * TILE_R
    return pl.pallas_call(
        load_kernel,
        out_shape=jax.ShapeDtypeStruct((n_exp, gram.shape[0] + rows, TILE_C), BF16),
        compiler_params=params(8),
        cost_estimate=cost(0, 1e6),
        name="line_load",
    )(shares, gram)


def spread_kernel(terms, load_ref, chunk_ref):
    rows = chunk_ref.shape[1]
    total = load_ref[0, terms:].astype(F32)
    for j in range(1, load_ref.shape[0]):
        total = total + load_ref[j, terms:].astype(F32)
    total = total[:rows].astype(BF16)
    for i in range(chunk_ref.shape[0]):
        chunk_ref[i] = total


def spread(loads, terms, n_rep, rows):
    return pl.pallas_call(
        functools.partial(spread_kernel, terms),
        out_shape=jax.ShapeDtypeStruct((n_rep, rows, TILE_C), BF16),
        compiler_params=params(8),
        cost_estimate=cost(0, 1e6),
        name="spread",
    )(loads)


def inverse_kernel(load_ref, lt_ref, w_ref, basis_ref, wide_ref):
    rank = lt_ref.shape[0]
    half = rank // 2
    packed = None
    for j in range(load_ref.shape[0]):
        terms = load_ref[j, 0 : 3 * half].astype(F32)
        part = terms[:half] + terms[half : 2 * half] + terms[2 * half :]
        packed = part if packed is None else packed + part
    gram = jnp.concatenate([packed[:, :rank], packed[:, rank:]], axis=0)
    row = lax.broadcasted_iota(jnp.int32, (rank, rank), 0)
    col = lax.broadcasted_iota(jnp.int32, (rank, rank), 1)
    a = jnp.concatenate([gram, jnp.where(row == col, 1.0, 0.0).astype(F32)], axis=1)
    group = 4
    for k in range(0, rank, group):
        cols = [jnp.broadcast_to(a[:, k + j : k + j + 1], a.shape) for j in range(group)]
        rows = [a[k + j : k + j + 1, :] for j in range(group)]
        for j in range(group):
            pivot = cols[j][k + j : k + j + 1, :]
            wide_ref[k + j : k + j + 1, :] = rows[j] * lax.rsqrt(pivot)
            factor = cols[j] * (1.0 / pivot)
            for m in range(j + 1, group):
                cols[m] = cols[m] - factor * cols[m][k + j : k + j + 1, :]
                rows[m] = rows[m] - factor[k + m : k + m + 1, :] * rows[j]
            a = a - factor * rows[j]
    w = wide_ref[:, rank:]
    w_ref[...] = w
    basis = jnp.dot(w, lt_ref[...], precision=HIGHEST, preferred_element_type=F32)
    basis_ref[...] = basis.T.astype(BF16)


def inverse_factor(loads, lt):
    rank, rows = lt.shape
    return pl.pallas_call(
        inverse_kernel,
        out_shape=[
            jax.ShapeDtypeStruct((rank, rank), F32),
            jax.ShapeDtypeStruct((rows, rank), BF16),
        ],
        scratch_shapes=[pltpu.VMEM((rank, 2 * rank), F32)],
        compiler_params=params(8),
        cost_estimate=cost(4e9, 1e5),
        name="inverse_factor",
    )(loads, lt)


def finish_kernel(replicas, w_ref, chunk_ref, basis_ref, merged_ref, right_hbm, err_hbm, right_ref, err_ref, sems):
    rank, cols = right_ref.shape
    across = cols // TILE_C
    pieces = []
    for a in range(rank // TILE_R):
        pieces.append(jnp.concatenate([chunk_ref[a * across + b] for b in range(across)], axis=1))
    product = jnp.concatenate(pieces, axis=0)
    new_right = left_times(w_ref[...], product, (((1,), (0,)), ((), ()))) * (1.0 / replicas)
    right_ref[...] = new_right
    copies = [pltpu.make_async_copy(right_ref, right_hbm, sems.at[0])]
    copies[0].start()
    rounded = new_right.astype(BF16)
    rows, block = err_ref.shape[0], 128
    for i in range(rows // block):
        here = slice(i * block, (i + 1) * block)
        approx = jnp.dot(basis_ref[here, :], rounded, preferred_element_type=F32)
        err_ref[here, :] = (merged_ref[here, :] - approx).astype(BF16)
        copies.append(
            pltpu.make_async_copy(err_ref.at[here, :], err_hbm.at[0, here, :], sems.at[i + 1])
        )
        copies[-1].start()
    for copy in copies:
        copy.wait()


def finish(replicas, w, chunks, basis, merged):
    rows, rank = basis.shape
    cols = merged.shape[1]
    return pl.pallas_call(
        functools.partial(finish_kernel, replicas),
        out_specs=[HBM] * 2,
        out_shape=[
            jax.ShapeDtypeStruct((rank, cols), F32),
            jax.ShapeDtypeStruct((1, rows, cols), BF16),
        ],
        scratch_shapes=[
            pltpu.VMEM((rank, cols), F32),
            pltpu.VMEM((rows, cols), BF16),
            pltpu.SemaphoreType.DMA((rows // 128 + 1,)),
        ],
        compiler_params=params(16),
        cost_estimate=cost(2 * rows * cols * 128, 6 * rows * cols),
        name="finish",
    )(w, chunks, basis, merged)


def expert_kernel(n_exp, chunk, *refs):
    slab_ref, grad_refs = refs[0], refs[1 : n_exp + 1]
    one_hbm, two_hbm, first_hbm, second_hbm, step_hbm = refs[n_exp + 1 : n_exp + 6]
    rows, one, two, first, second, step, in_sems, out_sems = refs[n_exp + 6 :]
    units, width = one.shape
    tokens = grad_refs[0].shape[1]
    place = lax.axis_index("exp")

    def loads(c):
        here = slice(c * chunk, (c + 1) * chunk)
        pairs = [
            (grad_refs[k].at[0, :, here], rows.at[k * tokens : (k + 1) * tokens, here])
            for k in range(n_exp)
        ]
        pairs += [(one_hbm.at[0, :, here], one.at[:, here]), (two_hbm.at[0, :, here], two.at[:, here])]
        return [pltpu.make_async_copy(a, b, in_sems.at[c, i]) for i, (a, b) in enumerate(pairs)]

    def stores(c):
        here = slice(c * chunk, (c + 1) * chunk)
        pairs = [(first, first_hbm), (second, second_hbm), (step, step_hbm)]
        return [
            pltpu.make_async_copy(a.at[:, here], b.at[0, :, here], out_sems.at[c, i])
            for i, (a, b) in enumerate(pairs)
        ]

    count = width // chunk
    for c in range(count):
        for copy in loads(c):
            copy.start()
    hid = jnp.concatenate(
        [slab_ref[lax.rem(place + n_exp - k, n_exp)] for k in range(n_exp)], axis=1
    )
    for c in range(count):
        here = slice(c * chunk, (c + 1) * chunk)
        for copy in loads(c):
            copy.wait()
        grad = jnp.dot(hid, rows[:, here], preferred_element_type=F32)
        first_new = beta_one * one[:, here] + (1.0 - beta_one) * grad
        second_new = beta_two * two[:, here] + (1.0 - beta_two) * grad * grad
        first[:, here] = first_new
        second[:, here] = second_new
        scaled = second_new * (1.0 / correction_two)
        bottom = scaled * lax.rsqrt(scaled) + epsilon
        step[:, here] = (
            first_new * (1.0 / correction_one) * pl.reciprocal(bottom, approx=True)
        ).astype(BF16)
        for copy in stores(c):
            copy.start()
    for c in range(count):
        for copy in stores(c):
            copy.wait()


def expert_step(slabs, grads, moment_one, moment_two):
    _, units, width = moment_one.shape
    chunk = 256
    n_exp = len(grads)
    tokens = grads[0].shape[1]
    return pl.pallas_call(
        functools.partial(expert_kernel, n_exp, chunk),
        in_specs=[VMEM, HBM] + [pl.BlockSpec(memory_space=pl.ANY)] * (n_exp - 1) + [HBM] * 2,
        out_specs=[HBM] * 3,
        out_shape=[
            jax.ShapeDtypeStruct((1, units, width), F32),
            jax.ShapeDtypeStruct((1, units, width), F32),
            jax.ShapeDtypeStruct((1, units, width), BF16),
        ],
        scratch_shapes=[
            pltpu.VMEM((n_exp * tokens, width), BF16),
            pltpu.VMEM((units, width), F32),
            pltpu.VMEM((units, width), F32),
            pltpu.VMEM((units, width), F32),
            pltpu.VMEM((units, width), F32),
            pltpu.VMEM((units, width), BF16),
            pltpu.SemaphoreType.DMA((width // chunk, n_exp + 2)),
            pltpu.SemaphoreType.DMA((width // chunk, 3)),
        ],
        compiler_params=params(24),
        cost_estimate=cost(2 * units * width * tokens * n_exp, 20 * units * width),
        name="expert_step",
    )(slabs, *in_hbm(grads[0]), *grads[1:], *in_hbm(moment_one, moment_two))


def swap(x, axis, size, mask):
    return lax.ppermute(x, axis, [(i, i ^ mask) for i in range(size)])


def shift(x, size, k):
    return lax.ppermute(x, "exp", [(i, (i + k) % size) for i in range(size)])


def after(x, y):
    return lax.optimization_barrier((x, y))[0]


def body(n_rep, n_exp, activations, kv_grad, errors, right_factor, hidden, out_grad, moment_one, moment_two):
    grads = [out_grad, shift(out_grad, n_exp, 1)]
    merged, lt = merge(activations, kv_grad, errors, right_factor.T)

    lt = (lt + swap(lt, "rep", n_rep, 1)).astype(BF16)
    bit = 2
    parts = [lt]
    while bit < n_rep:
        while len(parts) > 1:
            parts = [a.astype(F32) + b.astype(F32) for a, b in zip(parts[0::2], parts[1::2])]
        own = parts[0].astype(BF16)
        masks = [bit] if 2 * bit >= n_rep else [bit, 2 * bit, 3 * bit]
        parts = [own] + [swap(own, "rep", n_rep, m) for m in masks]
        bit *= len(parts)

    grads.append(shift(after(grads[1], parts[1]), n_exp, 1))
    lt, gram, chunks = right_product(parts, merged)

    slabs = unit_slabs(after(hidden, chunks), n_exp)
    slabs = lax.all_to_all(slabs, "exp", 0, 0, tiled=True)

    rows = chunks.shape[0] * TILE_R // n_rep
    shares = lax.all_to_all(chunks.reshape(n_rep, rows, TILE_C), "rep", 0, 0, tiled=True)
    load = line_load(shares, gram, n_exp)
    loads = lax.all_to_all(load, "exp", 0, 0, tiled=True)
    share = spread(loads, gram.shape[0], n_rep, rows)
    for k in range(3, n_exp):
        grads.append(shift(after(grads[-1], share), n_exp, 1))
    back = lax.all_to_all(share, "rep", 0, 0, tiled=True).reshape(chunks.shape)
    w, basis = inverse_factor(loads, lt)

    new_right, new_error = finish(n_rep, w, back, basis, merged)
    first_new, second_new, step = expert_step(slabs, grads, moment_one, moment_two)
    return new_error, new_right.T, first_new, second_new, step


def solution(mesh):
    placed = (
        P("rep", "exp"),
        P("rep", None),
        P("rep", "exp", None),
        P(),
        P("rep", "exp", None),
        P("rep", "exp", None),
        P("rep", "exp", None),
        P("rep", "exp", None),
    )
    return jax.shard_map(
        functools.partial(body, mesh.shape["rep"], mesh.shape["exp"]),
        mesh=mesh,
        in_specs=placed,
        out_specs=(
            P("rep", "exp", None),
            P(),
            P("rep", "exp", None),
            P("rep", "exp", None),
            P("rep", "exp", None),
        ),
        check_vma=False,
    )
```

```python
import functools

import jax
import jax.numpy as jnp
from jax import lax
from jax.experimental import pallas as pl
from jax.experimental.pallas import tpu as pltpu
from jax.sharding import PartitionSpec as P

HIGHEST = lax.Precision.HIGHEST
F32 = jnp.float32
BF16 = jnp.bfloat16
beta_one = 0.9
beta_two = 0.99
correction_one = 1.0 - 0.9**10
correction_two = 1.0 - 0.99**10
epsilon = 1e-08

ROWS_FIRST = (((0,), (0,)), ((), ()))
COLS_LAST = (((1,), (1,)), ((), ()))
TILE_R, TILE_C = 16, 128
HBM = pl.BlockSpec(memory_space=pltpu.HBM)
ANY = pl.BlockSpec(memory_space=pl.ANY)
VMEM = pl.BlockSpec(memory_space=pltpu.VMEM)


def params(mebibytes):
    return pltpu.CompilerParams(vmem_limit_bytes=mebibytes * 1024 * 1024)


def in_hbm(*arrays):
    return [pltpu.with_memory_space_constraint(x, pltpu.HBM) for x in arrays]


SMALL = pl.CostEstimate(flops=1000, bytes_accessed=1000, transcendentals=0)


def split_two(x):
    hi = x.astype(BF16)
    return hi, (x - hi.astype(F32)).astype(BF16)


def left_times(left, right_bf16, dims):
    rows = left.shape[0]
    hi, lo = split_two(left)
    both = jnp.concatenate([hi, lo], axis=0)
    out = lax.dot_general(both, right_bf16, dims, preferred_element_type=F32)
    return out[:rows] + out[rows:]


def merge_kernel(block, acts_hbm, kv_hbm, err_hbm, vt_hbm, merged_ref, lt_ref, acts, kv, err, vt, sems):
    tokens, rows = acts.shape
    part = tokens // 4
    half = tokens // 2
    count = rows // block

    def acts_copy(i):
        here = slice(i * block, (i + 1) * block)
        return pltpu.make_async_copy(acts_hbm.at[:, here], acts.at[:, here], sems.at[5 + i])

    def err_copy(i):
        here = slice(i * block, (i + 1) * block)
        return pltpu.make_async_copy(err_hbm.at[0, here, :], err.at[here, :], sems.at[5 + count + i])

    def kv_copy(i):
        here = slice(i * part, (i + 1) * part)
        return pltpu.make_async_copy(kv_hbm.at[here, :], kv.at[here, :], sems.at[i])

    vt_copy = pltpu.make_async_copy(vt_hbm, vt, sems.at[4])
    acts_copy(0).start()
    for i in range(4):
        kv_copy(i).start()
    err_copy(0).start()
    vt_copy.start()
    for i in range(count):
        here = slice(i * block, (i + 1) * block)
        acts_copy(i).wait()
        if i == 0:
            kv_copy(0).wait()
            kv_copy(1).wait()
            for later in range(1, count):
                acts_copy(later).start()
                err_copy(later).start()
            merged = lax.dot_general(
                acts[:half, here], kv[:half, :], ROWS_FIRST, preferred_element_type=F32
            )
            kv_copy(2).wait()
            kv_copy(3).wait()
            merged = merged + lax.dot_general(
                acts[half:, here], kv[half:, :], ROWS_FIRST, preferred_element_type=F32
            )
        else:
            merged = lax.dot_general(acts[:, here], kv[...], ROWS_FIRST, preferred_element_type=F32)
        err_copy(i).wait()
        merged = merged + err[here, :].astype(F32)
        merged_ref[here, :] = merged
        if i == 0:
            vt_copy.wait()
            both = jnp.concatenate(split_two(vt[...]), axis=0)
        left = lax.dot_general(merged.astype(BF16), both, COLS_LAST, preferred_element_type=F32).T
        lt_ref[:, here] = left[: left.shape[0] // 2] + left[left.shape[0] // 2 :]


def merge(acts, kv, err, vt):
    tokens, rows = acts.shape
    cols = kv.shape[1]
    rank = vt.shape[0]
    block = 256
    return pl.pallas_call(
        functools.partial(merge_kernel, block),
        in_specs=[HBM] * 4,
        out_specs=[VMEM] * 2,
        out_shape=[
            jax.ShapeDtypeStruct((rows, cols), F32),
            jax.ShapeDtypeStruct((rank, rows), F32),
        ],
        scratch_shapes=[
            pltpu.VMEM((tokens, rows), BF16),
            pltpu.VMEM((tokens, cols), BF16),
            pltpu.VMEM((rows, cols), BF16),
            pltpu.VMEM((rank, cols), F32),
            pltpu.SemaphoreType.DMA((5 + 2 * (rows // block),)),
        ],
        compiler_params=params(24),
        cost_estimate=SMALL,
        name="merge",
    )(*in_hbm(acts, kv, err, vt))


def slab_kernel(hidden_ref, slab_ref):
    slab_ref[...] = hidden_ref[0].T.reshape(slab_ref.shape)


def unit_slabs(hidden, parts):
    _, tokens, units = hidden.shape
    return pl.pallas_call(
        slab_kernel,
        out_shape=jax.ShapeDtypeStruct((parts, units // parts, tokens), BF16),
        compiler_params=params(8),
        cost_estimate=SMALL,
        name="unit_slabs",
    )(hidden)


def right_kernel(n_parts, n_exp, *refs):
    part_refs, merged_ref, slab_ref = refs[:n_parts], refs[n_parts], refs[n_parts + 1]
    lt_hbm, own_hbm, chunk_ref = refs[n_parts + 2 : n_parts + 5]
    load_refs = refs[n_parts + 5 : n_parts + 4 + n_exp]
    lt_ref, own_ref, sems = refs[n_parts + 4 + n_exp :]
    parts = [ref[...].astype(F32) for ref in part_refs]
    while len(parts) > 1:
        parts = [a + b for a, b in zip(parts[0::2], parts[1::2])]
    lt = parts[0]
    rank = lt.shape[0]
    lt_ref[...] = lt
    lt_copy = pltpu.make_async_copy(lt_ref, lt_hbm, sems.at[0])
    lt_copy.start()
    gram = lax.dot_general(lt, lt, COLS_LAST, precision=HIGHEST, preferred_element_type=F32)
    half = rank // 2
    packed = jnp.concatenate([gram[:half], gram[half:]], axis=1)
    high = packed.astype(BF16)
    rest = packed - high.astype(F32)
    middle = rest.astype(BF16)
    low = (rest - middle.astype(F32)).astype(BF16)
    place = lax.axis_index("exp")
    units = slab_ref.shape[1]
    for k, load_ref in enumerate((own_ref,) + tuple(load_refs)):
        load_ref[0:units] = slab_ref[lax.rem(place + k, n_exp)]
        load_ref[units : units + half] = high
        load_ref[units + half : units + 2 * half] = middle
        load_ref[units + 2 * half : units + 3 * half] = low
    own_copy = pltpu.make_async_copy(own_ref, own_hbm, sems.at[1])
    own_copy.start()
    product = left_times(lt, merged_ref[...].astype(BF16), (((1,), (0,)), ((), ()))).astype(BF16)
    across = product.shape[1] // TILE_C
    for a in range(rank // TILE_R):
        for b in range(across):
            chunk_ref[a * across + b] = product[
                a * TILE_R : (a + 1) * TILE_R, b * TILE_C : (b + 1) * TILE_C
            ]
    lt_copy.wait()
    own_copy.wait()


def right_product(parts, merged, slabs):
    rank, rows = parts[0].shape
    cols = merged.shape[1]
    chunks = rank * cols // (TILE_R * TILE_C)
    n_exp, units, tokens = slabs.shape
    assert tokens == 2 * rank
    load = (units + 3 * (rank // 2), tokens)
    out = pl.pallas_call(
        functools.partial(right_kernel, len(parts), n_exp),
        out_specs=[HBM, HBM] + [VMEM] * n_exp,
        out_shape=[
            pltpu.HBM((rank, rows), F32),
            pltpu.HBM(load, BF16),
            jax.ShapeDtypeStruct((chunks, TILE_R, TILE_C), BF16),
        ]
        + [jax.ShapeDtypeStruct(load, BF16)] * (n_exp - 1),
        scratch_shapes=[
            pltpu.VMEM((rank, rows), F32),
            pltpu.VMEM(load, BF16),
            pltpu.SemaphoreType.DMA((2,)),
        ],
        compiler_params=params(16),
        cost_estimate=SMALL,
        name="right_product",
    )(*parts, merged, slabs)
    return out[0], out[2], [out[1]] + list(out[3:])


def fold_kernel(share_ref, out_ref):
    total = share_ref[0].astype(F32)
    for i in range(1, share_ref.shape[0]):
        total = total + share_ref[i].astype(F32)
    total = total.astype(BF16)
    for i in range(out_ref.shape[0]):
        out_ref[i] = total


def fold(shares):
    return pl.pallas_call(
        fold_kernel,
        out_shape=jax.ShapeDtypeStruct(shares.shape, BF16),
        compiler_params=params(4),
        cost_estimate=SMALL,
        name="fold",
    )(shares)


def inverse_kernel(n_exp, *refs):
    load_hbms, lt_hbm = refs[:n_exp], refs[n_exp]
    w_ref, basis_ref, terms_ref, lt_ref, wide_ref, sems = refs[n_exp + 1 :]
    rank = lt_ref.shape[0]
    half = rank // 2
    units = load_hbms[0].shape[0] - 3 * half
    copies = [
        pltpu.make_async_copy(load_hbms[k].at[units : units + 3 * half], terms_ref.at[k], sems.at[k])
        for k in range(n_exp)
    ]
    lt_copy = pltpu.make_async_copy(lt_hbm, lt_ref, sems.at[n_exp])
    for copy in copies:
        copy.start()
    lt_copy.start()
    for copy in copies:
        copy.wait()
    place = lax.axis_index("exp")
    packed = None
    for j in range(n_exp):
        terms = terms_ref[lax.rem(place + n_exp - j, n_exp)].astype(F32)
        part = terms[:half] + terms[half : 2 * half] + terms[2 * half :]
        packed = part if packed is None else packed + part
    gram = jnp.concatenate([packed[:, :rank], packed[:, rank:]], axis=0)
    row = lax.broadcasted_iota(jnp.int32, (rank, rank), 0)
    col = lax.broadcasted_iota(jnp.int32, (rank, rank), 1)
    a = jnp.concatenate([gram, jnp.where(row == col, 1.0, 0.0).astype(F32)], axis=1)
    group = 4
    for k in range(0, rank, group):
        cols = [jnp.broadcast_to(a[:, k + j : k + j + 1], a.shape) for j in range(group)]
        rows = [a[k + j : k + j + 1, :] for j in range(group)]
        for j in range(group):
            pivot = cols[j][k + j : k + j + 1, :]
            wide_ref[k + j : k + j + 1, :] = rows[j] * lax.rsqrt(pivot)
            factor = cols[j] * (1.0 / pivot)
            for m in range(j + 1, group):
                cols[m] = cols[m] - factor * cols[m][k + j : k + j + 1, :]
                rows[m] = rows[m] - factor[k + m : k + m + 1, :] * rows[j]
            a = a - factor * rows[j]
    w = wide_ref[:, rank:]
    w_ref[...] = w
    lt_copy.wait()
    basis = jnp.dot(w, lt_ref[...], precision=HIGHEST, preferred_element_type=F32)
    basis_ref[...] = basis.T.astype(BF16)


def inverse_factor(loads, lt):
    rank, rows = lt.shape
    n_exp = len(loads)
    return pl.pallas_call(
        functools.partial(inverse_kernel, n_exp),
        in_specs=[HBM] + [ANY] * (n_exp - 1) + [HBM],
        out_shape=[
            jax.ShapeDtypeStruct((rank, rank), F32),
            jax.ShapeDtypeStruct((rows, rank), BF16),
        ],
        scratch_shapes=[
            pltpu.VMEM((n_exp, 3 * (rank // 2), 2 * rank), BF16),
            pltpu.VMEM((rank, rows), F32),
            pltpu.VMEM((rank, 2 * rank), F32),
            pltpu.SemaphoreType.DMA((n_exp + 1,)),
        ],
        compiler_params=params(8),
        cost_estimate=SMALL,
        name="inverse_factor",
    )(*in_hbm(loads[0]), *loads[1:], *in_hbm(lt))


def finish_kernel(replicas, w_ref, chunk_ref, basis_ref, merged_ref, right_hbm, err_hbm, right_ref, err_ref, sems):
    rank, cols = right_ref.shape
    across = cols // TILE_C
    pieces = []
    for a in range(rank // TILE_R):
        pieces.append(jnp.concatenate([chunk_ref[a * across + b] for b in range(across)], axis=1))
    product = jnp.concatenate(pieces, axis=0)
    new_right = left_times(w_ref[...], product, (((1,), (0,)), ((), ()))) * (1.0 / replicas)
    right_ref[...] = new_right
    copies = [pltpu.make_async_copy(right_ref, right_hbm, sems.at[0])]
    copies[0].start()
    rounded = new_right.astype(BF16)
    rows, block = err_ref.shape[0], 128
    for i in range(rows // block):
        here = slice(i * block, (i + 1) * block)
        approx = jnp.dot(basis_ref[here, :], rounded, preferred_element_type=F32)
        err_ref[here, :] = (merged_ref[here, :] - approx).astype(BF16)
        copies.append(
            pltpu.make_async_copy(err_ref.at[here, :], err_hbm.at[0, here, :], sems.at[i + 1])
        )
        copies[-1].start()
    for copy in copies:
        copy.wait()


def finish(replicas, w, chunks, basis, merged):
    rows, rank = basis.shape
    cols = merged.shape[1]
    return pl.pallas_call(
        functools.partial(finish_kernel, replicas),
        out_specs=[HBM] * 2,
        out_shape=[
            jax.ShapeDtypeStruct((rank, cols), F32),
            jax.ShapeDtypeStruct((1, rows, cols), BF16),
        ],
        scratch_shapes=[
            pltpu.VMEM((rank, cols), F32),
            pltpu.VMEM((rows, cols), BF16),
            pltpu.SemaphoreType.DMA((rows // 128 + 1,)),
        ],
        compiler_params=params(16),
        cost_estimate=SMALL,
        name="finish",
    )(w, chunks, basis, merged)


def expert_kernel(n_exp, chunk, *refs):
    load_hbms, grad_hbms = refs[:n_exp], refs[n_exp : 2 * n_exp]
    one_hbm, two_hbm, first_hbm, second_hbm, step_hbm = refs[2 * n_exp : 2 * n_exp + 5]
    hid, rows, one, two, first, second, step, in_sems, out_sems = refs[2 * n_exp + 5 :]
    units, width = one.shape
    tokens = grad_hbms[0].shape[1]
    count = width // chunk

    slabs = [
        pltpu.make_async_copy(load_hbms[k].at[0:units], hid.at[k], in_sems.at[count, k])
        for k in range(n_exp)
    ]

    def loads(c):
        here = slice(c * chunk, (c + 1) * chunk)
        pairs = [
            (grad_hbms[k].at[0, :, here], rows.at[k * tokens : (k + 1) * tokens, here])
            for k in range(n_exp)
        ]
        pairs += [(one_hbm.at[0, :, here], one.at[:, here]), (two_hbm.at[0, :, here], two.at[:, here])]
        return [pltpu.make_async_copy(a, b, in_sems.at[c, i]) for i, (a, b) in enumerate(pairs)]

    def stores(c):
        here = slice(c * chunk, (c + 1) * chunk)
        pairs = [(first, first_hbm), (second, second_hbm), (step, step_hbm)]
        return [
            pltpu.make_async_copy(a.at[:, here], b.at[0, :, here], out_sems.at[c, i])
            for i, (a, b) in enumerate(pairs)
        ]

    for copy in slabs:
        copy.start()
    for c in range(count):
        for copy in loads(c):
            copy.start()
    for copy in slabs:
        copy.wait()
    left = jnp.concatenate([hid[k] for k in range(n_exp)], axis=1)
    for c in range(count):
        here = slice(c * chunk, (c + 1) * chunk)
        for copy in loads(c):
            copy.wait()
        grad = jnp.dot(left, rows[:, here], preferred_element_type=F32)
        first_new = beta_one * one[:, here] + (1.0 - beta_one) * grad
        second_new = beta_two * two[:, here] + (1.0 - beta_two) * grad * grad
        first[:, here] = first_new
        second[:, here] = second_new
        scaled = second_new * (1.0 / correction_two)
        bottom = scaled * lax.rsqrt(scaled) + epsilon
        step[:, here] = (
            first_new * (1.0 / correction_one) * pl.reciprocal(bottom, approx=True)
        ).astype(BF16)
        for copy in stores(c):
            copy.start()
    for c in range(count):
        for copy in stores(c):
            copy.wait()


def expert_step(slabs, grads, moment_one, moment_two):
    _, units, width = moment_one.shape
    chunk = 512
    n_exp = len(grads)
    tokens = grads[0].shape[1]
    return pl.pallas_call(
        functools.partial(expert_kernel, n_exp, chunk),
        in_specs=([HBM] + [ANY] * (n_exp - 1)) * 2 + [HBM] * 2,
        out_specs=[HBM] * 3,
        out_shape=[
            jax.ShapeDtypeStruct((1, units, width), F32),
            jax.ShapeDtypeStruct((1, units, width), F32),
            jax.ShapeDtypeStruct((1, units, width), BF16),
        ],
        scratch_shapes=[
            pltpu.VMEM((n_exp, units, tokens), BF16),
            pltpu.VMEM((n_exp * tokens, width), BF16),
            pltpu.VMEM((units, width), F32),
            pltpu.VMEM((units, width), F32),
            pltpu.VMEM((units, width), F32),
            pltpu.VMEM((units, width), F32),
            pltpu.VMEM((units, width), BF16),
            pltpu.SemaphoreType.DMA((width // chunk + 1, n_exp + 2)),
            pltpu.SemaphoreType.DMA((width // chunk, 3)),
        ],
        compiler_params=params(24),
        cost_estimate=SMALL,
        name="expert_step",
    )(
        *in_hbm(slabs[0]), *slabs[1:], *in_hbm(grads[0]), *grads[1:], *in_hbm(moment_one, moment_two)
    )


def swap(x, axis, size, mask):
    return lax.ppermute(x, axis, [(i, i ^ mask) for i in range(size)])


def shift(x, size, k):
    return lax.ppermute(x, "exp", [(i, (i + k) % size) for i in range(size)])


def after(x, y):
    return lax.optimization_barrier((x, y))[0]


def body(n_rep, n_exp, activations, kv_grad, errors, right_factor, hidden, out_grad, moment_one, moment_two):
    grads = {0: out_grad, 1: shift(out_grad, n_exp, 1)}
    merged, lt = merge(activations, kv_grad, errors, right_factor.T)

    lt = (lt + swap(lt, "rep", n_rep, 1)).astype(BF16)
    slabs = unit_slabs(after(hidden, lt), n_exp)
    if n_exp > 2:
        grads[n_exp - 1] = shift(after(out_grad, slabs), n_exp, -1)
    bit = 2
    parts = [lt]
    while bit < n_rep:
        while len(parts) > 1:
            parts = [a.astype(F32) + b.astype(F32) for a, b in zip(parts[0::2], parts[1::2])]
        own = parts[0].astype(BF16)
        masks = [bit] if 2 * bit >= n_rep else [bit, 2 * bit, 3 * bit]
        parts = [own] + [swap(own, "rep", n_rep, m) for m in masks]
        bit *= len(parts)
    lt, chunks, loads = right_product(parts, merged, slabs)

    loads = [loads[0]] + [shift(loads[k], n_exp, k) for k in range(1, n_exp)]
    w, basis = inverse_factor(loads, lt)

    if chunks.shape[0] == n_rep * n_exp:
        both = ("rep", "exp")
        share = fold(lax.all_to_all(chunks, both, 0, 0, tiled=True))
        chunks = lax.all_to_all(share, both, 0, 0, tiled=True)
    else:
        share = chunks
        chunks = lax.psum(chunks.astype(F32), ("rep", "exp")).astype(BF16)

    left, right = 1, n_exp - 1
    while right - left > 1:
        if left <= n_exp - right:
            grads[left + 1] = shift(after(grads[left], share), n_exp, 1)
            left += 1
        else:
            grads[right - 1] = shift(after(grads[right], share), n_exp, -1)
            right -= 1

    new_right, new_error = finish(n_rep, w, chunks, basis, merged)
    first_new, second_new, step = expert_step(
        loads, [grads[k] for k in range(n_exp)], moment_one, moment_two
    )
    return new_error, new_right.T, first_new, second_new, step


def solution(mesh):
    placed = (
        P("rep", "exp"),
        P("rep", None),
        P("rep", "exp", None),
        P(),
        P("rep", "exp", None),
        P("rep", "exp", None),
        P("rep", "exp", None),
        P("rep", "exp", None),
    )
    return jax.shard_map(
        functools.partial(body, mesh.shape["rep"], mesh.shape["exp"]),
        mesh=mesh,
        in_specs=placed,
        out_specs=(
            P("rep", "exp", None),
            P(),
            P("rep", "exp", None),
            P("rep", "exp", None),
            P("rep", "exp", None),
        ),
        check_vma=False,
    )
```

```python
import functools

import jax
import jax.numpy as jnp
from jax import lax
from jax.experimental import pallas as pl
from jax.experimental.pallas import tpu as pltpu
from jax.sharding import PartitionSpec as P

HIGHEST = lax.Precision.HIGHEST
F32 = jnp.float32
BF16 = jnp.bfloat16
beta_one = 0.9
beta_two = 0.99
correction_one = 1.0 - 0.9**10
correction_two = 1.0 - 0.99**10
epsilon = 1e-08

ROWS_FIRST = (((0,), (0,)), ((), ()))
COLS_LAST = (((1,), (1,)), ((), ()))
TILE_R, TILE_C = 16, 128
HBM = pl.BlockSpec(memory_space=pltpu.HBM)
ANY = pl.BlockSpec(memory_space=pl.ANY)
VMEM = pl.BlockSpec(memory_space=pltpu.VMEM)


def params(mebibytes):
    return pltpu.CompilerParams(vmem_limit_bytes=mebibytes * 1024 * 1024)


def in_hbm(*arrays):
    return [pltpu.with_memory_space_constraint(x, pltpu.HBM) for x in arrays]


SMALL = pl.CostEstimate(flops=1000, bytes_accessed=1000, transcendentals=0)


def split_two(x):
    hi = x.astype(BF16)
    return hi, (x - hi.astype(F32)).astype(BF16)


def left_times(left, right_bf16, dims):
    rows = left.shape[0]
    hi, lo = split_two(left)
    both = jnp.concatenate([hi, lo], axis=0)
    out = lax.dot_general(both, right_bf16, dims, preferred_element_type=F32)
    return out[:rows] + out[rows:]


def merge_kernel(acts_ref, kv_ref, err_ref, vt_ref, merged_ref, lt_ref):
    merged = lax.dot_general(acts_ref[...], kv_ref[...], ROWS_FIRST, preferred_element_type=F32)
    merged = merged + err_ref[0].astype(F32)
    merged_ref[...] = merged
    lt_ref[...] = left_times(vt_ref[...], merged.astype(BF16), COLS_LAST)


def merge(acts, kv, err, vt):
    tokens, rows = acts.shape
    cols = kv.shape[1]
    rank = vt.shape[0]
    block = 256
    return pl.pallas_call(
        merge_kernel,
        grid=(rows // block,),
        in_specs=[
            pl.BlockSpec((tokens, block), lambda i: (0, i)),
            pl.BlockSpec((tokens, cols), lambda i: (0, 0)),
            pl.BlockSpec((1, block, cols), lambda i: (0, i, 0)),
            pl.BlockSpec((rank, cols), lambda i: (0, 0)),
        ],
        out_specs=[
            pl.BlockSpec((block, cols), lambda i: (i, 0)),
            pl.BlockSpec((rank, block), lambda i: (0, i)),
        ],
        out_shape=[
            jax.ShapeDtypeStruct((rows, cols), F32),
            jax.ShapeDtypeStruct((rank, rows), F32),
        ],
        compiler_params=params(24),
        cost_estimate=SMALL,
        name="merge",
    )(*[pltpu.with_memory_space_constraint(x, pltpu.HBM) for x in (acts, kv, err, vt)])


def slab_kernel(hidden_ref, own_ref, *refs):
    send_refs, all_ref = refs[:-1], refs[-1]
    n_exp = all_ref.shape[0]
    all_ref[...] = hidden_ref[0].T.reshape(all_ref.shape)
    place = lax.axis_index("exp")
    for k, ref in enumerate((own_ref,) + tuple(send_refs)):
        ref[...] = all_ref[lax.rem(place + k, n_exp)]


def unit_slabs(hidden, n_exp):
    _, tokens, units = hidden.shape
    slab = (units // n_exp, tokens)
    return pl.pallas_call(
        slab_kernel,
        out_shape=[jax.ShapeDtypeStruct(slab, BF16)] * n_exp,
        scratch_shapes=[pltpu.VMEM((n_exp,) + slab, BF16)],
        compiler_params=params(8),
        cost_estimate=SMALL,
        name="unit_slabs",
    )(hidden)


def right_kernel(n_parts, *refs):
    part_refs, merged_ref = refs[:n_parts], refs[n_parts]
    lt_ref, gram_ref, chunk_ref = refs[n_parts + 1 :]
    parts = [ref[...].astype(F32) for ref in part_refs]
    while len(parts) > 1:
        parts = [a + b for a, b in zip(parts[0::2], parts[1::2])]
    lt = parts[0]
    rank = lt.shape[0]
    lt_ref[...] = lt
    product = left_times(lt, merged_ref[...].astype(BF16), (((1,), (0,)), ((), ()))).astype(BF16)
    across = product.shape[1] // TILE_C
    for a in range(rank // TILE_R):
        for b in range(across):
            chunk_ref[a * across + b] = product[
                a * TILE_R : (a + 1) * TILE_R, b * TILE_C : (b + 1) * TILE_C
            ]
    gram = lax.dot_general(lt, lt, COLS_LAST, precision=HIGHEST, preferred_element_type=F32)
    half = rank // 2
    packed = jnp.concatenate([gram[:half], gram[half:]], axis=1)
    high = packed.astype(BF16)
    rest = packed - high.astype(F32)
    middle = rest.astype(BF16)
    low = (rest - middle.astype(F32)).astype(BF16)
    gram_ref[0:half] = high
    gram_ref[half : 2 * half] = middle
    gram_ref[2 * half : 3 * half] = low


def right_product(parts, merged):
    rank, rows = parts[0].shape
    cols = merged.shape[1]
    chunks = rank * cols // (TILE_R * TILE_C)
    return pl.pallas_call(
        functools.partial(right_kernel, len(parts)),
        out_shape=[
            jax.ShapeDtypeStruct((rank, rows), F32),
            jax.ShapeDtypeStruct((3 * (rank // 2), 2 * rank), BF16),
            jax.ShapeDtypeStruct((chunks, TILE_R, TILE_C), BF16),
        ],
        compiler_params=params(16),
        cost_estimate=SMALL,
        name="right_product",
    )(*parts, merged)


def fold_kernel(share_ref, out_ref):
    total = share_ref[0].astype(F32)
    for i in range(1, share_ref.shape[0]):
        total = total + share_ref[i].astype(F32)
    total = total.astype(BF16)
    for i in range(out_ref.shape[0]):
        out_ref[i] = total


def fold(shares):
    return pl.pallas_call(
        fold_kernel,
        out_shape=jax.ShapeDtypeStruct(shares.shape, BF16),
        compiler_params=params(4),
        cost_estimate=SMALL,
        name="fold",
    )(shares)


def inverse_kernel(n_exp, *refs):
    load_hbms, lt_hbm = refs[:n_exp], refs[n_exp]
    w_ref, basis_ref, terms_ref, lt_ref, wide_ref, sems = refs[n_exp + 1 :]
    rank = lt_ref.shape[0]
    half = rank // 2
    copies = [
        pltpu.make_async_copy(load_hbms[k], terms_ref.at[k], sems.at[k])
        for k in range(n_exp)
    ]
    lt_copy = pltpu.make_async_copy(lt_hbm, lt_ref, sems.at[n_exp])
    for copy in copies:
        copy.start()
    lt_copy.start()
    for copy in copies:
        copy.wait()
    place = lax.axis_index("exp")
    packed = None
    for j in range(n_exp):
        terms = terms_ref[lax.rem(place + n_exp - j, n_exp)].astype(F32)
        part = terms[:half] + terms[half : 2 * half] + terms[2 * half :]
        packed = part if packed is None else packed + part
    gram = jnp.concatenate([packed[:, :rank], packed[:, rank:]], axis=0)
    row = lax.broadcasted_iota(jnp.int32, (rank, rank), 0)
    col = lax.broadcasted_iota(jnp.int32, (rank, rank), 1)
    a = jnp.concatenate([gram, jnp.where(row == col, 1.0, 0.0).astype(F32)], axis=1)
    group = 4
    for k in range(0, rank, group):
        cols = [jnp.broadcast_to(a[:, k + j : k + j + 1], a.shape) for j in range(group)]
        rows = [a[k + j : k + j + 1, :] for j in range(group)]
        for j in range(group):
            pivot = cols[j][k + j : k + j + 1, :]
            wide_ref[k + j : k + j + 1, :] = rows[j] * lax.rsqrt(pivot)
            factor = cols[j] * (1.0 / pivot)
            for m in range(j + 1, group):
                cols[m] = cols[m] - factor * cols[m][k + j : k + j + 1, :]
                rows[m] = rows[m] - factor[k + m : k + m + 1, :] * rows[j]
            a = a - factor * rows[j]
    w = wide_ref[:, rank:]
    w_ref[...] = w
    lt_copy.wait()
    basis = jnp.dot(w, lt_ref[...], precision=HIGHEST, preferred_element_type=F32)
    basis_ref[...] = basis.T.astype(BF16)


def inverse_factor(loads, lt):
    rank, rows = lt.shape
    n_exp = len(loads)
    return pl.pallas_call(
        functools.partial(inverse_kernel, n_exp),
        in_specs=[ANY] * (n_exp + 1),
        out_shape=[
            jax.ShapeDtypeStruct((rank, rank), F32),
            jax.ShapeDtypeStruct((rows, rank), BF16),
        ],
        scratch_shapes=[
            pltpu.VMEM((n_exp, 3 * (rank // 2), 2 * rank), BF16),
            pltpu.VMEM((rank, rows), F32),
            pltpu.VMEM((rank, 2 * rank), F32),
            pltpu.SemaphoreType.DMA((n_exp + 1,)),
        ],
        compiler_params=params(8),
        cost_estimate=SMALL,
        name="inverse_factor",
    )(*loads, lt)


def finish_kernel(
    replicas, w_any, chunk_ref, basis_any, merged_ref, right_hbm, err_hbm, w_ref, basis_ref, right_ref, err_ref, sems
):
    rank, cols = right_ref.shape
    rows, block = err_ref.shape[0], 128
    w_copy = pltpu.make_async_copy(w_any, w_ref, sems.at[rows // block + 1])
    w_copy.start()
    basis_copy = pltpu.make_async_copy(basis_any, basis_ref, sems.at[rows // block + 2])
    basis_copy.start()
    across = cols // TILE_C
    pieces = []
    for a in range(rank // TILE_R):
        pieces.append(jnp.concatenate([chunk_ref[a * across + b] for b in range(across)], axis=1))
    product = jnp.concatenate(pieces, axis=0)
    w_copy.wait()
    new_right = left_times(w_ref[...], product, (((1,), (0,)), ((), ()))) * (1.0 / replicas)
    right_ref[...] = new_right
    copies = [pltpu.make_async_copy(right_ref, right_hbm, sems.at[0])]
    copies[0].start()
    rounded = new_right.astype(BF16)
    basis_copy.wait()
    for i in range(rows // block):
        here = slice(i * block, (i + 1) * block)
        approx = jnp.dot(basis_ref[here, :], rounded, preferred_element_type=F32)
        err_ref[here, :] = (merged_ref[here, :] - approx).astype(BF16)
        copies.append(
            pltpu.make_async_copy(err_ref.at[here, :], err_hbm.at[0, here, :], sems.at[i + 1])
        )
        copies[-1].start()
    for copy in copies:
        copy.wait()


def finish(replicas, w, chunks, basis, merged):
    rows, rank = basis.shape
    cols = merged.shape[1]
    return pl.pallas_call(
        functools.partial(finish_kernel, replicas),
        in_specs=[ANY, VMEM, ANY, VMEM],
        out_specs=[HBM] * 2,
        out_shape=[
            jax.ShapeDtypeStruct((rank, cols), F32),
            jax.ShapeDtypeStruct((1, rows, cols), BF16),
        ],
        scratch_shapes=[
            pltpu.VMEM((rank, rank), F32),
            pltpu.VMEM((rows, rank), BF16),
            pltpu.VMEM((rank, cols), F32),
            pltpu.VMEM((rows, cols), BF16),
            pltpu.SemaphoreType.DMA((rows // 128 + 3,)),
        ],
        compiler_params=params(16),
        cost_estimate=SMALL,
        name="finish",
    )(w, chunks, basis, merged)


def expert_kernel(n_exp, chunk, *refs):
    load_hbms, grad_hbms = refs[:n_exp], refs[n_exp : 2 * n_exp]
    one_hbm, two_hbm, first_hbm, second_hbm, step_hbm = refs[2 * n_exp : 2 * n_exp + 5]
    hid, rows, one, two, first, second, step, in_sems, out_sems = refs[2 * n_exp + 5 :]
    units, width = one.shape
    tokens = grad_hbms[0].shape[1]
    count = width // chunk

    slabs = [
        pltpu.make_async_copy(load_hbms[k], hid.at[k], in_sems.at[count, k])
        for k in range(n_exp)
    ]

    def loads(c):
        here = slice(c * chunk, (c + 1) * chunk)
        pairs = [
            (grad_hbms[k].at[0, :, here], rows.at[k * tokens : (k + 1) * tokens, here])
            for k in range(n_exp)
        ]
        pairs += [(one_hbm.at[0, :, here], one.at[:, here]), (two_hbm.at[0, :, here], two.at[:, here])]
        return [pltpu.make_async_copy(a, b, in_sems.at[c, i]) for i, (a, b) in enumerate(pairs)]

    def stores(c):
        here = slice(c * chunk, (c + 1) * chunk)
        pairs = [(first, first_hbm), (second, second_hbm), (step, step_hbm)]
        return [
            pltpu.make_async_copy(a.at[:, here], b.at[0, :, here], out_sems.at[c, i])
            for i, (a, b) in enumerate(pairs)
        ]

    for copy in slabs:
        copy.start()
    for c in range(count):
        for copy in loads(c):
            copy.start()
    for copy in slabs:
        copy.wait()
    left = jnp.concatenate([hid[k] for k in range(n_exp)], axis=1)
    for c in range(count):
        here = slice(c * chunk, (c + 1) * chunk)
        for copy in loads(c):
            copy.wait()
        grad = jnp.dot(left, rows[:, here], preferred_element_type=F32)
        first_new = beta_one * one[:, here] + (1.0 - beta_one) * grad
        second_new = beta_two * two[:, here] + (1.0 - beta_two) * grad * grad
        first[:, here] = first_new
        second[:, here] = second_new
        scaled = second_new * (1.0 / correction_two)
        bottom = scaled * lax.rsqrt(scaled) + epsilon
        step[:, here] = (
            first_new * (1.0 / correction_one) * pl.reciprocal(bottom, approx=True)
        ).astype(BF16)
        for copy in stores(c):
            copy.start()
    for c in range(count):
        for copy in stores(c):
            copy.wait()


def expert_step(slabs, grads, moment_one, moment_two):
    _, units, width = moment_one.shape
    chunk = 512
    n_exp = len(grads)
    tokens = grads[0].shape[1]
    return pl.pallas_call(
        functools.partial(expert_kernel, n_exp, chunk),
        in_specs=[ANY] * n_exp + [HBM] + [ANY] * (n_exp - 1) + [HBM] * 2,
        out_specs=[HBM] * 3,
        out_shape=[
            jax.ShapeDtypeStruct((1, units, width), F32),
            jax.ShapeDtypeStruct((1, units, width), F32),
            jax.ShapeDtypeStruct((1, units, width), BF16),
        ],
        scratch_shapes=[
            pltpu.VMEM((n_exp, units, tokens), BF16),
            pltpu.VMEM((n_exp * tokens, width), BF16),
            pltpu.VMEM((units, width), F32),
            pltpu.VMEM((units, width), F32),
            pltpu.VMEM((units, width), F32),
            pltpu.VMEM((units, width), F32),
            pltpu.VMEM((units, width), BF16),
            pltpu.SemaphoreType.DMA((width // chunk + 1, n_exp + 2)),
            pltpu.SemaphoreType.DMA((width // chunk, 3)),
        ],
        compiler_params=params(24),
        cost_estimate=SMALL,
        name="expert_step",
    )(
        *slabs, *in_hbm(grads[0]), *grads[1:], *in_hbm(moment_one, moment_two)
    )


def swap(x, axis, size, mask):
    return lax.ppermute(x, axis, [(i, i ^ mask) for i in range(size)])


def shift(x, size, k):
    return lax.ppermute(x, "exp", [(i, (i + k) % size) for i in range(size)])


def after(x, y):
    return lax.optimization_barrier((x, y))[0]


def body(n_rep, n_exp, activations, kv_grad, errors, right_factor, hidden, out_grad, moment_one, moment_two):
    grads = {0: out_grad, 1: shift(out_grad, n_exp, 1)}
    if n_exp > 2:
        grads[n_exp - 1] = shift(out_grad, n_exp, -1)
    merged, lt = merge(activations, kv_grad, errors, right_factor.T)

    lt = (lt + swap(lt, "rep", n_rep, 1)).astype(BF16)
    slabs = unit_slabs(after(hidden, lt), n_exp)
    bit = 2
    parts = [lt]
    while bit < n_rep:
        while len(parts) > 1:
            parts = [a.astype(F32) + b.astype(F32) for a, b in zip(parts[0::2], parts[1::2])]
        own = parts[0].astype(BF16)
        masks = [bit] if 2 * bit >= n_rep else [bit, 2 * bit, 3 * bit]
        parts = [own] + [swap(own, "rep", n_rep, m) for m in masks]
        bit *= len(parts)
    lt, gram, chunks = right_product(parts, merged)

    slabs = [slabs[0]] + [shift(after(slabs[k], gram), n_exp, k) for k in range(1, n_exp)]
    grams = [gram] + [shift(gram, n_exp, k) for k in range(1, n_exp)]

    if chunks.shape[0] == n_rep * n_exp:
        both = ("rep", "exp")
        shares = lax.all_to_all(chunks, both, 0, 0, tiled=True)
        shares, grams, grads = lax.optimization_barrier((shares, grams, grads))
        share = fold(shares)
        chunks = lax.all_to_all(share, both, 0, 0, tiled=True)
    else:
        share = chunks
        chunks = lax.psum(chunks.astype(F32), ("rep", "exp")).astype(BF16)
    w, basis = inverse_factor(grams, lt)

    left, right = 1, n_exp - 1
    while right - left > 1:
        if left <= n_exp - right:
            grads[left + 1] = shift(after(grads[left], share), n_exp, 1)
            left += 1
        else:
            grads[right - 1] = shift(after(grads[right], share), n_exp, -1)
            right -= 1

    new_right, new_error = finish(n_rep, w, chunks, basis, merged)
    first_new, second_new, step = expert_step(
        slabs, [grads[k] for k in range(n_exp)], moment_one, moment_two
    )
    return new_error, new_right.T, first_new, second_new, step


def solution(mesh):
    placed = (
        P("rep", "exp"),
        P("rep", None),
        P("rep", "exp", None),
        P(),
        P("rep", "exp", None),
        P("rep", "exp", None),
        P("rep", "exp", None),
        P("rep", "exp", None),
    )
    return jax.shard_map(
        functools.partial(body, mesh.shape["rep"], mesh.shape["exp"]),
        mesh=mesh,
        in_specs=placed,
        out_specs=(
            P("rep", "exp", None),
            P(),
            P("rep", "exp", None),
            P("rep", "exp", None),
            P("rep", "exp", None),
        ),
        check_vma=False,
    )
```

```python
import functools

import jax
import jax.numpy as jnp
from jax import lax
from jax.experimental import pallas as pl
from jax.experimental.pallas import tpu as pltpu
from jax.sharding import PartitionSpec as P

HIGHEST = lax.Precision.HIGHEST
F32 = jnp.float32
BF16 = jnp.bfloat16
beta_one = 0.9
beta_two = 0.99
correction_one = 1.0 - 0.9**10
correction_two = 1.0 - 0.99**10
epsilon = 1e-08

ROWS_FIRST = (((0,), (0,)), ((), ()))
COLS_LAST = (((1,), (1,)), ((), ()))
TILE_R, TILE_C = 16, 128
HBM = pl.BlockSpec(memory_space=pltpu.HBM)
ANY = pl.BlockSpec(memory_space=pl.ANY)
VMEM = pl.BlockSpec(memory_space=pltpu.VMEM)


def params(mebibytes):
    return pltpu.CompilerParams(vmem_limit_bytes=mebibytes * 1024 * 1024)


def in_hbm(*arrays):
    return [pltpu.with_memory_space_constraint(x, pltpu.HBM) for x in arrays]


SMALL = pl.CostEstimate(flops=1000, bytes_accessed=1000, transcendentals=0)


def split_two(x):
    hi = x.astype(BF16)
    return hi, (x - hi.astype(F32)).astype(BF16)


def left_times(left, right_bf16, dims):
    rows = left.shape[0]
    hi, lo = split_two(left)
    both = jnp.concatenate([hi, lo], axis=0)
    out = lax.dot_general(both, right_bf16, dims, preferred_element_type=F32)
    return out[:rows] + out[rows:]


def merge_kernel(acts_ref, kv_ref, err_ref, vt_ref, merged_ref, lt_ref):
    merged = lax.dot_general(acts_ref[...], kv_ref[...], ROWS_FIRST, preferred_element_type=F32)
    merged = merged + err_ref[0].astype(F32)
    merged_ref[...] = merged
    lt_ref[...] = left_times(vt_ref[...], merged.astype(BF16), COLS_LAST)


def merge(acts, kv, err, vt):
    tokens, rows = acts.shape
    cols = kv.shape[1]
    rank = vt.shape[0]
    block = 256
    return pl.pallas_call(
        merge_kernel,
        grid=(rows // block,),
        in_specs=[
            pl.BlockSpec((tokens, block), lambda i: (0, i)),
            pl.BlockSpec((tokens, cols), lambda i: (0, 0)),
            pl.BlockSpec((1, block, cols), lambda i: (0, i, 0)),
            pl.BlockSpec((rank, cols), lambda i: (0, 0)),
        ],
        out_specs=[
            pl.BlockSpec((block, cols), lambda i: (i, 0)),
            pl.BlockSpec((rank, block), lambda i: (0, i)),
        ],
        out_shape=[
            jax.ShapeDtypeStruct((rows, cols), F32),
            jax.ShapeDtypeStruct((rank, rows), F32),
        ],
        compiler_params=params(24),
        cost_estimate=SMALL,
        name="merge",
    )(*[pltpu.with_memory_space_constraint(x, pltpu.HBM) for x in (acts, kv, err, vt)])


def slab_kernel(hidden_ref, own_ref, *refs):
    send_refs, all_ref = refs[:-1], refs[-1]
    n_exp = all_ref.shape[0]
    all_ref[...] = hidden_ref[0].T.reshape(all_ref.shape)
    place = lax.axis_index("exp")
    for k, ref in enumerate((own_ref,) + tuple(send_refs)):
        ref[...] = all_ref[lax.rem(place + k, n_exp)]


def unit_slabs(hidden, n_exp):
    _, tokens, units = hidden.shape
    slab = (units // n_exp, tokens)
    return pl.pallas_call(
        slab_kernel,
        out_shape=[jax.ShapeDtypeStruct(slab, BF16)] * n_exp,
        scratch_shapes=[pltpu.VMEM((n_exp,) + slab, BF16)],
        compiler_params=params(8),
        cost_estimate=SMALL,
        name="unit_slabs",
    )(hidden)


def right_kernel(n_parts, *refs):
    part_refs, merged_ref = refs[:n_parts], refs[n_parts]
    lt_ref, gram_ref, keep_ref, send_ref, all_ref = refs[n_parts + 1 :]
    parts = [ref[...].astype(F32) for ref in part_refs]
    while len(parts) > 1:
        parts = [a + b for a, b in zip(parts[0::2], parts[1::2])]
    lt = parts[0]
    rank = lt.shape[0]
    lt_ref[...] = lt
    product = left_times(lt, merged_ref[...].astype(BF16), (((1,), (0,)), ((), ())))
    across = product.shape[1] // TILE_C
    for a in range(rank // TILE_R):
        for b in range(across):
            at = (a * across + b) * TILE_R
            all_ref[at : at + TILE_R, :] = product[
                a * TILE_R : (a + 1) * TILE_R, b * TILE_C : (b + 1) * TILE_C
            ]
    cut(0, all_ref, keep_ref, send_ref)
    gram = lax.dot_general(lt, lt, COLS_LAST, precision=HIGHEST, preferred_element_type=F32)
    half = rank // 2
    packed = jnp.concatenate([gram[:half], gram[half:]], axis=1)
    high = packed.astype(BF16)
    rest = packed - high.astype(F32)
    middle = rest.astype(BF16)
    low = (rest - middle.astype(F32)).astype(BF16)
    gram_ref[0:half] = high
    gram_ref[half : 2 * half] = middle
    gram_ref[2 * half : 3 * half] = low


def my_bit(bit):
    return lax.rem(lax.axis_index("rep") // (1 << bit), 2)


def rows_of(which, count):
    return pl.ds(pl.multiple_of(which * count, count), count)


def cut(bit, all_ref, keep_ref, send_ref):
    half = keep_ref.shape[0]
    mine = my_bit(bit)
    keep_ref[...] = all_ref[rows_of(mine, half), :]
    send_ref[...] = all_ref[rows_of(1 - mine, half), :].astype(BF16)


def right_product(parts, merged):
    rank, rows = parts[0].shape
    cols = merged.shape[1]
    tall = rank * cols // TILE_C
    return pl.pallas_call(
        functools.partial(right_kernel, len(parts)),
        out_shape=[
            jax.ShapeDtypeStruct((rank, rows), F32),
            jax.ShapeDtypeStruct((3 * (rank // 2), 2 * rank), BF16),
            jax.ShapeDtypeStruct((tall // 2, TILE_C), F32),
            jax.ShapeDtypeStruct((tall // 2, TILE_C), BF16),
        ],
        scratch_shapes=[pltpu.VMEM((tall, TILE_C), F32)],
        compiler_params=params(16),
        cost_estimate=SMALL,
        name="right_product",
    )(*parts, merged)


def halve_kernel(bit, keep_ref, got_ref, next_ref, send_ref, all_ref):
    all_ref[...] = keep_ref[...] + got_ref[...].astype(F32)
    cut(bit, all_ref, next_ref, send_ref)


def halve(bit, keep, got):
    rows = keep.shape[0]
    return pl.pallas_call(
        functools.partial(halve_kernel, bit),
        out_shape=[
            jax.ShapeDtypeStruct((rows // 2, TILE_C), F32),
            jax.ShapeDtypeStruct((rows // 2, TILE_C), BF16),
        ],
        scratch_shapes=[pltpu.VMEM((rows, TILE_C), F32)],
        compiler_params=params(4),
        cost_estimate=SMALL,
        name="halve",
    )(keep, got)


def load_kernel(keep_ref, got_ref, gram_ref, load_ref):
    terms = gram_ref.shape[0]
    load_ref[0:terms] = gram_ref[...]
    load_ref[terms:] = (keep_ref[...] + got_ref[...].astype(F32)).astype(BF16)


def line_load(keep, got, gram):
    return pl.pallas_call(
        load_kernel,
        out_shape=jax.ShapeDtypeStruct((gram.shape[0] + keep.shape[0], TILE_C), BF16),
        compiler_params=params(4),
        cost_estimate=SMALL,
        name="line_load",
    )(keep, got, gram)


def line_kernel(terms, *refs):
    load_refs, out_ref, parts_ref = refs[:-2], refs[-2], refs[-1]
    n_exp = len(load_refs)
    for k in range(n_exp):
        parts_ref[k] = load_refs[k][terms:].astype(F32)
    place = lax.axis_index("exp")
    total = None
    for j in range(n_exp):
        part = parts_ref[lax.rem(place + n_exp - j, n_exp)]
        total = part if total is None else total + part
    out_ref[...] = total.astype(BF16)


def line_sum(loads, terms):
    rows = loads[0].shape[0] - terms
    return pl.pallas_call(
        functools.partial(line_kernel, terms),
        out_shape=jax.ShapeDtypeStruct((rows, TILE_C), BF16),
        scratch_shapes=[pltpu.VMEM((len(loads), rows, TILE_C), F32)],
        compiler_params=params(4),
        cost_estimate=SMALL,
        name="line_sum",
    )(*loads)


def double_kernel(bit, own_ref, got_ref, out_ref):
    half = own_ref.shape[0]
    mine = my_bit(bit)
    out_ref[rows_of(mine, half), :] = own_ref[...]
    out_ref[rows_of(1 - mine, half), :] = got_ref[...]


def double(bit, own, got):
    rows = own.shape[0]
    return pl.pallas_call(
        functools.partial(double_kernel, bit),
        out_shape=jax.ShapeDtypeStruct((2 * rows, TILE_C), BF16),
        compiler_params=params(4),
        cost_estimate=SMALL,
        name="double",
    )(own, got)


def inverse_kernel(n_exp, *refs):
    load_hbms, lt_hbm = refs[:n_exp], refs[n_exp]
    w_ref, basis_ref, terms_ref, lt_ref, wide_ref, sems = refs[n_exp + 1 :]
    rank = lt_ref.shape[0]
    half = rank // 2
    copies = [
        pltpu.make_async_copy(load_hbms[k].at[0 : 3 * half], terms_ref.at[k], sems.at[k])
        for k in range(n_exp)
    ]
    lt_copy = pltpu.make_async_copy(lt_hbm, lt_ref, sems.at[n_exp])
    for copy in copies:
        copy.start()
    lt_copy.start()
    for copy in copies:
        copy.wait()
    place = lax.axis_index("exp")
    packed = None
    for j in range(n_exp):
        terms = terms_ref[lax.rem(place + n_exp - j, n_exp)].astype(F32)
        part = terms[:half] + terms[half : 2 * half] + terms[2 * half :]
        packed = part if packed is None else packed + part
    gram = jnp.concatenate([packed[:, :rank], packed[:, rank:]], axis=0)
    row = lax.broadcasted_iota(jnp.int32, (rank, rank), 0)
    col = lax.broadcasted_iota(jnp.int32, (rank, rank), 1)
    a = jnp.concatenate([gram, jnp.where(row == col, 1.0, 0.0).astype(F32)], axis=1)
    group = 4
    for k in range(0, rank, group):
        cols = [jnp.broadcast_to(a[:, k + j : k + j + 1], a.shape) for j in range(group)]
        rows = [a[k + j : k + j + 1, :] for j in range(group)]
        for j in range(group):
            pivot = cols[j][k + j : k + j + 1, :]
            wide_ref[k + j : k + j + 1, :] = rows[j] * lax.rsqrt(pivot)
            factor = cols[j] * (1.0 / pivot)
            for m in range(j + 1, group):
                cols[m] = cols[m] - factor * cols[m][k + j : k + j + 1, :]
                rows[m] = rows[m] - factor[k + m : k + m + 1, :] * rows[j]
            a = a - factor * rows[j]
    w = wide_ref[:, rank:]
    w_ref[...] = w
    lt_copy.wait()
    basis = jnp.dot(w, lt_ref[...], precision=HIGHEST, preferred_element_type=F32)
    basis_ref[...] = basis.T.astype(BF16)


def inverse_factor(loads, lt):
    rank, rows = lt.shape
    n_exp = len(loads)
    return pl.pallas_call(
        functools.partial(inverse_kernel, n_exp),
        in_specs=[ANY] * (n_exp + 1),
        out_shape=[
            jax.ShapeDtypeStruct((rank, rank), F32),
            jax.ShapeDtypeStruct((rows, rank), BF16),
        ],
        scratch_shapes=[
            pltpu.VMEM((n_exp, 3 * (rank // 2), 2 * rank), BF16),
            pltpu.VMEM((rank, rows), F32),
            pltpu.VMEM((rank, 2 * rank), F32),
            pltpu.SemaphoreType.DMA((n_exp + 1,)),
        ],
        compiler_params=params(8),
        cost_estimate=SMALL,
        name="inverse_factor",
    )(*loads, lt)


def finish_kernel(
    replicas, w_ref, own_ref, got_ref, basis_ref, merged_ref, right_hbm, err_hbm, all_ref, right_ref, err_ref, sems
):
    rank, cols = right_ref.shape
    rows, block = err_ref.shape[0], 128
    double_kernel(0, own_ref, got_ref, all_ref)
    across = cols // TILE_C
    pieces = []
    for a in range(rank // TILE_R):
        at = [(a * across + b) * TILE_R for b in range(across)]
        pieces.append(jnp.concatenate([all_ref[i : i + TILE_R, :] for i in at], axis=1))
    product = jnp.concatenate(pieces, axis=0)
    new_right = left_times(w_ref[...], product, (((1,), (0,)), ((), ()))) * (1.0 / replicas)
    right_ref[...] = new_right
    copies = [pltpu.make_async_copy(right_ref, right_hbm, sems.at[0])]
    copies[0].start()
    rounded = new_right.astype(BF16)
    for i in range(rows // block):
        here = slice(i * block, (i + 1) * block)
        approx = jnp.dot(basis_ref[here, :], rounded, preferred_element_type=F32)
        err_ref[here, :] = (merged_ref[here, :] - approx).astype(BF16)
        copies.append(
            pltpu.make_async_copy(err_ref.at[here, :], err_hbm.at[0, here, :], sems.at[i + 1])
        )
        copies[-1].start()
    for copy in copies:
        copy.wait()


def finish(replicas, w, own, got, basis, merged):
    rows, rank = basis.shape
    cols = merged.shape[1]
    return pl.pallas_call(
        functools.partial(finish_kernel, replicas),
        in_specs=[VMEM] * 5,
        out_specs=[HBM] * 2,
        out_shape=[
            jax.ShapeDtypeStruct((rank, cols), F32),
            jax.ShapeDtypeStruct((1, rows, cols), BF16),
        ],
        scratch_shapes=[
            pltpu.VMEM((2 * own.shape[0], TILE_C), BF16),
            pltpu.VMEM((rank, cols), F32),
            pltpu.VMEM((rows, cols), BF16),
            pltpu.SemaphoreType.DMA((rows // 128 + 1,)),
        ],
        compiler_params=params(16),
        cost_estimate=SMALL,
        name="finish",
    )(w, own, got, basis, merged)


def expert_kernel(n_exp, chunk, *refs):
    load_hbms, grad_hbms = refs[:n_exp], refs[n_exp : 2 * n_exp]
    one_hbm, two_hbm, first_hbm, second_hbm, step_hbm = refs[2 * n_exp : 2 * n_exp + 5]
    hid, rows, one, two, first, second, step, in_sems, out_sems = refs[2 * n_exp + 5 :]
    units, width = one.shape
    tokens = grad_hbms[0].shape[1]
    count = width // chunk

    slabs = [
        pltpu.make_async_copy(load_hbms[k], hid.at[k], in_sems.at[count, k])
        for k in range(n_exp)
    ]

    def loads(c):
        here = slice(c * chunk, (c + 1) * chunk)
        pairs = [
            (grad_hbms[k].at[0, :, here], rows.at[k * tokens : (k + 1) * tokens, here])
            for k in range(n_exp)
        ]
        pairs += [(one_hbm.at[0, :, here], one.at[:, here]), (two_hbm.at[0, :, here], two.at[:, here])]
        return [pltpu.make_async_copy(a, b, in_sems.at[c, i]) for i, (a, b) in enumerate(pairs)]

    def stores(c):
        here = slice(c * chunk, (c + 1) * chunk)
        pairs = [(first, first_hbm), (second, second_hbm), (step, step_hbm)]
        return [
            pltpu.make_async_copy(a.at[:, here], b.at[0, :, here], out_sems.at[c, i])
            for i, (a, b) in enumerate(pairs)
        ]

    for copy in slabs:
        copy.start()
    for c in range(count):
        for copy in loads(c):
            copy.start()
    for copy in slabs:
        copy.wait()
    left = jnp.concatenate([hid[k] for k in range(n_exp)], axis=1)
    for c in range(count):
        here = slice(c * chunk, (c + 1) * chunk)
        for copy in loads(c):
            copy.wait()
        grad = jnp.dot(left, rows[:, here], preferred_element_type=F32)
        first_new = beta_one * one[:, here] + (1.0 - beta_one) * grad
        second_new = beta_two * two[:, here] + (1.0 - beta_two) * grad * grad
        first[:, here] = first_new
        second[:, here] = second_new
        scaled = second_new * (1.0 / correction_two)
        bottom = scaled * lax.rsqrt(scaled) + epsilon
        step[:, here] = (
            first_new * (1.0 / correction_one) * pl.reciprocal(bottom, approx=True)
        ).astype(BF16)
        for copy in stores(c):
            copy.start()
    for c in range(count):
        for copy in stores(c):
            copy.wait()


def expert_step(slabs, grads, moment_one, moment_two):
    _, units, width = moment_one.shape
    chunk = 512
    n_exp = len(grads)
    tokens = grads[0].shape[1]
    return pl.pallas_call(
        functools.partial(expert_kernel, n_exp, chunk),
        in_specs=[ANY] * n_exp + [HBM] + [ANY] * (n_exp - 1) + [HBM] * 2,
        out_specs=[HBM] * 3,
        out_shape=[
            jax.ShapeDtypeStruct((1, units, width), F32),
            jax.ShapeDtypeStruct((1, units, width), F32),
            jax.ShapeDtypeStruct((1, units, width), BF16),
        ],
        scratch_shapes=[
            pltpu.VMEM((n_exp, units, tokens), BF16),
            pltpu.VMEM((n_exp * tokens, width), BF16),
            pltpu.VMEM((units, width), F32),
            pltpu.VMEM((units, width), F32),
            pltpu.VMEM((units, width), F32),
            pltpu.VMEM((units, width), F32),
            pltpu.VMEM((units, width), BF16),
            pltpu.SemaphoreType.DMA((width // chunk + 1, n_exp + 2)),
            pltpu.SemaphoreType.DMA((width // chunk, 3)),
        ],
        compiler_params=params(24),
        cost_estimate=SMALL,
        name="expert_step",
    )(
        *slabs, *in_hbm(grads[0]), *grads[1:], *in_hbm(moment_one, moment_two)
    )


def swap(x, axis, size, mask):
    return lax.ppermute(x, axis, [(i, i ^ mask) for i in range(size)])


def shift(x, size, k):
    return lax.ppermute(x, "exp", [(i, (i + k) % size) for i in range(size)])


def after(x, y):
    return lax.optimization_barrier((x, y))[0]


def body(n_rep, n_exp, activations, kv_grad, errors, right_factor, hidden, out_grad, moment_one, moment_two):
    grads = {0: out_grad, 1: shift(out_grad, n_exp, 1)}
    if n_exp > 2:
        grads[n_exp - 1] = shift(out_grad, n_exp, -1)
    merged, lt = merge(activations, kv_grad, errors, right_factor.T)

    lt = (lt + swap(lt, "rep", n_rep, 1)).astype(BF16)
    slabs = unit_slabs(after(hidden, lt), n_exp)
    bit = 2
    parts = [lt]
    while bit < n_rep:
        while len(parts) > 1:
            parts = [a.astype(F32) + b.astype(F32) for a, b in zip(parts[0::2], parts[1::2])]
        own = parts[0].astype(BF16)
        masks = [bit] if 2 * bit >= n_rep else [bit, 2 * bit, 3 * bit]
        parts = [own] + [swap(own, "rep", n_rep, m) for m in masks]
        bit *= len(parts)
    parts, grads[1] = lax.optimization_barrier((parts, grads[1]))
    lt, gram, keep, send = right_product(parts, merged)

    bits = n_rep.bit_length() - 1
    assert n_rep == 1 << bits and keep.shape[0] >> (bits - 1) >= 8
    for bit in range(1, bits):
        keep, send = halve(bit, keep, swap(send, "rep", n_rep, 1 << (bit - 1)))
    got = swap(send, "rep", n_rep, 1 << (bits - 1))
    got, grads = lax.optimization_barrier((got, grads))

    load = line_load(keep, got, gram)
    loads = [load] + [shift(load, n_exp, k) for k in range(1, n_exp)]
    share = line_sum(loads, gram.shape[0])
    w, basis = inverse_factor(loads, lt)

    left, right = 1, n_exp - 1
    while right - left > 1:
        if left <= n_exp - right:
            grads[left + 1] = shift(after(grads[left], share), n_exp, 1)
            left += 1
        else:
            grads[right - 1] = shift(after(grads[right], share), n_exp, -1)
            right -= 1
    slabs = [slabs[0]] + [shift(after(slabs[k], share), n_exp, k) for k in range(1, n_exp)]

    for bit in range(bits - 1, 0, -1):
        share = double(bit, share, swap(share, "rep", n_rep, 1 << bit))
    new_right, new_error = finish(n_rep, w, share, swap(share, "rep", n_rep, 1), basis, merged)
    first_new, second_new, step = expert_step(
        slabs, [grads[k] for k in range(n_exp)], moment_one, moment_two
    )
    return new_error, new_right.T, first_new, second_new, step


def solution(mesh):
    placed = (
        P("rep", "exp"),
        P("rep", None),
        P("rep", "exp", None),
        P(),
        P("rep", "exp", None),
        P("rep", "exp", None),
        P("rep", "exp", None),
        P("rep", "exp", None),
    )
    return jax.shard_map(
        functools.partial(body, mesh.shape["rep"], mesh.shape["exp"]),
        mesh=mesh,
        in_specs=placed,
        out_specs=(
            P("rep", "exp", None),
            P(),
            P("rep", "exp", None),
            P("rep", "exp", None),
            P("rep", "exp", None),
        ),
        check_vma=False,
    )
```

```python
import functools

import jax
import jax.numpy as jnp
from jax import lax
from jax.experimental import pallas as pl
from jax.experimental.pallas import tpu as pltpu
from jax.sharding import PartitionSpec as P

HIGHEST = lax.Precision.HIGHEST
F32 = jnp.float32
BF16 = jnp.bfloat16
beta_one = 0.9
beta_two = 0.99
correction_one = 1.0 - 0.9**10
correction_two = 1.0 - 0.99**10
epsilon = 1e-08

ROWS_FIRST = (((0,), (0,)), ((), ()))
COLS_LAST = (((1,), (1,)), ((), ()))
TILE_R, TILE_C = 16, 128
HBM = pl.BlockSpec(memory_space=pltpu.HBM)
ANY = pl.BlockSpec(memory_space=pl.ANY)
VMEM = pl.BlockSpec(memory_space=pltpu.VMEM)


def params(mebibytes):
    return pltpu.CompilerParams(vmem_limit_bytes=mebibytes * 1024 * 1024)


def in_hbm(*arrays):
    return [pltpu.with_memory_space_constraint(x, pltpu.HBM) for x in arrays]


SMALL = pl.CostEstimate(flops=1000, bytes_accessed=1000, transcendentals=0)


def split_two(x):
    hi = x.astype(BF16)
    return hi, (x - hi.astype(F32)).astype(BF16)


def left_times(left, right_bf16, dims):
    rows = left.shape[0]
    hi, lo = split_two(left)
    both = jnp.concatenate([hi, lo], axis=0)
    out = lax.dot_general(both, right_bf16, dims, preferred_element_type=F32)
    return out[:rows] + out[rows:]


def merge_kernel(acts_ref, kv_ref, err_ref, vt_ref, merged_ref, lt_ref):
    merged = lax.dot_general(acts_ref[...], kv_ref[...], ROWS_FIRST, preferred_element_type=F32)
    merged = (merged + err_ref[0].astype(F32)).astype(BF16)
    merged_ref[...] = merged
    lt_ref[...] = left_times(vt_ref[...], merged, COLS_LAST)


def merge(acts, kv, err, vt):
    tokens, rows = acts.shape
    cols = kv.shape[1]
    rank = vt.shape[0]
    block = 256
    return pl.pallas_call(
        merge_kernel,
        grid=(rows // block,),
        in_specs=[
            pl.BlockSpec((tokens, block), lambda i: (0, i)),
            pl.BlockSpec((tokens, cols), lambda i: (0, 0)),
            pl.BlockSpec((1, block, cols), lambda i: (0, i, 0)),
            pl.BlockSpec((rank, cols), lambda i: (0, 0)),
        ],
        out_specs=[
            pl.BlockSpec((block, cols), lambda i: (i, 0)),
            pl.BlockSpec((rank, block), lambda i: (0, i)),
        ],
        out_shape=[
            jax.ShapeDtypeStruct((rows, cols), BF16),
            jax.ShapeDtypeStruct((rank, rows), F32),
        ],
        compiler_params=params(24),
        cost_estimate=SMALL,
        name="merge",
    )(*[pltpu.with_memory_space_constraint(x, pltpu.HBM) for x in (acts, kv, err, vt)])


def pack_kernel(hidden_ref, gram_ref, *refs):
    load_refs, all_ref = refs[:-1], refs[-1]
    n_exp, units = all_ref.shape[:2]
    terms = gram_ref.shape[0]
    all_ref[...] = hidden_ref[0].T.reshape(all_ref.shape)
    place = lax.axis_index("exp")
    for k, ref in enumerate(load_refs):
        ref[0:terms] = gram_ref[...]
        ref[terms : terms + units] = all_ref[lax.rem(place + k, n_exp)]


def pack(hidden, gram, n_exp):
    _, tokens, units = hidden.shape
    slab = (units // n_exp, tokens)
    load = (gram.shape[0] + slab[0], tokens)
    return pl.pallas_call(
        pack_kernel,
        out_shape=[jax.ShapeDtypeStruct(load, BF16)] * n_exp,
        scratch_shapes=[pltpu.VMEM((n_exp,) + slab, BF16)],
        compiler_params=params(8),
        cost_estimate=SMALL,
        name="pack",
    )(hidden, gram)


def right_kernel(n_parts, *refs):
    part_refs, merged_ref = refs[:n_parts], refs[n_parts]
    lt_ref, gram_ref, chunk_ref = refs[n_parts + 1 :]
    parts = [ref[...].astype(F32) for ref in part_refs]
    while len(parts) > 1:
        parts = [a + b for a, b in zip(parts[0::2], parts[1::2])]
    lt = parts[0]
    rank = lt.shape[0]
    lt_ref[...] = lt
    product = left_times(lt, merged_ref[...], (((1,), (0,)), ((), ()))).astype(BF16)
    across = product.shape[1] // TILE_C
    for a in range(rank // TILE_R):
        for b in range(across):
            chunk_ref[a * across + b] = product[
                a * TILE_R : (a + 1) * TILE_R, b * TILE_C : (b + 1) * TILE_C
            ]
    gram = lax.dot_general(lt, lt, COLS_LAST, precision=HIGHEST, preferred_element_type=F32)
    half = rank // 2
    packed = jnp.concatenate([gram[:half], gram[half:]], axis=1)
    high = packed.astype(BF16)
    rest = packed - high.astype(F32)
    middle = rest.astype(BF16)
    low = (rest - middle.astype(F32)).astype(BF16)
    gram_ref[0:half] = high
    gram_ref[half : 2 * half] = middle
    gram_ref[2 * half : 3 * half] = low


def right_product(parts, merged):
    rank, rows = parts[0].shape
    cols = merged.shape[1]
    chunks = rank * cols // (TILE_R * TILE_C)
    return pl.pallas_call(
        functools.partial(right_kernel, len(parts)),
        out_shape=[
            jax.ShapeDtypeStruct((rank, rows), F32),
            jax.ShapeDtypeStruct((3 * (rank // 2), 2 * rank), BF16),
            jax.ShapeDtypeStruct((chunks, TILE_R, TILE_C), BF16),
        ],
        compiler_params=params(16),
        cost_estimate=SMALL,
        name="right_product",
    )(*parts, merged)


def fold_kernel(share_ref, out_ref):
    total = share_ref[0].astype(F32)
    for i in range(1, share_ref.shape[0]):
        total = total + share_ref[i].astype(F32)
    total = total.astype(BF16)
    for i in range(out_ref.shape[0]):
        out_ref[i] = total


def fold(shares):
    return pl.pallas_call(
        fold_kernel,
        out_shape=jax.ShapeDtypeStruct(shares.shape, BF16),
        compiler_params=params(4),
        cost_estimate=SMALL,
        name="fold",
    )(shares)


def inverse_kernel(n_exp, *refs):
    load_hbms, lt_hbm = refs[:n_exp], refs[n_exp]
    w_ref, basis_ref, terms_ref, lt_ref, wide_ref, sems = refs[n_exp + 1 :]
    rank = lt_ref.shape[0]
    half = rank // 2
    copies = [
        pltpu.make_async_copy(load_hbms[k].at[0 : 3 * half], terms_ref.at[k], sems.at[k])
        for k in range(n_exp)
    ]
    lt_copy = pltpu.make_async_copy(lt_hbm, lt_ref, sems.at[n_exp])
    for copy in copies:
        copy.start()
    lt_copy.start()
    for copy in copies:
        copy.wait()
    place = lax.axis_index("exp")
    packed = None
    for j in range(n_exp):
        terms = terms_ref[lax.rem(place + n_exp - j, n_exp)].astype(F32)
        part = terms[:half] + terms[half : 2 * half] + terms[2 * half :]
        packed = part if packed is None else packed + part
    gram = jnp.concatenate([packed[:, :rank], packed[:, rank:]], axis=0)
    row = lax.broadcasted_iota(jnp.int32, (rank, rank), 0)
    col = lax.broadcasted_iota(jnp.int32, (rank, rank), 1)
    a = jnp.concatenate([gram, jnp.where(row == col, 1.0, 0.0).astype(F32)], axis=1)
    group = 4
    for k in range(0, rank, group):
        cols = [jnp.broadcast_to(a[:, k + j : k + j + 1], a.shape) for j in range(group)]
        rows = [a[k + j : k + j + 1, :] for j in range(group)]
        for j in range(group):
            pivot = cols[j][k + j : k + j + 1, :]
            wide_ref[k + j : k + j + 1, :] = rows[j] * lax.rsqrt(pivot)
            factor = cols[j] * (1.0 / pivot)
            for m in range(j + 1, group):
                cols[m] = cols[m] - factor * cols[m][k + j : k + j + 1, :]
                rows[m] = rows[m] - factor[k + m : k + m + 1, :] * rows[j]
            a = a - factor * rows[j]
    w = wide_ref[:, rank:]
    w_ref[...] = w
    lt_copy.wait()
    basis = jnp.dot(w, lt_ref[...], precision=HIGHEST, preferred_element_type=F32)
    basis_ref[...] = basis.T.astype(BF16)


def inverse_factor(loads, lt):
    rank, rows = lt.shape
    n_exp = len(loads)
    return pl.pallas_call(
        functools.partial(inverse_kernel, n_exp),
        in_specs=[ANY] * (n_exp + 1),
        out_shape=[
            jax.ShapeDtypeStruct((rank, rank), F32),
            jax.ShapeDtypeStruct((rows, rank), BF16),
        ],
        scratch_shapes=[
            pltpu.VMEM((n_exp, 3 * (rank // 2), 2 * rank), BF16),
            pltpu.VMEM((rank, rows), F32),
            pltpu.VMEM((rank, 2 * rank), F32),
            pltpu.SemaphoreType.DMA((n_exp + 1,)),
        ],
        compiler_params=params(8),
        cost_estimate=pl.CostEstimate(flops=4_000_000_000, bytes_accessed=1000, transcendentals=0),
        name="inverse_factor",
    )(*loads, lt)


def finish_kernel(
    replicas, w_any, chunk_ref, basis_any, merged_ref, right_hbm, err_hbm, w_ref, basis_ref, right_ref, err_ref, sems
):
    rank, cols = right_ref.shape
    rows, block = err_ref.shape[0], 128
    w_copy = pltpu.make_async_copy(w_any, w_ref, sems.at[rows // block + 1])
    w_copy.start()
    basis_copy = pltpu.make_async_copy(basis_any, basis_ref, sems.at[rows // block + 2])
    basis_copy.start()
    across = cols // TILE_C
    pieces = []
    for a in range(rank // TILE_R):
        pieces.append(jnp.concatenate([chunk_ref[a * across + b] for b in range(across)], axis=1))
    product = jnp.concatenate(pieces, axis=0)
    w_copy.wait()
    new_right = left_times(w_ref[...], product, (((1,), (0,)), ((), ()))) * (1.0 / replicas)
    right_ref[...] = new_right
    copies = [pltpu.make_async_copy(right_ref, right_hbm, sems.at[0])]
    copies[0].start()
    rounded = new_right.astype(BF16)
    basis_copy.wait()
    for i in range(rows // block):
        here = slice(i * block, (i + 1) * block)
        approx = jnp.dot(basis_ref[here, :], rounded, preferred_element_type=F32)
        err_ref[here, :] = (merged_ref[here, :].astype(F32) - approx).astype(BF16)
        copies.append(
            pltpu.make_async_copy(err_ref.at[here, :], err_hbm.at[0, here, :], sems.at[i + 1])
        )
        copies[-1].start()
    for copy in copies:
        copy.wait()


def finish(replicas, w, chunks, basis, merged):
    rows, rank = basis.shape
    cols = merged.shape[1]
    return pl.pallas_call(
        functools.partial(finish_kernel, replicas),
        in_specs=[ANY, VMEM, ANY, VMEM],
        out_specs=[HBM] * 2,
        out_shape=[
            jax.ShapeDtypeStruct((rank, cols), F32),
            jax.ShapeDtypeStruct((1, rows, cols), BF16),
        ],
        scratch_shapes=[
            pltpu.VMEM((rank, rank), F32),
            pltpu.VMEM((rows, rank), BF16),
            pltpu.VMEM((rank, cols), F32),
            pltpu.VMEM((rows, cols), BF16),
            pltpu.SemaphoreType.DMA((rows // 128 + 3,)),
        ],
        compiler_params=params(16),
        cost_estimate=SMALL,
        name="finish",
    )(w, chunks, basis, merged)


def expert_kernel(n_exp, chunk, *refs):
    load_hbms, grad_hbms = refs[:n_exp], refs[n_exp : 2 * n_exp]
    one_hbm, two_hbm, first_hbm, second_hbm, step_hbm = refs[2 * n_exp : 2 * n_exp + 5]
    hid, rows, one, two, first, second, step, in_sems, out_sems = refs[2 * n_exp + 5 :]
    units, width = one.shape
    tokens = grad_hbms[0].shape[1]
    count = width // chunk
    terms = load_hbms[0].shape[0] - units

    slabs = [
        pltpu.make_async_copy(load_hbms[k].at[terms : terms + units], hid.at[k], in_sems.at[count, k])
        for k in range(n_exp)
    ]

    def loads(c):
        here = slice(c * chunk, (c + 1) * chunk)
        pairs = [
            (grad_hbms[k].at[0, :, here], rows.at[k * tokens : (k + 1) * tokens, here])
            for k in range(n_exp)
        ]
        pairs += [(one_hbm.at[0, :, here], one.at[:, here]), (two_hbm.at[0, :, here], two.at[:, here])]
        return [pltpu.make_async_copy(a, b, in_sems.at[c, i]) for i, (a, b) in enumerate(pairs)]

    def stores(c):
        here = slice(c * chunk, (c + 1) * chunk)
        pairs = [(first, first_hbm), (second, second_hbm), (step, step_hbm)]
        return [
            pltpu.make_async_copy(a.at[:, here], b.at[0, :, here], out_sems.at[c, i])
            for i, (a, b) in enumerate(pairs)
        ]

    for copy in slabs:
        copy.start()
    for c in range(count):
        for copy in loads(c):
            copy.start()
    for copy in slabs:
        copy.wait()
    left = jnp.concatenate([hid[k] for k in range(n_exp)], axis=1)
    for c in range(count):
        here = slice(c * chunk, (c + 1) * chunk)
        for copy in loads(c):
            copy.wait()
        grad = jnp.dot(left, rows[:, here], preferred_element_type=F32)
        first_new = beta_one * one[:, here] + (1.0 - beta_one) * grad
        second_new = beta_two * two[:, here] + (1.0 - beta_two) * grad * grad
        first[:, here] = first_new
        second[:, here] = second_new
        scaled = second_new * (1.0 / correction_two)
        bottom = scaled * lax.rsqrt(scaled) + epsilon
        step[:, here] = (
            first_new * (1.0 / correction_one) * pl.reciprocal(bottom, approx=True)
        ).astype(BF16)
        for copy in stores(c):
            copy.start()
    for c in range(count):
        for copy in stores(c):
            copy.wait()


def expert_step(slabs, grads, moment_one, moment_two):
    _, units, width = moment_one.shape
    chunk = 512
    n_exp = len(grads)
    tokens = grads[0].shape[1]
    return pl.pallas_call(
        functools.partial(expert_kernel, n_exp, chunk),
        in_specs=[ANY] * n_exp + [HBM] + [ANY] * (n_exp - 1) + [HBM] * 2,
        out_specs=[HBM] * 3,
        out_shape=[
            jax.ShapeDtypeStruct((1, units, width), F32),
            jax.ShapeDtypeStruct((1, units, width), F32),
            jax.ShapeDtypeStruct((1, units, width), BF16),
        ],
        scratch_shapes=[
            pltpu.VMEM((n_exp, units, tokens), BF16),
            pltpu.VMEM((n_exp * tokens, width), BF16),
            pltpu.VMEM((units, width), F32),
            pltpu.VMEM((units, width), F32),
            pltpu.VMEM((units, width), F32),
            pltpu.VMEM((units, width), F32),
            pltpu.VMEM((units, width), BF16),
            pltpu.SemaphoreType.DMA((width // chunk + 1, n_exp + 2)),
            pltpu.SemaphoreType.DMA((width // chunk, 3)),
        ],
        compiler_params=params(24),
        cost_estimate=SMALL,
        name="expert_step",
    )(
        *slabs, *in_hbm(grads[0]), *grads[1:], *in_hbm(moment_one, moment_two)
    )


def swap(x, axis, size, mask):
    return lax.ppermute(x, axis, [(i, i ^ mask) for i in range(size)])


def shift(x, size, k):
    return lax.ppermute(x, "exp", [(i, (i + k) % size) for i in range(size)])


def after(x, y):
    return lax.optimization_barrier((x, y))[0]


def body(n_rep, n_exp, activations, kv_grad, errors, right_factor, hidden, out_grad, moment_one, moment_two):
    grads = {0: out_grad, 1: shift(out_grad, n_exp, 1)}
    if n_exp > 2:
        grads[n_exp - 1] = shift(out_grad, n_exp, -1)
    merged, lt = merge(activations, kv_grad, errors, right_factor.T)

    lt = (lt + swap(lt, "rep", n_rep, 1)).astype(BF16)
    bit = 2
    parts = [lt]
    while bit < n_rep:
        while len(parts) > 1:
            parts = [a.astype(F32) + b.astype(F32) for a, b in zip(parts[0::2], parts[1::2])]
        own = parts[0].astype(BF16)
        masks = [bit] if 2 * bit >= n_rep else [bit, 2 * bit, 3 * bit]
        parts = [own] + [swap(own, "rep", n_rep, m) for m in masks]
        bit *= len(parts)
    lt, gram, chunks = right_product(parts, merged)

    loads = pack(hidden, gram, n_exp)
    loads = [loads[0]] + [shift(loads[k], n_exp, k) for k in range(1, n_exp)]

    if chunks.shape[0] == n_rep * n_exp:
        both = ("rep", "exp")
        shares = lax.all_to_all(chunks, both, 0, 0, tiled=True)
        shares, grads = lax.optimization_barrier((shares, grads))
        share = fold(shares)
        chunks = lax.all_to_all(share, both, 0, 0, tiled=True)
    else:
        share = chunks
        chunks = lax.psum(chunks.astype(F32), ("rep", "exp")).astype(BF16)
    w, basis = inverse_factor(loads, lt)

    left, right = 1, n_exp - 1
    while right - left > 1:
        if left <= n_exp - right:
            grads[left + 1] = shift(after(grads[left], share), n_exp, 1)
            left += 1
        else:
            grads[right - 1] = shift(after(grads[right], share), n_exp, -1)
            right -= 1

    new_right, new_error = finish(n_rep, w, chunks, basis, merged)
    first_new, second_new, step = expert_step(
        loads, [grads[k] for k in range(n_exp)], moment_one, moment_two
    )
    return new_error, new_right.T, first_new, second_new, step


def solution(mesh):
    placed = (
        P("rep", "exp"),
        P("rep", None),
        P("rep", "exp", None),
        P(),
        P("rep", "exp", None),
        P("rep", "exp", None),
        P("rep", "exp", None),
        P("rep", "exp", None),
    )
    return jax.shard_map(
        functools.partial(body, mesh.shape["rep"], mesh.shape["exp"]),
        mesh=mesh,
        in_specs=placed,
        out_specs=(
            P("rep", "exp", None),
            P(),
            P("rep", "exp", None),
            P("rep", "exp", None),
            P("rep", "exp", None),
        ),
        check_vma=False,
    )
```

```python
import functools

import jax
import jax.numpy as jnp
from jax import lax
from jax.experimental import pallas as pl
from jax.experimental.pallas import tpu as pltpu
from jax.sharding import PartitionSpec as P

HIGHEST = lax.Precision.HIGHEST
F32 = jnp.float32
BF16 = jnp.bfloat16
beta_one = 0.9
beta_two = 0.99
correction_one = 1.0 - 0.9**10
correction_two = 1.0 - 0.99**10
epsilon = 1e-08

ROWS_FIRST = (((0,), (0,)), ((), ()))
COLS_LAST = (((1,), (1,)), ((), ()))
TILE_R, TILE_C = 16, 128
HBM = pl.BlockSpec(memory_space=pltpu.HBM)
ANY = pl.BlockSpec(memory_space=pl.ANY)
VMEM = pl.BlockSpec(memory_space=pltpu.VMEM)


def params(mebibytes):
    return pltpu.CompilerParams(vmem_limit_bytes=mebibytes * 1024 * 1024)


def in_hbm(*arrays):
    return [pltpu.with_memory_space_constraint(x, pltpu.HBM) for x in arrays]


SMALL = pl.CostEstimate(flops=1000, bytes_accessed=1000, transcendentals=0)


def split_two(x):
    hi = x.astype(BF16)
    return hi, (x - hi.astype(F32)).astype(BF16)


def left_times(left, right_bf16, dims):
    rows = left.shape[0]
    hi, lo = split_two(left)
    both = jnp.concatenate([hi, lo], axis=0)
    out = lax.dot_general(both, right_bf16, dims, preferred_element_type=F32)
    return out[:rows] + out[rows:]


def merge_kernel(acts_ref, kv_ref, err_ref, vt_ref, merged_ref, lt_ref):
    merged = lax.dot_general(acts_ref[...], kv_ref[...], ROWS_FIRST, preferred_element_type=F32)
    merged = (merged + err_ref[0].astype(F32)).astype(BF16)
    merged_ref[...] = merged
    lt_ref[...] = left_times(vt_ref[...], merged, COLS_LAST)


def merge(acts, kv, err, vt):
    tokens, rows = acts.shape
    cols = kv.shape[1]
    rank = vt.shape[0]
    block = 256
    return pl.pallas_call(
        merge_kernel,
        grid=(rows // block,),
        in_specs=[
            pl.BlockSpec((tokens, block), lambda i: (0, i)),
            pl.BlockSpec((tokens, cols), lambda i: (0, 0)),
            pl.BlockSpec((1, block, cols), lambda i: (0, i, 0)),
            pl.BlockSpec((rank, cols), lambda i: (0, 0)),
        ],
        out_specs=[
            pl.BlockSpec((block, cols), lambda i: (i, 0)),
            pl.BlockSpec((rank, block), lambda i: (0, i)),
        ],
        out_shape=[
            jax.ShapeDtypeStruct((rows, cols), BF16),
            jax.ShapeDtypeStruct((rank, rows), F32),
        ],
        compiler_params=params(24),
        cost_estimate=SMALL,
        name="merge",
    )(*[pltpu.with_memory_space_constraint(x, pltpu.HBM) for x in (acts, kv, err, vt)])


def slab_kernel(hidden_ref, own_ref, *refs):
    send_refs, all_ref = refs[:-1], refs[-1]
    n_exp = all_ref.shape[0]
    all_ref[...] = hidden_ref[0].T.reshape(all_ref.shape)
    place = lax.axis_index("exp")
    for k, ref in enumerate((own_ref,) + tuple(send_refs)):
        ref[...] = all_ref[lax.rem(place + k, n_exp)]


def unit_slabs(hidden, n_exp):
    _, tokens, units = hidden.shape
    slab = (units // n_exp, tokens)
    return pl.pallas_call(
        slab_kernel,
        out_shape=[jax.ShapeDtypeStruct(slab, BF16)] * n_exp,
        scratch_shapes=[pltpu.VMEM((n_exp,) + slab, BF16)],
        compiler_params=params(8),
        cost_estimate=SMALL,
        name="unit_slabs",
    )(hidden)


def as_terms(x, hold=lambda rounded: rounded):
    high = hold(x.astype(BF16)).astype(F32)
    rest = x - high
    middle = hold(rest.astype(BF16)).astype(F32)
    low = rest - middle
    return jnp.concatenate([high, middle], axis=-1), jnp.concatenate([low, jnp.zeros_like(low)], axis=-1)


def from_terms(first, second):
    rank = first.shape[-1] // 2
    return first[..., :rank] + first[..., rank:] + second[..., :rank]


def right_kernel(n_parts, *refs):
    part_refs, merged_ref = refs[:n_parts], refs[n_parts]
    lt_ref, chunk_ref = refs[n_parts + 1 :]
    parts = [ref[...].astype(F32) for ref in part_refs]
    while len(parts) > 1:
        parts = [a + b for a, b in zip(parts[0::2], parts[1::2])]
    lt = parts[0]
    rank = lt.shape[0]
    lt_ref[...] = lt.astype(BF16)
    product = left_times(lt, merged_ref[...], (((1,), (0,)), ((), ()))).astype(BF16)
    across = product.shape[1] // TILE_C
    for a in range(rank // TILE_R):
        for b in range(across):
            chunk_ref[a * across + b, 0:TILE_R] = product[
                a * TILE_R : (a + 1) * TILE_R, b * TILE_C : (b + 1) * TILE_C
            ]
    first, second = as_terms(
        lax.dot_general(lt, lt, COLS_LAST, precision=HIGHEST, preferred_element_type=F32)
    )
    chunks, pieces = chunk_ref.shape[0], rank // 8
    for i in range(pieces):
        here = slice(8 * i, 8 * i + 8)
        piece = jnp.concatenate([first[here], second[here]], axis=0).astype(BF16)
        for c in range(i * chunks // pieces, (i + 1) * chunks // pieces):
            chunk_ref[c, TILE_R:] = piece


def right_product(parts, merged):
    rank, rows = parts[0].shape
    cols = merged.shape[1]
    assert 2 * rank == TILE_C
    chunks = rank * cols // (TILE_R * TILE_C)
    return pl.pallas_call(
        functools.partial(right_kernel, len(parts)),
        out_shape=[
            jax.ShapeDtypeStruct((rank, rows), BF16),
            jax.ShapeDtypeStruct((chunks, 2 * TILE_R, TILE_C), BF16),
        ],
        compiler_params=params(16),
        cost_estimate=SMALL,
        name="right_product",
    )(*parts, merged)


def fold_kernel(n_exp, share_ref, out_ref):
    total = share_ref[0, 0:TILE_R].astype(F32)
    for i in range(1, share_ref.shape[0]):
        total = total + share_ref[i, 0:TILE_R].astype(F32)
    total = total.astype(BF16)
    gram = None
    for j in range(n_exp):
        terms = share_ref[j, TILE_R:].astype(F32)
        part = from_terms(terms[:8], terms[8:])
        gram = part if gram is None else gram + part
    piece = jnp.concatenate(as_terms(gram), axis=0).astype(BF16)
    for i in range(out_ref.shape[0]):
        out_ref[i, 0:TILE_R] = total
        out_ref[i, TILE_R:] = piece


def fold(shares, n_exp):
    return pl.pallas_call(
        functools.partial(fold_kernel, n_exp),
        out_shape=jax.ShapeDtypeStruct(shares.shape, BF16),
        compiler_params=params(4),
        cost_estimate=SMALL,
        name="fold",
    )(shares)


def fold_any(chunks):
    wide = chunks.astype(F32)
    total = lax.psum(wide[:, :TILE_R], ("rep", "exp"))
    terms = lax.psum(wide[:, TILE_R:], "exp")
    pieces = as_terms(from_terms(terms[:, :8], terms[:, 8:]), lax.optimization_barrier)
    return jnp.concatenate([total, *pieces], axis=1).astype(BF16)


def inverse_of_factor(gram, wide_ref):
    rank = gram.shape[0]
    row = lax.broadcasted_iota(jnp.int32, (rank, rank), 0)
    col = lax.broadcasted_iota(jnp.int32, (rank, rank), 1)
    a = jnp.concatenate([gram, jnp.where(row == col, 1.0, 0.0).astype(F32)], axis=1)
    group = 4
    for k in range(0, rank, group):
        cols = [jnp.broadcast_to(a[:, k + j : k + j + 1], a.shape) for j in range(group)]
        rows = [a[k + j : k + j + 1, :] for j in range(group)]
        for j in range(group):
            pivot = cols[j][k + j : k + j + 1, :]
            wide_ref[k + j : k + j + 1, :] = rows[j] * lax.rsqrt(pivot)
            factor = cols[j] * (1.0 / pivot)
            for m in range(j + 1, group):
                cols[m] = cols[m] - factor * cols[m][k + j : k + j + 1, :]
                rows[m] = rows[m] - factor[k + m : k + m + 1, :] * rows[j]
            a = a - factor * rows[j]
    return wide_ref[:, rank:]


def finish_kernel(
    replicas, chunk_ref, lt_any, merged_ref, right_hbm, err_hbm, lt_ref, wide_ref, right_ref, err_ref, sems
):
    rank, cols = right_ref.shape
    rows, block = err_ref.shape[0], 128
    lt_copy = pltpu.make_async_copy(lt_any, lt_ref, sems.at[rows // block + 1])
    lt_copy.start()
    chunks, count = chunk_ref.shape[0], rank // 8
    gram = []
    for i in range(count):
        terms = chunk_ref[i * chunks // count, TILE_R:].astype(F32)
        gram.append(from_terms(terms[:8], terms[8:]))
    w = inverse_of_factor(jnp.concatenate(gram, axis=0), wide_ref)
    across = cols // TILE_C
    pieces = []
    for a in range(rank // TILE_R):
        pieces.append(
            jnp.concatenate([chunk_ref[a * across + b, 0:TILE_R] for b in range(across)], axis=1)
        )
    product = jnp.concatenate(pieces, axis=0)
    inner = (((1,), (0,)), ((), ()))
    new_right = left_times(w, product, inner) * (1.0 / replicas)
    right_ref[...] = new_right
    copies = [pltpu.make_async_copy(right_ref, right_hbm, sems.at[0])]
    copies[0].start()
    rounded = new_right.astype(BF16)
    lt_copy.wait()
    basis = left_times(w, lt_ref[...], inner).T.astype(BF16)
    for i in range(rows // block):
        here = slice(i * block, (i + 1) * block)
        approx = jnp.dot(basis[here, :], rounded, preferred_element_type=F32)
        err_ref[here, :] = (merged_ref[here, :].astype(F32) - approx).astype(BF16)
        copies.append(
            pltpu.make_async_copy(err_ref.at[here, :], err_hbm.at[0, here, :], sems.at[i + 1])
        )
        copies[-1].start()
    for copy in copies:
        copy.wait()


def finish(replicas, chunks, lt, merged):
    rank, rows = lt.shape
    cols = merged.shape[1]
    return pl.pallas_call(
        functools.partial(finish_kernel, replicas),
        in_specs=[VMEM, ANY, VMEM],
        out_specs=[HBM] * 2,
        out_shape=[
            jax.ShapeDtypeStruct((rank, cols), F32),
            jax.ShapeDtypeStruct((1, rows, cols), BF16),
        ],
        scratch_shapes=[
            pltpu.VMEM((rank, rows), BF16),
            pltpu.VMEM((rank, 2 * rank), F32),
            pltpu.VMEM((rank, cols), F32),
            pltpu.VMEM((rows, cols), BF16),
            pltpu.SemaphoreType.DMA((rows // 128 + 2,)),
        ],
        compiler_params=params(16),
        cost_estimate=SMALL,
        name="finish",
    )(chunks, lt, merged)


def expert_kernel(n_exp, chunk, *refs):
    load_hbms, grad_hbms = refs[:n_exp], refs[n_exp : 2 * n_exp]
    one_hbm, two_hbm, first_hbm, second_hbm, step_hbm = refs[2 * n_exp : 2 * n_exp + 5]
    hid, rows, one, two, first, second, step, in_sems, out_sems = refs[2 * n_exp + 5 :]
    units, width = one.shape
    tokens = grad_hbms[0].shape[1]
    count = width // chunk

    slabs = [
        pltpu.make_async_copy(load_hbms[k], hid.at[k], in_sems.at[count, k])
        for k in range(n_exp)
    ]

    def loads(c):
        here = slice(c * chunk, (c + 1) * chunk)
        pairs = [
            (grad_hbms[k].at[0, :, here], rows.at[k * tokens : (k + 1) * tokens, here])
            for k in range(n_exp)
        ]
        pairs += [(one_hbm.at[0, :, here], one.at[:, here]), (two_hbm.at[0, :, here], two.at[:, here])]
        return [pltpu.make_async_copy(a, b, in_sems.at[c, i]) for i, (a, b) in enumerate(pairs)]

    def stores(c):
        here = slice(c * chunk, (c + 1) * chunk)
        pairs = [(first, first_hbm), (second, second_hbm), (step, step_hbm)]
        return [
            pltpu.make_async_copy(a.at[:, here], b.at[0, :, here], out_sems.at[c, i])
            for i, (a, b) in enumerate(pairs)
        ]

    for copy in slabs:
        copy.start()
    for c in range(count):
        for copy in loads(c):
            copy.start()
    for copy in slabs:
        copy.wait()
    left = jnp.concatenate([hid[k] for k in range(n_exp)], axis=1)
    for c in range(count):
        here = slice(c * chunk, (c + 1) * chunk)
        for copy in loads(c):
            copy.wait()
        grad = jnp.dot(left, rows[:, here], preferred_element_type=F32)
        first_new = beta_one * one[:, here] + (1.0 - beta_one) * grad
        second_new = beta_two * two[:, here] + (1.0 - beta_two) * grad * grad
        first[:, here] = first_new
        second[:, here] = second_new
        scaled = second_new * (1.0 / correction_two)
        bottom = scaled * lax.rsqrt(scaled) + epsilon
        step[:, here] = (
            first_new * (1.0 / correction_one) * pl.reciprocal(bottom, approx=True)
        ).astype(BF16)
        for copy in stores(c):
            copy.start()
    for c in range(count):
        for copy in stores(c):
            copy.wait()


def expert_step(slabs, grads, moment_one, moment_two):
    _, units, width = moment_one.shape
    chunk = 512
    n_exp = len(grads)
    tokens = grads[0].shape[1]
    return pl.pallas_call(
        functools.partial(expert_kernel, n_exp, chunk),
        in_specs=[ANY] * n_exp + [HBM] + [ANY] * (n_exp - 1) + [HBM] * 2,
        out_specs=[HBM] * 3,
        out_shape=[
            jax.ShapeDtypeStruct((1, units, width), F32),
            jax.ShapeDtypeStruct((1, units, width), F32),
            jax.ShapeDtypeStruct((1, units, width), BF16),
        ],
        scratch_shapes=[
            pltpu.VMEM((n_exp, units, tokens), BF16),
            pltpu.VMEM((n_exp * tokens, width), BF16),
            pltpu.VMEM((units, width), F32),
            pltpu.VMEM((units, width), F32),
            pltpu.VMEM((units, width), F32),
            pltpu.VMEM((units, width), F32),
            pltpu.VMEM((units, width), BF16),
            pltpu.SemaphoreType.DMA((width // chunk + 1, n_exp + 2)),
            pltpu.SemaphoreType.DMA((width // chunk, 3)),
        ],
        compiler_params=params(24),
        cost_estimate=SMALL,
        name="expert_step",
    )(
        *slabs, *in_hbm(grads[0]), *grads[1:], *in_hbm(moment_one, moment_two)
    )


def swap(x, axis, size, mask):
    return lax.ppermute(x, axis, [(i, i ^ mask) for i in range(size)])


def shift(x, size, k):
    return lax.ppermute(x, "exp", [(i, (i + k) % size) for i in range(size)])


def after(x, y):
    return lax.optimization_barrier((x, y))[0]


def body(n_rep, n_exp, activations, kv_grad, errors, right_factor, hidden, out_grad, moment_one, moment_two):
    grads = {0: out_grad, 1: shift(out_grad, n_exp, 1)}
    if n_exp > 2:
        grads[n_exp - 1] = shift(out_grad, n_exp, -1)
    merged, lt = merge(activations, kv_grad, errors, right_factor.T)

    lt = (lt + swap(lt, "rep", n_rep, 1)).astype(BF16)
    slabs = unit_slabs(after(hidden, lt), n_exp)
    bit = 2
    parts = [lt]
    while bit < n_rep:
        while len(parts) > 1:
            parts = [a.astype(F32) + b.astype(F32) for a, b in zip(parts[0::2], parts[1::2])]
        own = parts[0].astype(BF16)
        masks = [bit] if 2 * bit >= n_rep else [bit, 2 * bit, 3 * bit]
        parts = [own] + [swap(own, "rep", n_rep, m) for m in masks]
        bit *= len(parts)
    lt, chunks = right_product(parts, merged)

    if chunks.shape[0] == n_rep * n_exp and 8 * n_rep == lt.shape[0]:
        both = ("rep", "exp")
        shares = lax.all_to_all(chunks, both, 0, 0, tiled=True)
        shares, grads = lax.optimization_barrier((shares, grads))
        share = fold(shares, n_exp)
        chunks = lax.all_to_all(share, both, 0, 0, tiled=True)
    else:
        share = chunks
        chunks = fold_any(chunks)

    slabs = [slabs[0]] + [shift(after(slabs[k], share), n_exp, k) for k in range(1, n_exp)]
    left, right = 1, n_exp - 1
    while right - left > 1:
        if left <= n_exp - right:
            grads[left + 1] = shift(after(grads[left], share), n_exp, 1)
            left += 1
        else:
            grads[right - 1] = shift(after(grads[right], share), n_exp, -1)
            right -= 1

    new_right, new_error = finish(n_rep, chunks, lt, merged)
    first_new, second_new, step = expert_step(
        slabs, [grads[k] for k in range(n_exp)], moment_one, moment_two
    )
    return new_error, new_right.T, first_new, second_new, step


def solution(mesh):
    placed = (
        P("rep", "exp"),
        P("rep", None),
        P("rep", "exp", None),
        P(),
        P("rep", "exp", None),
        P("rep", "exp", None),
        P("rep", "exp", None),
        P("rep", "exp", None),
    )
    return jax.shard_map(
        functools.partial(body, mesh.shape["rep"], mesh.shape["exp"]),
        mesh=mesh,
        in_specs=placed,
        out_specs=(
            P("rep", "exp", None),
            P(),
            P("rep", "exp", None),
            P("rep", "exp", None),
            P("rep", "exp", None),
        ),
        check_vma=False,
    )
```

```python
import functools

import jax
import jax.numpy as jnp
from jax import lax
from jax.experimental import pallas as pl
from jax.experimental.pallas import tpu as pltpu
from jax.sharding import PartitionSpec as P

HIGHEST = lax.Precision.HIGHEST
F32 = jnp.float32
BF16 = jnp.bfloat16
beta_one = 0.9
beta_two = 0.99
correction_one = 1.0 - 0.9**10
correction_two = 1.0 - 0.99**10
epsilon = 1e-08

ROWS_FIRST = (((0,), (0,)), ((), ()))
COLS_LAST = (((1,), (1,)), ((), ()))
TILE_R, TILE_C = 16, 128
HBM = pl.BlockSpec(memory_space=pltpu.HBM)
ANY = pl.BlockSpec(memory_space=pl.ANY)
VMEM = pl.BlockSpec(memory_space=pltpu.VMEM)


def params(mebibytes):
    return pltpu.CompilerParams(vmem_limit_bytes=mebibytes * 1024 * 1024)


def in_hbm(*arrays):
    return [pltpu.with_memory_space_constraint(x, pltpu.HBM) for x in arrays]


SMALL = pl.CostEstimate(flops=1000, bytes_accessed=1000, transcendentals=0)


def split_two(x):
    hi = x.astype(BF16)
    return hi, (x - hi.astype(F32)).astype(BF16)


def left_times(left, right_bf16, dims):
    rows = left.shape[0]
    hi, lo = split_two(left)
    both = jnp.concatenate([hi, lo], axis=0)
    out = lax.dot_general(both, right_bf16, dims, preferred_element_type=F32)
    return out[:rows] + out[rows:]


def merge_kernel(acts_ref, kv_ref, err_ref, vt_ref, merged_ref, lt_ref):
    merged = lax.dot_general(acts_ref[...], kv_ref[...], ROWS_FIRST, preferred_element_type=F32)
    merged = (merged + err_ref[0].astype(F32)).astype(BF16)
    merged_ref[...] = merged
    lt_ref[...] = left_times(vt_ref[...], merged, COLS_LAST)


def merge(acts, kv, err, vt):
    tokens, rows = acts.shape
    cols = kv.shape[1]
    rank = vt.shape[0]
    block = 256
    return pl.pallas_call(
        merge_kernel,
        grid=(rows // block,),
        in_specs=[
            pl.BlockSpec((tokens, block), lambda i: (0, i)),
            pl.BlockSpec((tokens, cols), lambda i: (0, 0)),
            pl.BlockSpec((1, block, cols), lambda i: (0, i, 0)),
            pl.BlockSpec((rank, cols), lambda i: (0, 0)),
        ],
        out_specs=[
            pl.BlockSpec((block, cols), lambda i: (i, 0)),
            pl.BlockSpec((rank, block), lambda i: (0, i)),
        ],
        out_shape=[
            jax.ShapeDtypeStruct((rows, cols), BF16),
            jax.ShapeDtypeStruct((rank, rows), F32),
        ],
        compiler_params=params(24),
        cost_estimate=pl.CostEstimate(flops=4_000_000_000, bytes_accessed=8_000_000, transcendentals=0),
        name="merge",
    )(*[pltpu.with_memory_space_constraint(x, pltpu.HBM) for x in (acts, kv, err, vt)])


def slab_kernel(hidden_ref, own_ref, *refs):
    send_refs, all_ref = refs[:-1], refs[-1]
    n_exp = all_ref.shape[0]
    all_ref[...] = hidden_ref[0].T.reshape(all_ref.shape)
    place = lax.axis_index("exp")
    for k, ref in enumerate((own_ref,) + tuple(send_refs)):
        ref[...] = all_ref[lax.rem(place + k, n_exp)]


def unit_slabs(hidden, n_exp):
    _, tokens, units = hidden.shape
    slab = (units // n_exp, tokens)
    return pl.pallas_call(
        slab_kernel,
        out_shape=[jax.ShapeDtypeStruct(slab, BF16)] * n_exp,
        scratch_shapes=[pltpu.VMEM((n_exp,) + slab, BF16)],
        compiler_params=params(8),
        cost_estimate=SMALL,
        name="unit_slabs",
    )(hidden)


def as_terms(x, hold=lambda rounded: rounded):
    high = hold(x.astype(BF16)).astype(F32)
    rest = x - high
    middle = hold(rest.astype(BF16)).astype(F32)
    low = rest - middle
    return jnp.concatenate([high, middle], axis=-1), jnp.concatenate([low, jnp.zeros_like(low)], axis=-1)


def from_terms(first, second):
    rank = first.shape[-1] // 2
    return first[..., :rank] + first[..., rank:] + second[..., :rank]


def right_kernel(n_parts, *refs):
    part_refs, merged_ref = refs[:n_parts], refs[n_parts]
    lt_ref, chunk_ref, terms_ref = refs[n_parts + 1 :]
    parts = [ref[...].astype(F32) for ref in part_refs]
    while len(parts) > 1:
        parts = [a + b for a, b in zip(parts[0::2], parts[1::2])]
    lt = parts[0]
    rank = lt.shape[0]
    lt_ref[...] = lt.astype(BF16)
    product = left_times(lt, merged_ref[...], (((1,), (0,)), ((), ()))).astype(BF16)
    across = product.shape[1] // TILE_C
    for a in range(rank // TILE_R):
        for b in range(across):
            chunk_ref[a * across + b, 0:TILE_R] = product[
                a * TILE_R : (a + 1) * TILE_R, b * TILE_C : (b + 1) * TILE_C
            ]
    first, second = as_terms(
        lax.dot_general(lt, lt, COLS_LAST, precision=HIGHEST, preferred_element_type=F32)
    )
    terms_ref[0] = first
    terms_ref[1] = second
    piece = lax.rem(lax.axis_index("rep"), rank // 8)
    here = pl.ds(pl.multiple_of(piece * 8, 8), 8)
    piece = jnp.concatenate([terms_ref[0, here, :], terms_ref[1, here, :]], axis=0).astype(BF16)
    for c in range(chunk_ref.shape[0]):
        chunk_ref[c, TILE_R:] = piece


def right_product(parts, merged):
    rank, rows = parts[0].shape
    cols = merged.shape[1]
    assert 2 * rank == TILE_C
    chunks = rank * cols // (TILE_R * TILE_C)
    return pl.pallas_call(
        functools.partial(right_kernel, len(parts)),
        out_shape=[
            jax.ShapeDtypeStruct((rank, rows), BF16),
            jax.ShapeDtypeStruct((chunks, 2 * TILE_R, TILE_C), BF16),
        ],
        scratch_shapes=[pltpu.VMEM((2, rank, TILE_C), F32)],
        compiler_params=params(16),
        cost_estimate=SMALL,
        name="right_product",
    )(*parts, merged)


def fold_kernel(n_exp, share_ref, out_ref, gram_ref):
    total = share_ref[0, 0:TILE_R].astype(F32)
    for i in range(1, share_ref.shape[0]):
        total = total + share_ref[i, 0:TILE_R].astype(F32)
    total = total.astype(BF16)
    for i in range(out_ref.shape[0]):
        out_ref[i] = total
    for r in range(share_ref.shape[0] // n_exp):
        rows = None
        for j in range(n_exp):
            terms = share_ref[r * n_exp + j, TILE_R:].astype(F32)
            part = from_terms(terms[:8], terms[8:])
            rows = part if rows is None else rows + part
        gram_ref[8 * r : 8 * r + 8, :] = rows


def fold(shares, n_exp):
    count = shares.shape[0]
    rank = 8 * (count // n_exp)
    return pl.pallas_call(
        functools.partial(fold_kernel, n_exp),
        out_shape=[
            jax.ShapeDtypeStruct((count, TILE_R, TILE_C), BF16),
            jax.ShapeDtypeStruct((rank, rank), F32),
        ],
        compiler_params=params(4),
        cost_estimate=SMALL,
        name="fold",
    )(shares)


def fold_any(chunks, lt):
    total = lax.psum(chunks[:, :TILE_R].astype(F32), ("rep", "exp")).astype(BF16)
    wide = lt.astype(F32)
    return total, lax.psum(jnp.dot(wide, wide.T, precision=HIGHEST), "exp")


def inverse_of_factor(gram, wide_ref):
    rank = gram.shape[0]
    row = lax.broadcasted_iota(jnp.int32, (rank, rank), 0)
    col = lax.broadcasted_iota(jnp.int32, (rank, rank), 1)
    a = jnp.concatenate([gram, jnp.where(row == col, 1.0, 0.0).astype(F32)], axis=1)
    group = 4
    for k in range(0, rank, group):
        cols = [jnp.broadcast_to(a[:, k + j : k + j + 1], a.shape) for j in range(group)]
        rows = [a[k + j : k + j + 1, :] for j in range(group)]
        for j in range(group):
            pivot = cols[j][k + j : k + j + 1, :]
            wide_ref[k + j : k + j + 1, :] = rows[j] * lax.rsqrt(pivot)
            factor = cols[j] * (1.0 / pivot)
            for m in range(j + 1, group):
                cols[m] = cols[m] - factor * cols[m][k + j : k + j + 1, :]
                rows[m] = rows[m] - factor[k + m : k + m + 1, :] * rows[j]
            a = a - factor * rows[j]
    return wide_ref[:, rank:]


def inverse_kernel(gram_any, lt_any, w_ref, basis_ref, gram_ref, lt_ref, wide_ref, sems):
    gram_copy = pltpu.make_async_copy(gram_any, gram_ref, sems.at[0])
    gram_copy.start()
    lt_copy = pltpu.make_async_copy(lt_any, lt_ref, sems.at[1])
    lt_copy.start()
    gram_copy.wait()
    w = inverse_of_factor(gram_ref[...], wide_ref)
    w_ref[...] = w
    lt_copy.wait()
    basis_ref[...] = left_times(w, lt_ref[...], (((1,), (0,)), ((), ()))).T.astype(BF16)


def inverse_factor(gram, lt):
    rank, rows = lt.shape
    return pl.pallas_call(
        inverse_kernel,
        in_specs=[ANY] * 2,
        out_shape=[pltpu.HBM((rank, rank), F32), pltpu.HBM((rows, rank), BF16)],
        scratch_shapes=[
            pltpu.VMEM((rank, rank), F32),
            pltpu.VMEM((rank, rows), BF16),
            pltpu.VMEM((rank, 2 * rank), F32),
            pltpu.SemaphoreType.DMA((2,)),
        ],
        compiler_params=params(8),
        cost_estimate=pl.CostEstimate(flops=4_000_000_000, bytes_accessed=1000, transcendentals=0),
        name="inverse_factor",
    )(gram, lt)


def finish_kernel(
    replicas, w_any, chunk_ref, basis_any, merged_ref, right_hbm, err_hbm, w_ref, basis_ref, right_ref, err_ref, sems
):
    rank, cols = right_ref.shape
    rows, block = err_ref.shape[0], 128
    w_copy = pltpu.make_async_copy(w_any, w_ref, sems.at[rows // block + 1])
    w_copy.start()
    basis_copy = pltpu.make_async_copy(basis_any, basis_ref, sems.at[rows // block + 2])
    basis_copy.start()
    across = cols // TILE_C
    pieces = []
    for a in range(rank // TILE_R):
        pieces.append(jnp.concatenate([chunk_ref[a * across + b] for b in range(across)], axis=1))
    product = jnp.concatenate(pieces, axis=0)
    w_copy.wait()
    new_right = left_times(w_ref[...], product, (((1,), (0,)), ((), ()))) * (1.0 / replicas)
    right_ref[...] = new_right
    copies = [pltpu.make_async_copy(right_ref, right_hbm, sems.at[0])]
    copies[0].start()
    rounded = new_right.astype(BF16)
    basis_copy.wait()
    for i in range(rows // block):
        here = slice(i * block, (i + 1) * block)
        approx = jnp.dot(basis_ref[here, :], rounded, preferred_element_type=F32)
        err_ref[here, :] = (merged_ref[here, :].astype(F32) - approx).astype(BF16)
        copies.append(
            pltpu.make_async_copy(err_ref.at[here, :], err_hbm.at[0, here, :], sems.at[i + 1])
        )
        copies[-1].start()
    for copy in copies:
        copy.wait()


def finish(replicas, w, chunks, basis, merged):
    rows, rank = basis.shape
    cols = merged.shape[1]
    return pl.pallas_call(
        functools.partial(finish_kernel, replicas),
        in_specs=[HBM, VMEM, HBM, VMEM],
        out_specs=[HBM] * 2,
        out_shape=[
            jax.ShapeDtypeStruct((rank, cols), F32),
            jax.ShapeDtypeStruct((1, rows, cols), BF16),
        ],
        scratch_shapes=[
            pltpu.VMEM((rank, rank), F32),
            pltpu.VMEM((rows, rank), BF16),
            pltpu.VMEM((rank, cols), F32),
            pltpu.VMEM((rows, cols), BF16),
            pltpu.SemaphoreType.DMA((rows // 128 + 3,)),
        ],
        compiler_params=params(16),
        cost_estimate=SMALL,
        name="finish",
    )(*in_hbm(w), chunks, *in_hbm(basis), merged)


def expert_kernel(n_exp, n_grad, chunk, *refs):
    load_hbms, grad_hbms = refs[:n_exp], refs[n_exp : n_exp + n_grad]
    one_hbm, two_hbm, first_hbm, second_hbm, step_hbm = refs[n_exp + n_grad : n_exp + n_grad + 5]
    hid, rows, one, two, first, second, step, in_sems, out_sems = refs[n_exp + n_grad + 5 :]
    units, width = one.shape
    count = width // chunk

    slabs = [
        pltpu.make_async_copy(load_hbms[k], hid.at[k], in_sems.at[count, k])
        for k in range(n_exp)
    ]

    def loads(c):
        here = slice(c * chunk, (c + 1) * chunk)
        pairs, at = [], 0
        for grad_hbm in grad_hbms:
            end = at + grad_hbm.shape[1]
            pairs.append((grad_hbm.at[0, :, here], rows.at[at:end, here]))
            at = end
        pairs += [(one_hbm.at[0, :, here], one.at[:, here]), (two_hbm.at[0, :, here], two.at[:, here])]
        return [pltpu.make_async_copy(a, b, in_sems.at[c, i]) for i, (a, b) in enumerate(pairs)]

    def stores(c):
        here = slice(c * chunk, (c + 1) * chunk)
        pairs = [(first, first_hbm), (second, second_hbm), (step, step_hbm)]
        return [
            pltpu.make_async_copy(a.at[:, here], b.at[0, :, here], out_sems.at[c, i])
            for i, (a, b) in enumerate(pairs)
        ]

    for copy in slabs:
        copy.start()
    for c in range(count):
        for copy in loads(c):
            copy.start()
    for copy in slabs:
        copy.wait()
    left = jnp.concatenate([hid[k] for k in range(n_exp)], axis=1)
    for c in range(count):
        here = slice(c * chunk, (c + 1) * chunk)
        for copy in loads(c):
            copy.wait()
        grad = jnp.dot(left, rows[:, here], preferred_element_type=F32)
        first_new = beta_one * one[:, here] + (1.0 - beta_one) * grad
        second_new = beta_two * two[:, here] + (1.0 - beta_two) * grad * grad
        first[:, here] = first_new
        second[:, here] = second_new
        scaled = second_new * (1.0 / correction_two)
        bottom = scaled * lax.rsqrt(scaled) + epsilon
        step[:, here] = (
            first_new * (1.0 / correction_one) * pl.reciprocal(bottom, approx=True)
        ).astype(BF16)
        for copy in stores(c):
            copy.start()
    for c in range(count):
        for copy in stores(c):
            copy.wait()


def expert_step(slabs, grads, moment_one, moment_two):
    _, units, width = moment_one.shape
    chunk = 512
    n_exp, n_grad = len(slabs), len(grads)
    tokens = slabs[0].shape[1]
    return pl.pallas_call(
        functools.partial(expert_kernel, n_exp, n_grad, chunk),
        in_specs=[ANY] * n_exp + [HBM] + [ANY] * (n_grad - 1) + [HBM] * 2,
        out_specs=[HBM] * 3,
        out_shape=[
            jax.ShapeDtypeStruct((1, units, width), F32),
            jax.ShapeDtypeStruct((1, units, width), F32),
            jax.ShapeDtypeStruct((1, units, width), BF16),
        ],
        scratch_shapes=[
            pltpu.VMEM((n_exp, units, tokens), BF16),
            pltpu.VMEM((n_exp * tokens, width), BF16),
            pltpu.VMEM((units, width), F32),
            pltpu.VMEM((units, width), F32),
            pltpu.VMEM((units, width), F32),
            pltpu.VMEM((units, width), F32),
            pltpu.VMEM((units, width), BF16),
            pltpu.SemaphoreType.DMA((width // chunk + 1, n_grad + 2)),
            pltpu.SemaphoreType.DMA((width // chunk, 3)),
        ],
        compiler_params=params(24),
        cost_estimate=SMALL,
        name="expert_step",
    )(
        *slabs, *in_hbm(grads[0]), *grads[1:], *in_hbm(moment_one, moment_two)
    )


def swap(x, axis, size, mask):
    return lax.ppermute(x, axis, [(i, i ^ mask) for i in range(size)])


def shift(x, size, k):
    return lax.ppermute(x, "exp", [(i, (i + k) % size) for i in range(size)])


def after(x, y):
    return lax.optimization_barrier((x, y))[0]


def body(n_rep, n_exp, activations, kv_grad, errors, right_factor, hidden, out_grad, moment_one, moment_two):
    half = out_grad.shape[1] // 2
    left_first = shift(out_grad[:, :half], n_exp, -1)
    merged, lt = merge(activations, kv_grad, errors, right_factor.T)

    lt, left_first = lax.optimization_barrier((lt, left_first))
    grads = {0: [out_grad], 1: [shift(out_grad, n_exp, 1)]}
    grads[n_exp - 1] = [left_first, shift(out_grad[:, half:], n_exp, -1)]

    lt = (lt + swap(lt, "rep", n_rep, 1)).astype(BF16)
    slabs = unit_slabs(after(hidden, lt), n_exp)
    bit = 2
    parts = [lt]
    while bit < n_rep:
        while len(parts) > 1:
            parts = [a.astype(F32) + b.astype(F32) for a, b in zip(parts[0::2], parts[1::2])]
        own = parts[0].astype(BF16)
        masks = [bit] if 2 * bit >= n_rep else [bit, 2 * bit, 3 * bit]
        parts = [own] + [swap(own, "rep", n_rep, m) for m in masks]
        bit *= len(parts)
    lt, chunks = right_product(parts, merged)

    fits = chunks.shape[0] == n_rep * n_exp and 8 * n_rep == lt.shape[0]
    both = ("rep", "exp")
    if fits:
        shares = lax.all_to_all(chunks, both, 0, 0, tiled=True)
        shares, grads = lax.optimization_barrier((shares, grads))
        share, gram = fold(shares, n_exp)
        chunks = lax.all_to_all(share, both, 0, 0, tiled=True)
    else:
        share, gram = fold_any(chunks, lt)
        chunks = share
    w, basis = inverse_factor(gram, lt)

    slabs = [slabs[0]] + [shift(after(slabs[k], share), n_exp, k) for k in range(1, n_exp)]
    left, right = 1, n_exp - 1
    while right - left > 1:
        if left <= n_exp - right:
            grads[left + 1] = [shift(after(g, share), n_exp, 1) for g in grads[left]]
            left += 1
        else:
            grads[right - 1] = [shift(after(g, share), n_exp, -1) for g in grads[right]]
            right -= 1

    new_right, new_error = finish(n_rep, w, chunks, basis, merged)
    first_new, second_new, step = expert_step(
        slabs, [g for k in range(n_exp) for g in grads[k]], moment_one, moment_two
    )
    return new_error, new_right.T, first_new, second_new, step


def solution(mesh):
    placed = (
        P("rep", "exp"),
        P("rep", None),
        P("rep", "exp", None),
        P(),
        P("rep", "exp", None),
        P("rep", "exp", None),
        P("rep", "exp", None),
        P("rep", "exp", None),
    )
    return jax.shard_map(
        functools.partial(body, mesh.shape["rep"], mesh.shape["exp"]),
        mesh=mesh,
        in_specs=placed,
        out_specs=(
            P("rep", "exp", None),
            P(),
            P("rep", "exp", None),
            P("rep", "exp", None),
            P("rep", "exp", None),
        ),
        check_vma=False,
    )
```

```python
import functools

import jax
import jax.numpy as jnp
from jax import lax
from jax.experimental import pallas as pl
from jax.experimental.pallas import tpu as pltpu
from jax.sharding import PartitionSpec as P

HIGHEST = lax.Precision.HIGHEST
F32 = jnp.float32
BF16 = jnp.bfloat16
beta_one = 0.9
beta_two = 0.99
correction_one = 1.0 - 0.9**10
correction_two = 1.0 - 0.99**10
epsilon = 1e-08

ROWS_FIRST = (((0,), (0,)), ((), ()))
COLS_LAST = (((1,), (1,)), ((), ()))
TILE_R, TILE_C = 16, 128
HBM = pl.BlockSpec(memory_space=pltpu.HBM)
ANY = pl.BlockSpec(memory_space=pl.ANY)
VMEM = pl.BlockSpec(memory_space=pltpu.VMEM)


def params(mebibytes):
    return pltpu.CompilerParams(vmem_limit_bytes=mebibytes * 1024 * 1024)


def in_hbm(*arrays):
    return [pltpu.with_memory_space_constraint(x, pltpu.HBM) for x in arrays]


SMALL = pl.CostEstimate(flops=1000, bytes_accessed=1000, transcendentals=0)


def split_two(x):
    hi = x.astype(BF16)
    return hi, (x - hi.astype(F32)).astype(BF16)


def left_times(left, right_bf16, dims):
    rows = left.shape[0]
    hi, lo = split_two(left)
    both = jnp.concatenate([hi, lo], axis=0)
    out = lax.dot_general(both, right_bf16, dims, preferred_element_type=F32)
    return out[:rows] + out[rows:]


def merge_kernel(acts_ref, kv_ref, err_ref, vt_ref, merged_ref, lt_ref):
    merged = lax.dot_general(acts_ref[...], kv_ref[...], ROWS_FIRST, preferred_element_type=F32)
    merged = (merged + err_ref[0].astype(F32)).astype(BF16)
    merged_ref[...] = merged
    lt_ref[...] = left_times(vt_ref[...], merged, COLS_LAST)


def merge(acts, kv, err, vt):
    tokens, rows = acts.shape
    cols = kv.shape[1]
    rank = vt.shape[0]
    block = 256
    return pl.pallas_call(
        merge_kernel,
        grid=(rows // block,),
        in_specs=[
            pl.BlockSpec((tokens, block), lambda i: (0, i)),
            pl.BlockSpec((tokens, cols), lambda i: (0, 0)),
            pl.BlockSpec((1, block, cols), lambda i: (0, i, 0)),
            pl.BlockSpec((rank, cols), lambda i: (0, 0)),
        ],
        out_specs=[
            pl.BlockSpec((block, cols), lambda i: (i, 0)),
            pl.BlockSpec((rank, block), lambda i: (0, i)),
        ],
        out_shape=[
            jax.ShapeDtypeStruct((rows, cols), BF16),
            jax.ShapeDtypeStruct((rank, rows), F32),
        ],
        compiler_params=params(24),
        cost_estimate=pl.CostEstimate(flops=4_000_000_000, bytes_accessed=8_000_000, transcendentals=0),
        name="merge",
    )(*[pltpu.with_memory_space_constraint(x, pltpu.HBM) for x in (acts, kv, err, vt)])


def slab_kernel(hidden_ref, own_ref, *refs):
    send_refs, all_ref = refs[:-1], refs[-1]
    n_exp = all_ref.shape[0]
    all_ref[...] = hidden_ref[0].T.reshape(all_ref.shape)
    place = lax.axis_index("exp")
    for k, ref in enumerate((own_ref,) + tuple(send_refs)):
        ref[...] = all_ref[lax.rem(place + k, n_exp)]


def unit_slabs(hidden, n_exp):
    _, tokens, units = hidden.shape
    slab = (units // n_exp, tokens)
    return pl.pallas_call(
        slab_kernel,
        out_shape=[pltpu.HBM(slab, BF16)] * n_exp,
        scratch_shapes=[pltpu.VMEM((n_exp,) + slab, BF16)],
        compiler_params=params(8),
        cost_estimate=SMALL,
        name="unit_slabs",
    )(hidden)


def as_terms(x, hold=lambda rounded: rounded):
    high = hold(x.astype(BF16)).astype(F32)
    rest = x - high
    middle = hold(rest.astype(BF16)).astype(F32)
    low = rest - middle
    return jnp.concatenate([high, middle], axis=-1), jnp.concatenate([low, jnp.zeros_like(low)], axis=-1)


def from_terms(first, second):
    rank = first.shape[-1] // 2
    return first[..., :rank] + first[..., rank:] + second[..., :rank]


def right_kernel(n_parts, *refs):
    part_refs, merged_ref = refs[:n_parts], refs[n_parts]
    lt_ref, chunk_ref, terms_ref = refs[n_parts + 1 :]
    parts = [ref[...].astype(F32) for ref in part_refs]
    while len(parts) > 1:
        parts = [a + b for a, b in zip(parts[0::2], parts[1::2])]
    lt = parts[0]
    rank = lt.shape[0]
    lt_ref[...] = lt.astype(BF16)
    product = left_times(lt, merged_ref[...], (((1,), (0,)), ((), ()))).astype(BF16)
    across = product.shape[1] // TILE_C
    for a in range(rank // TILE_R):
        for b in range(across):
            chunk_ref[a * across + b, 0:TILE_R] = product[
                a * TILE_R : (a + 1) * TILE_R, b * TILE_C : (b + 1) * TILE_C
            ]
    first, second = as_terms(
        lax.dot_general(lt, lt, COLS_LAST, precision=HIGHEST, preferred_element_type=F32)
    )
    terms_ref[0] = first
    terms_ref[1] = second
    piece = lax.rem(lax.axis_index("rep"), rank // 8)
    here = pl.ds(pl.multiple_of(piece * 8, 8), 8)
    piece = jnp.concatenate([terms_ref[0, here, :], terms_ref[1, here, :]], axis=0).astype(BF16)
    for c in range(chunk_ref.shape[0]):
        chunk_ref[c, TILE_R:] = piece


def right_product(parts, merged):
    rank, rows = parts[0].shape
    cols = merged.shape[1]
    assert 2 * rank == TILE_C
    chunks = rank * cols // (TILE_R * TILE_C)
    return pl.pallas_call(
        functools.partial(right_kernel, len(parts)),
        out_shape=[
            jax.ShapeDtypeStruct((rank, rows), BF16),
            jax.ShapeDtypeStruct((chunks, 2 * TILE_R, TILE_C), BF16),
        ],
        scratch_shapes=[pltpu.VMEM((2, rank, TILE_C), F32)],
        compiler_params=params(16),
        cost_estimate=SMALL,
        name="right_product",
    )(*parts, merged)


def fold_kernel(n_exp, share_ref, out_ref, gram_ref):
    total = share_ref[0, 0:TILE_R].astype(F32)
    for i in range(1, share_ref.shape[0]):
        total = total + share_ref[i, 0:TILE_R].astype(F32)
    total = total.astype(BF16)
    for i in range(out_ref.shape[0]):
        out_ref[i] = total
    for r in range(share_ref.shape[0] // n_exp):
        rows = None
        for j in range(n_exp):
            terms = share_ref[r * n_exp + j, TILE_R:].astype(F32)
            part = from_terms(terms[:8], terms[8:])
            rows = part if rows is None else rows + part
        gram_ref[8 * r : 8 * r + 8, :] = rows


def fold(shares, n_exp):
    count = shares.shape[0]
    rank = 8 * (count // n_exp)
    return pl.pallas_call(
        functools.partial(fold_kernel, n_exp),
        out_shape=[
            jax.ShapeDtypeStruct((count, TILE_R, TILE_C), BF16),
            jax.ShapeDtypeStruct((rank, rank), F32),
        ],
        compiler_params=params(4),
        cost_estimate=SMALL,
        name="fold",
    )(shares)


def fold_any(chunks, lt):
    total = lax.psum(chunks[:, :TILE_R].astype(F32), ("rep", "exp")).astype(BF16)
    wide = lt.astype(F32)
    return total, lax.psum(jnp.dot(wide, wide.T, precision=HIGHEST), "exp")


def inverse_of_factor(gram, wide_ref):
    rank = gram.shape[0]
    row = lax.broadcasted_iota(jnp.int32, (rank, rank), 0)
    col = lax.broadcasted_iota(jnp.int32, (rank, rank), 1)
    a = jnp.concatenate([gram, jnp.where(row == col, 1.0, 0.0).astype(F32)], axis=1)
    group = 4
    for k in range(0, rank, group):
        cols = [jnp.broadcast_to(a[:, k + j : k + j + 1], a.shape) for j in range(group)]
        rows = [a[k + j : k + j + 1, :] for j in range(group)]
        for j in range(group):
            pivot = cols[j][k + j : k + j + 1, :]
            wide_ref[k + j : k + j + 1, :] = rows[j] * lax.rsqrt(pivot)
            factor = cols[j] * (1.0 / pivot)
            for m in range(j + 1, group):
                cols[m] = cols[m] - factor * cols[m][k + j : k + j + 1, :]
                rows[m] = rows[m] - factor[k + m : k + m + 1, :] * rows[j]
            a = a - factor * rows[j]
    return wide_ref[:, rank:]


def inverse_kernel(gram_any, lt_any, w_ref, basis_ref, gram_ref, lt_ref, wide_ref, sems):
    gram_copy = pltpu.make_async_copy(gram_any, gram_ref, sems.at[0])
    gram_copy.start()
    lt_copy = pltpu.make_async_copy(lt_any, lt_ref, sems.at[1])
    lt_copy.start()
    gram_copy.wait()
    w = inverse_of_factor(gram_ref[...], wide_ref)
    w_ref[...] = w
    lt_copy.wait()
    basis_ref[...] = left_times(w, lt_ref[...], (((1,), (0,)), ((), ()))).T.astype(BF16)


def inverse_factor(gram, lt):
    rank, rows = lt.shape
    return pl.pallas_call(
        inverse_kernel,
        in_specs=[ANY] * 2,
        out_shape=[pltpu.HBM((rank, rank), F32), pltpu.HBM((rows, rank), BF16)],
        scratch_shapes=[
            pltpu.VMEM((rank, rank), F32),
            pltpu.VMEM((rank, rows), BF16),
            pltpu.VMEM((rank, 2 * rank), F32),
            pltpu.SemaphoreType.DMA((2,)),
        ],
        compiler_params=params(8),
        cost_estimate=pl.CostEstimate(flops=4_000_000_000, bytes_accessed=1000, transcendentals=0),
        name="inverse_factor",
    )(*in_hbm(gram, lt))


def finish_kernel(
    replicas, w_any, chunk_ref, basis_any, merged_ref, right_hbm, err_hbm, w_ref, basis_ref, right_ref, err_ref, sems
):
    rank, cols = right_ref.shape
    rows, block = err_ref.shape[0], 128
    w_copy = pltpu.make_async_copy(w_any, w_ref, sems.at[rows // block + 1])
    w_copy.start()
    basis_copy = pltpu.make_async_copy(basis_any, basis_ref, sems.at[rows // block + 2])
    basis_copy.start()
    across = cols // TILE_C
    pieces = []
    for a in range(rank // TILE_R):
        pieces.append(jnp.concatenate([chunk_ref[a * across + b] for b in range(across)], axis=1))
    product = jnp.concatenate(pieces, axis=0)
    w_copy.wait()
    new_right = left_times(w_ref[...], product, (((1,), (0,)), ((), ()))) * (1.0 / replicas)
    right_ref[...] = new_right
    copies = [pltpu.make_async_copy(right_ref, right_hbm, sems.at[0])]
    copies[0].start()
    rounded = new_right.astype(BF16)
    basis_copy.wait()
    for i in range(rows // block):
        here = slice(i * block, (i + 1) * block)
        approx = jnp.dot(basis_ref[here, :], rounded, preferred_element_type=F32)
        err_ref[here, :] = (merged_ref[here, :].astype(F32) - approx).astype(BF16)
        copies.append(
            pltpu.make_async_copy(err_ref.at[here, :], err_hbm.at[0, here, :], sems.at[i + 1])
        )
        copies[-1].start()
    for copy in copies:
        copy.wait()


def finish(replicas, w, chunks, basis, merged):
    rows, rank = basis.shape
    cols = merged.shape[1]
    return pl.pallas_call(
        functools.partial(finish_kernel, replicas),
        in_specs=[HBM, VMEM, HBM, VMEM],
        out_specs=[HBM] * 2,
        out_shape=[
            jax.ShapeDtypeStruct((rank, cols), F32),
            jax.ShapeDtypeStruct((1, rows, cols), BF16),
        ],
        scratch_shapes=[
            pltpu.VMEM((rank, rank), F32),
            pltpu.VMEM((rows, rank), BF16),
            pltpu.VMEM((rank, cols), F32),
            pltpu.VMEM((rows, cols), BF16),
            pltpu.SemaphoreType.DMA((rows // 128 + 3,)),
        ],
        compiler_params=params(16),
        cost_estimate=SMALL,
        name="finish",
    )(*in_hbm(w), chunks, *in_hbm(basis), merged)


def expert_kernel(n_exp, n_grad, chunk, *refs):
    load_hbms, grad_hbms = refs[:n_exp], refs[n_exp : n_exp + n_grad]
    one_hbm, two_hbm, first_hbm, second_hbm, step_hbm = refs[n_exp + n_grad : n_exp + n_grad + 5]
    hid, rows, one, two, first, second, step, in_sems, out_sems = refs[n_exp + n_grad + 5 :]
    units, width = one.shape
    count = width // chunk

    slabs = [
        pltpu.make_async_copy(load_hbms[k], hid.at[k], in_sems.at[count, k])
        for k in range(n_exp)
    ]

    def loads(c):
        here = slice(c * chunk, (c + 1) * chunk)
        pairs, at = [], 0
        for grad_hbm in grad_hbms:
            end = at + grad_hbm.shape[1]
            pairs.append((grad_hbm.at[0, :, here], rows.at[at:end, here]))
            at = end
        pairs += [(one_hbm.at[0, :, here], one.at[:, here]), (two_hbm.at[0, :, here], two.at[:, here])]
        return [pltpu.make_async_copy(a, b, in_sems.at[c, i]) for i, (a, b) in enumerate(pairs)]

    def stores(c):
        here = slice(c * chunk, (c + 1) * chunk)
        pairs = [(first, first_hbm), (second, second_hbm), (step, step_hbm)]
        return [
            pltpu.make_async_copy(a.at[:, here], b.at[0, :, here], out_sems.at[c, i])
            for i, (a, b) in enumerate(pairs)
        ]

    for copy in slabs:
        copy.start()
    for c in range(count):
        for copy in loads(c):
            copy.start()
    for copy in slabs:
        copy.wait()
    left = jnp.concatenate([hid[k] for k in range(n_exp)], axis=1)
    for c in range(count):
        here = slice(c * chunk, (c + 1) * chunk)
        for copy in loads(c):
            copy.wait()
        grad = jnp.dot(left, rows[:, here], preferred_element_type=F32)
        first_new = beta_one * one[:, here] + (1.0 - beta_one) * grad
        second_new = beta_two * two[:, here] + (1.0 - beta_two) * grad * grad
        first[:, here] = first_new
        second[:, here] = second_new
        scaled = second_new * (1.0 / correction_two)
        bottom = scaled * lax.rsqrt(scaled) + epsilon
        step[:, here] = (
            first_new * (1.0 / correction_one) * pl.reciprocal(bottom, approx=True)
        ).astype(BF16)
        for copy in stores(c):
            copy.start()
    for c in range(count):
        for copy in stores(c):
            copy.wait()


def expert_step(slabs, grads, moment_one, moment_two):
    _, units, width = moment_one.shape
    chunk = 512
    n_exp, n_grad = len(slabs), len(grads)
    tokens = slabs[0].shape[1]
    return pl.pallas_call(
        functools.partial(expert_kernel, n_exp, n_grad, chunk),
        in_specs=[ANY] * n_exp + [HBM] + [ANY] * (n_grad - 1) + [HBM] * 2,
        out_specs=[HBM] * 3,
        out_shape=[
            jax.ShapeDtypeStruct((1, units, width), F32),
            jax.ShapeDtypeStruct((1, units, width), F32),
            jax.ShapeDtypeStruct((1, units, width), BF16),
        ],
        scratch_shapes=[
            pltpu.VMEM((n_exp, units, tokens), BF16),
            pltpu.VMEM((n_exp * tokens, width), BF16),
            pltpu.VMEM((units, width), F32),
            pltpu.VMEM((units, width), F32),
            pltpu.VMEM((units, width), F32),
            pltpu.VMEM((units, width), F32),
            pltpu.VMEM((units, width), BF16),
            pltpu.SemaphoreType.DMA((width // chunk + 1, n_grad + 2)),
            pltpu.SemaphoreType.DMA((width // chunk, 3)),
        ],
        compiler_params=params(24),
        cost_estimate=SMALL,
        name="expert_step",
    )(
        *slabs, *in_hbm(grads[0]), *grads[1:], *in_hbm(moment_one, moment_two)
    )


def swap(x, axis, size, mask):
    return lax.ppermute(x, axis, [(i, i ^ mask) for i in range(size)])


def shift(x, size, k):
    return lax.ppermute(x, "exp", [(i, (i + k) % size) for i in range(size)])


def after(x, y):
    return lax.optimization_barrier((x, y))[0]


def body(n_rep, n_exp, activations, kv_grad, errors, right_factor, hidden, out_grad, moment_one, moment_two):
    grads = {0: out_grad, n_exp - 1: shift(out_grad, n_exp, -1)}
    merged, lt = merge(activations, kv_grad, errors, right_factor.T)

    lt = lt + swap(lt, "rep", n_rep, 1)
    lt, grads[n_exp - 1] = lax.optimization_barrier((lt, grads[n_exp - 1]))
    lt = lt.astype(BF16)
    if n_exp > 2:
        grads[1] = shift(after(out_grad, lt), n_exp, 1)
    slabs = unit_slabs(after(hidden, lt), n_exp)
    bit = 2
    parts = [lt]
    while bit < n_rep:
        while len(parts) > 1:
            parts = [a.astype(F32) + b.astype(F32) for a, b in zip(parts[0::2], parts[1::2])]
        own = parts[0].astype(BF16)
        masks = [bit] if 2 * bit >= n_rep else [bit, 2 * bit, 3 * bit]
        parts = [own] + [swap(own, "rep", n_rep, m) for m in masks]
        bit *= len(parts)
    lt, chunks = right_product(parts, merged)

    fits = chunks.shape[0] == n_rep * n_exp and 8 * n_rep == lt.shape[0]
    both = ("rep", "exp")
    slabs = [slabs[0]] + [shift(after(slabs[k], chunks), n_exp, k) for k in range(1, n_exp)]
    if fits:
        shares = lax.all_to_all(chunks, both, 0, 0, tiled=True)
        shares, grads = lax.optimization_barrier((shares, grads))
        share, gram = fold(shares, n_exp)
        share, slabs = lax.optimization_barrier((share, slabs))
        chunks = lax.all_to_all(share, both, 0, 0, tiled=True)
    else:
        share, gram = fold_any(chunks, lt)
        chunks = share
    w, basis = inverse_factor(gram, lt)

    left, right = 1, n_exp - 1
    while right - left > 1:
        if left <= n_exp - right:
            grads[left + 1] = shift(after(grads[left], share), n_exp, 1)
            left += 1
        else:
            grads[right - 1] = shift(after(grads[right], share), n_exp, -1)
            right -= 1

    new_right, new_error = finish(n_rep, w, chunks, basis, merged)
    first_new, second_new, step = expert_step(
        slabs, [grads[k] for k in range(n_exp)], moment_one, moment_two
    )
    return new_error, new_right.T, first_new, second_new, step


def solution(mesh):
    placed = (
        P("rep", "exp"),
        P("rep", None),
        P("rep", "exp", None),
        P(),
        P("rep", "exp", None),
        P("rep", "exp", None),
        P("rep", "exp", None),
        P("rep", "exp", None),
    )
    return jax.shard_map(
        functools.partial(body, mesh.shape["rep"], mesh.shape["exp"]),
        mesh=mesh,
        in_specs=placed,
        out_specs=(
            P("rep", "exp", None),
            P(),
            P("rep", "exp", None),
            P("rep", "exp", None),
            P("rep", "exp", None),
        ),
        check_vma=False,
    )
```

```python
import functools

import jax
import jax.numpy as jnp
from jax import lax
from jax.experimental import pallas as pl
from jax.experimental.pallas import tpu as pltpu
from jax.sharding import PartitionSpec as P

HIGHEST = lax.Precision.HIGHEST
F32 = jnp.float32
BF16 = jnp.bfloat16
beta_one = 0.9
beta_two = 0.99
correction_one = 1.0 - 0.9**10
correction_two = 1.0 - 0.99**10
epsilon = 1e-08

ROWS_FIRST = (((0,), (0,)), ((), ()))
COLS_LAST = (((1,), (1,)), ((), ()))
TILE_R, TILE_C = 16, 128
HBM = pl.BlockSpec(memory_space=pltpu.HBM)
ANY = pl.BlockSpec(memory_space=pl.ANY)
VMEM = pl.BlockSpec(memory_space=pltpu.VMEM)


def params(mebibytes):
    return pltpu.CompilerParams(vmem_limit_bytes=mebibytes * 1024 * 1024)


def in_hbm(*arrays):
    return [pltpu.with_memory_space_constraint(x, pltpu.HBM) for x in arrays]


SMALL = pl.CostEstimate(flops=1000, bytes_accessed=1000, transcendentals=0)


def split_two(x):
    hi = x.astype(BF16)
    return hi, (x - hi.astype(F32)).astype(BF16)


def left_times(left, right_bf16, dims):
    rows = left.shape[0]
    hi, lo = split_two(left)
    both = jnp.concatenate([hi, lo], axis=0)
    out = lax.dot_general(both, right_bf16, dims, preferred_element_type=F32)
    return out[:rows] + out[rows:]


def merge_kernel(acts_ref, kv_ref, err_ref, vt_ref, merged_ref, lt_ref):
    merged = lax.dot_general(acts_ref[...], kv_ref[...], ROWS_FIRST, preferred_element_type=F32)
    merged = (merged + err_ref[0].astype(F32)).astype(BF16)
    merged_ref[...] = merged
    lt_ref[...] = left_times(vt_ref[...], merged, COLS_LAST)


def merge(acts, kv, err, vt):
    tokens, rows = acts.shape
    cols = kv.shape[1]
    rank = vt.shape[0]
    block = 256
    return pl.pallas_call(
        merge_kernel,
        grid=(rows // block,),
        in_specs=[
            pl.BlockSpec((tokens, block), lambda i: (0, i)),
            pl.BlockSpec((tokens, cols), lambda i: (0, 0)),
            pl.BlockSpec((1, block, cols), lambda i: (0, i, 0)),
            pl.BlockSpec((rank, cols), lambda i: (0, 0)),
        ],
        out_specs=[
            pl.BlockSpec((block, cols), lambda i: (i, 0)),
            pl.BlockSpec((rank, block), lambda i: (0, i)),
        ],
        out_shape=[
            jax.ShapeDtypeStruct((rows, cols), BF16),
            jax.ShapeDtypeStruct((rank, rows), F32),
        ],
        compiler_params=params(24),
        cost_estimate=pl.CostEstimate(flops=4_000_000_000, bytes_accessed=8_000_000, transcendentals=0),
        name="merge",
    )(*[pltpu.with_memory_space_constraint(x, pltpu.HBM) for x in (acts, kv, err, vt)])


def slab_kernel(hidden_ref, own_ref, *refs):
    send_refs, all_ref = refs[:-1], refs[-1]
    n_exp = all_ref.shape[0]
    all_ref[...] = hidden_ref[0].T.reshape(all_ref.shape)
    place = lax.axis_index("exp")
    for k, ref in enumerate((own_ref,) + tuple(send_refs)):
        ref[...] = all_ref[lax.rem(place + k, n_exp)]


def unit_slabs(hidden, n_exp):
    _, tokens, units = hidden.shape
    slab = (units // n_exp, tokens)
    return pl.pallas_call(
        slab_kernel,
        out_shape=[pltpu.HBM(slab, BF16)] * n_exp,
        scratch_shapes=[pltpu.VMEM((n_exp,) + slab, BF16)],
        compiler_params=params(8),
        cost_estimate=SMALL,
        name="unit_slabs",
    )(hidden)


def right_kernel(n_parts, *refs):
    part_refs, merged_ref = refs[:n_parts], refs[n_parts]
    lt_ref, gram_ref, chunk_ref = refs[n_parts + 1 :]
    parts = [ref[...].astype(F32) for ref in part_refs]
    while len(parts) > 1:
        parts = [a + b for a, b in zip(parts[0::2], parts[1::2])]
    lt = parts[0]
    rank = lt.shape[0]
    lt_ref[...] = lt.astype(BF16)
    gram = lax.dot_general(lt, lt, COLS_LAST, precision=HIGHEST, preferred_element_type=F32)
    half = rank // 2
    packed = jnp.concatenate([gram[:half], gram[half:]], axis=1)
    high = packed.astype(BF16)
    rest = packed - high.astype(F32)
    middle = rest.astype(BF16)
    low = (rest - middle.astype(F32)).astype(BF16)
    gram_ref[0:half] = high
    gram_ref[half : 2 * half] = middle
    gram_ref[2 * half : 3 * half] = low
    product = left_times(lt, merged_ref[...], (((1,), (0,)), ((), ()))).astype(BF16)
    across = product.shape[1] // TILE_C
    for a in range(rank // TILE_R):
        for b in range(across):
            chunk_ref[a * across + b] = product[
                a * TILE_R : (a + 1) * TILE_R, b * TILE_C : (b + 1) * TILE_C
            ]


def right_product(parts, merged):
    rank, rows = parts[0].shape
    cols = merged.shape[1]
    chunks = rank * cols // (TILE_R * TILE_C)
    return pl.pallas_call(
        functools.partial(right_kernel, len(parts)),
        out_shape=[
            jax.ShapeDtypeStruct((rank, rows), BF16),
            pltpu.HBM((3 * (rank // 2), 2 * rank), BF16),
            jax.ShapeDtypeStruct((chunks, TILE_R, TILE_C), BF16),
        ],
        compiler_params=params(16),
        cost_estimate=SMALL,
        name="right_product",
    )(*parts, merged)


def load_kernel(share_ref, gram_hbm, load_ref, gram_ref, sem):
    terms = gram_ref.shape[0]
    copy = pltpu.make_async_copy(gram_hbm, gram_ref, sem)
    copy.start()
    total = share_ref[0].astype(F32)
    for i in range(1, share_ref.shape[0]):
        total = total + share_ref[i].astype(F32)
    load_ref[terms:] = total.astype(BF16)
    copy.wait()
    load_ref[0:terms] = gram_ref[...]


def line_load(shares, gram):
    return pl.pallas_call(
        load_kernel,
        in_specs=[VMEM, HBM],
        out_shape=jax.ShapeDtypeStruct((gram.shape[0] + shares.shape[1], TILE_C), BF16),
        scratch_shapes=[pltpu.VMEM(gram.shape, BF16), pltpu.SemaphoreType.DMA],
        compiler_params=params(4),
        cost_estimate=SMALL,
        name="line_load",
    )(shares, *in_hbm(gram))


def line_kernel(terms, *refs):
    load_refs, out_ref, parts_ref = refs[:-2], refs[-2], refs[-1]
    n_exp = len(load_refs)
    for k in range(n_exp):
        parts_ref[k] = load_refs[k][terms:].astype(F32)
    place = lax.axis_index("exp")
    total = None
    for j in range(n_exp):
        part = parts_ref[lax.rem(place + n_exp - j, n_exp)]
        total = part if total is None else total + part
    total = total.astype(BF16)
    for i in range(out_ref.shape[0]):
        out_ref[i] = total


def line_sum(loads, terms, n_rep):
    rows = loads[0].shape[0] - terms
    return pl.pallas_call(
        functools.partial(line_kernel, terms),
        out_shape=jax.ShapeDtypeStruct((n_rep, rows, TILE_C), BF16),
        scratch_shapes=[pltpu.VMEM((len(loads), rows, TILE_C), F32)],
        compiler_params=params(4),
        cost_estimate=SMALL,
        name="line_sum",
    )(*loads)


def inverse_of_factor(gram, wide_ref):
    rank = gram.shape[0]
    row = lax.broadcasted_iota(jnp.int32, (rank, rank), 0)
    col = lax.broadcasted_iota(jnp.int32, (rank, rank), 1)
    a = jnp.concatenate([gram, jnp.where(row == col, 1.0, 0.0).astype(F32)], axis=1)
    group = 4
    for k in range(0, rank, group):
        cols = [jnp.broadcast_to(a[:, k + j : k + j + 1], a.shape) for j in range(group)]
        rows = [a[k + j : k + j + 1, :] for j in range(group)]
        for j in range(group):
            pivot = cols[j][k + j : k + j + 1, :]
            wide_ref[k + j : k + j + 1, :] = rows[j] * lax.rsqrt(pivot)
            factor = cols[j] * (1.0 / pivot)
            for m in range(j + 1, group):
                cols[m] = cols[m] - factor * cols[m][k + j : k + j + 1, :]
                rows[m] = rows[m] - factor[k + m : k + m + 1, :] * rows[j]
            a = a - factor * rows[j]
    return wide_ref[:, rank:]


def inverse_kernel(n_exp, *refs):
    load_hbms, lt_hbm = refs[:n_exp], refs[n_exp]
    w_ref, basis_ref, terms_ref, lt_ref, wide_ref, sems = refs[n_exp + 1 :]
    rank = lt_ref.shape[0]
    half = rank // 2
    copies = [
        pltpu.make_async_copy(load_hbms[k].at[0 : 3 * half], terms_ref.at[k], sems.at[k])
        for k in range(n_exp)
    ]
    lt_copy = pltpu.make_async_copy(lt_hbm, lt_ref, sems.at[n_exp])
    for copy in copies:
        copy.start()
    lt_copy.start()
    for copy in copies:
        copy.wait()
    place = lax.axis_index("exp")
    packed = None
    for j in range(n_exp):
        terms = terms_ref[lax.rem(place + n_exp - j, n_exp)].astype(F32)
        part = terms[:half] + terms[half : 2 * half] + terms[2 * half :]
        packed = part if packed is None else packed + part
    w = inverse_of_factor(jnp.concatenate([packed[:, :rank], packed[:, rank:]], axis=0), wide_ref)
    w_ref[...] = w
    lt_copy.wait()
    basis_ref[...] = left_times(w, lt_ref[...], (((1,), (0,)), ((), ()))).T.astype(BF16)


def inverse_factor(loads, lt):
    rank, rows = lt.shape
    n_exp = len(loads)
    return pl.pallas_call(
        functools.partial(inverse_kernel, n_exp),
        in_specs=[ANY] * n_exp + [HBM],
        out_shape=[pltpu.HBM((rank, rank), F32), pltpu.HBM((rows, rank), BF16)],
        scratch_shapes=[
            pltpu.VMEM((n_exp, 3 * (rank // 2), 2 * rank), BF16),
            pltpu.VMEM((rank, rows), BF16),
            pltpu.VMEM((rank, 2 * rank), F32),
            pltpu.SemaphoreType.DMA((n_exp + 1,)),
        ],
        compiler_params=params(8),
        cost_estimate=pl.CostEstimate(flops=4_000_000_000, bytes_accessed=1000, transcendentals=0),
        name="inverse_factor",
    )(*loads, *in_hbm(lt))


def finish_kernel(
    replicas, w_any, chunk_ref, basis_any, merged_ref, right_hbm, err_hbm, w_ref, basis_ref, right_ref, err_ref, sems
):
    rank, cols = right_ref.shape
    rows, block = err_ref.shape[0], 128
    w_copy = pltpu.make_async_copy(w_any, w_ref, sems.at[rows // block + 1])
    w_copy.start()
    basis_copy = pltpu.make_async_copy(basis_any, basis_ref, sems.at[rows // block + 2])
    basis_copy.start()
    across = cols // TILE_C
    pieces = []
    for a in range(rank // TILE_R):
        pieces.append(jnp.concatenate([chunk_ref[a * across + b] for b in range(across)], axis=1))
    product = jnp.concatenate(pieces, axis=0)
    w_copy.wait()
    new_right = left_times(w_ref[...], product, (((1,), (0,)), ((), ()))) * (1.0 / replicas)
    right_ref[...] = new_right
    copies = [pltpu.make_async_copy(right_ref, right_hbm, sems.at[0])]
    copies[0].start()
    rounded = new_right.astype(BF16)
    basis_copy.wait()
    for i in range(rows // block):
        here = slice(i * block, (i + 1) * block)
        approx = jnp.dot(basis_ref[here, :], rounded, preferred_element_type=F32)
        err_ref[here, :] = (merged_ref[here, :].astype(F32) - approx).astype(BF16)
        copies.append(
            pltpu.make_async_copy(err_ref.at[here, :], err_hbm.at[0, here, :], sems.at[i + 1])
        )
        copies[-1].start()
    for copy in copies:
        copy.wait()


def finish(replicas, w, chunks, basis, merged):
    rows, rank = basis.shape
    cols = merged.shape[1]
    return pl.pallas_call(
        functools.partial(finish_kernel, replicas),
        in_specs=[HBM, VMEM, HBM, VMEM],
        out_specs=[HBM] * 2,
        out_shape=[
            jax.ShapeDtypeStruct((rank, cols), F32),
            jax.ShapeDtypeStruct((1, rows, cols), BF16),
        ],
        scratch_shapes=[
            pltpu.VMEM((rank, rank), F32),
            pltpu.VMEM((rows, rank), BF16),
            pltpu.VMEM((rank, cols), F32),
            pltpu.VMEM((rows, cols), BF16),
            pltpu.SemaphoreType.DMA((rows // 128 + 3,)),
        ],
        compiler_params=params(16),
        cost_estimate=SMALL,
        name="finish",
    )(*in_hbm(w), chunks, *in_hbm(basis), merged)


def expert_kernel(n_exp, n_grad, chunk, *refs):
    load_hbms, grad_hbms = refs[:n_exp], refs[n_exp : n_exp + n_grad]
    one_hbm, two_hbm, first_hbm, second_hbm, step_hbm = refs[n_exp + n_grad : n_exp + n_grad + 5]
    hid, rows, one, two, first, second, step, in_sems, out_sems = refs[n_exp + n_grad + 5 :]
    units, width = one.shape
    count = width // chunk

    slabs = [
        pltpu.make_async_copy(load_hbms[k], hid.at[k], in_sems.at[count, k])
        for k in range(n_exp)
    ]

    def loads(c):
        here = slice(c * chunk, (c + 1) * chunk)
        pairs, at = [], 0
        for grad_hbm in grad_hbms:
            end = at + grad_hbm.shape[1]
            pairs.append((grad_hbm.at[0, :, here], rows.at[at:end, here]))
            at = end
        pairs += [(one_hbm.at[0, :, here], one.at[:, here]), (two_hbm.at[0, :, here], two.at[:, here])]
        return [pltpu.make_async_copy(a, b, in_sems.at[c, i]) for i, (a, b) in enumerate(pairs)]

    def stores(c):
        here = slice(c * chunk, (c + 1) * chunk)
        pairs = [(first, first_hbm), (second, second_hbm), (step, step_hbm)]
        return [
            pltpu.make_async_copy(a.at[:, here], b.at[0, :, here], out_sems.at[c, i])
            for i, (a, b) in enumerate(pairs)
        ]

    for copy in slabs:
        copy.start()
    for c in range(count):
        for copy in loads(c):
            copy.start()
    for copy in slabs:
        copy.wait()
    left = jnp.concatenate([hid[k] for k in range(n_exp)], axis=1)
    for c in range(count):
        here = slice(c * chunk, (c + 1) * chunk)
        for copy in loads(c):
            copy.wait()
        grad = jnp.dot(left, rows[:, here], preferred_element_type=F32)
        first_new = beta_one * one[:, here] + (1.0 - beta_one) * grad
        second_new = beta_two * two[:, here] + (1.0 - beta_two) * grad * grad
        first[:, here] = first_new
        second[:, here] = second_new
        scaled = second_new * (1.0 / correction_two)
        bottom = scaled * lax.rsqrt(scaled) + epsilon
        step[:, here] = (
            first_new * (1.0 / correction_one) * pl.reciprocal(bottom, approx=True)
        ).astype(BF16)
        for copy in stores(c):
            copy.start()
    for c in range(count):
        for copy in stores(c):
            copy.wait()


def expert_step(slabs, grads, moment_one, moment_two):
    _, units, width = moment_one.shape
    chunk = 512
    n_exp, n_grad = len(slabs), len(grads)
    tokens = slabs[0].shape[1]
    return pl.pallas_call(
        functools.partial(expert_kernel, n_exp, n_grad, chunk),
        in_specs=[ANY] * n_exp + [HBM] + [ANY] * (n_grad - 1) + [HBM] * 2,
        out_specs=[HBM] * 3,
        out_shape=[
            jax.ShapeDtypeStruct((1, units, width), F32),
            jax.ShapeDtypeStruct((1, units, width), F32),
            jax.ShapeDtypeStruct((1, units, width), BF16),
        ],
        scratch_shapes=[
            pltpu.VMEM((n_exp, units, tokens), BF16),
            pltpu.VMEM((n_exp * tokens, width), BF16),
            pltpu.VMEM((units, width), F32),
            pltpu.VMEM((units, width), F32),
            pltpu.VMEM((units, width), F32),
            pltpu.VMEM((units, width), F32),
            pltpu.VMEM((units, width), BF16),
            pltpu.SemaphoreType.DMA((width // chunk + 1, n_grad + 2)),
            pltpu.SemaphoreType.DMA((width // chunk, 3)),
        ],
        compiler_params=params(24),
        cost_estimate=SMALL,
        name="expert_step",
    )(
        *slabs, *in_hbm(grads[0]), *grads[1:], *in_hbm(moment_one, moment_two)
    )


def swap(x, axis, size, mask):
    return lax.ppermute(x, axis, [(i, i ^ mask) for i in range(size)])


def shift(x, size, k):
    return lax.ppermute(x, "exp", [(i, (i + k) % size) for i in range(size)])


def after(x, y):
    return lax.optimization_barrier((x, y))[0]


def body(n_rep, n_exp, activations, kv_grad, errors, right_factor, hidden, out_grad, moment_one, moment_two):
    grads = {0: out_grad, 1: shift(out_grad, n_exp, 1)}
    if n_exp > 2:
        grads[n_exp - 1] = shift(out_grad, n_exp, -1)
    merged, lt = merge(activations, kv_grad, errors, right_factor.T)

    lt = (lt + swap(lt, "rep", n_rep, 1)).astype(BF16)
    slabs = unit_slabs(after(hidden, lt), n_exp)
    bit = 2
    parts = [lt]
    while bit < n_rep:
        while len(parts) > 1:
            parts = [a.astype(F32) + b.astype(F32) for a, b in zip(parts[0::2], parts[1::2])]
        own = parts[0].astype(BF16)
        masks = [bit] if 2 * bit >= n_rep else [bit, 2 * bit, 3 * bit]
        parts = [own] + [swap(own, "rep", n_rep, m) for m in masks]
        bit *= len(parts)
    lt, gram, chunks = right_product(parts, merged)

    slabs = [slabs[0]] + [shift(after(slabs[k], lt), n_exp, k) for k in range(1, n_exp)]
    rows = chunks.shape[0] * TILE_R // n_rep
    shares = lax.all_to_all(chunks.reshape(n_rep, rows, TILE_C), "rep", 0, 0, tiled=True)
    shares, grads = lax.optimization_barrier((shares, grads))

    load = line_load(shares, gram)
    loads = [load] + [shift(load, n_exp, k) for k in range(1, n_exp)]
    loads, slabs = lax.optimization_barrier((loads, slabs))
    share = line_sum(loads, gram.shape[0], n_rep)
    w, basis = inverse_factor(loads, lt)
    chunks = lax.all_to_all(share, "rep", 0, 0, tiled=True).reshape(chunks.shape)

    left, right = 1, n_exp - 1
    while right - left > 1:
        if left <= n_exp - right:
            grads[left + 1] = shift(after(grads[left], share), n_exp, 1)
            left += 1
        else:
            grads[right - 1] = shift(after(grads[right], share), n_exp, -1)
            right -= 1

    new_right, new_error = finish(n_rep, w, chunks, basis, merged)
    first_new, second_new, step = expert_step(
        slabs, [grads[k] for k in range(n_exp)], moment_one, moment_two
    )
    return new_error, new_right.T, first_new, second_new, step


def solution(mesh):
    placed = (
        P("rep", "exp"),
        P("rep", None),
        P("rep", "exp", None),
        P(),
        P("rep", "exp", None),
        P("rep", "exp", None),
        P("rep", "exp", None),
        P("rep", "exp", None),
    )
    return jax.shard_map(
        functools.partial(body, mesh.shape["rep"], mesh.shape["exp"]),
        mesh=mesh,
        in_specs=placed,
        out_specs=(
            P("rep", "exp", None),
            P(),
            P("rep", "exp", None),
            P("rep", "exp", None),
            P("rep", "exp", None),
        ),
        check_vma=False,
    )
```

```python
import functools

import jax
import jax.numpy as jnp
from jax import lax
from jax.experimental import pallas as pl
from jax.experimental.pallas import tpu as pltpu
from jax.sharding import PartitionSpec as P

HIGHEST = lax.Precision.HIGHEST
F32 = jnp.float32
BF16 = jnp.bfloat16
beta_one = 0.9
beta_two = 0.99
correction_one = 1.0 - 0.9**10
correction_two = 1.0 - 0.99**10
epsilon = 1e-08

ROWS_FIRST = (((0,), (0,)), ((), ()))
COLS_LAST = (((1,), (1,)), ((), ()))
TILE_R, TILE_C = 16, 128
HBM = pl.BlockSpec(memory_space=pltpu.HBM)
ANY = pl.BlockSpec(memory_space=pl.ANY)
VMEM = pl.BlockSpec(memory_space=pltpu.VMEM)


def params(mebibytes):
    return pltpu.CompilerParams(vmem_limit_bytes=mebibytes * 1024 * 1024)


def in_hbm(*arrays):
    return [pltpu.with_memory_space_constraint(x, pltpu.HBM) for x in arrays]


SMALL = pl.CostEstimate(flops=1000, bytes_accessed=1000, transcendentals=0)


def split_two(x):
    hi = x.astype(BF16)
    return hi, (x - hi.astype(F32)).astype(BF16)


def left_times(left, right_bf16, dims):
    rows = left.shape[0]
    hi, lo = split_two(left)
    both = jnp.concatenate([hi, lo], axis=0)
    out = lax.dot_general(both, right_bf16, dims, preferred_element_type=F32)
    return out[:rows] + out[rows:]


def merge_kernel(acts_ref, kv_ref, err_ref, vt_ref, merged_ref, lt_ref):
    merged = lax.dot_general(acts_ref[...], kv_ref[...], ROWS_FIRST, preferred_element_type=F32)
    merged = (merged + err_ref[0].astype(F32)).astype(BF16)
    merged_ref[...] = merged
    lt_ref[...] = left_times(vt_ref[...], merged, COLS_LAST)


def merge(acts, kv, err, vt):
    tokens, rows = acts.shape
    cols = kv.shape[1]
    rank = vt.shape[0]
    block = 256
    return pl.pallas_call(
        merge_kernel,
        grid=(rows // block,),
        in_specs=[
            pl.BlockSpec((tokens, block), lambda i: (0, i)),
            pl.BlockSpec((tokens, cols), lambda i: (0, 0)),
            pl.BlockSpec((1, block, cols), lambda i: (0, i, 0)),
            pl.BlockSpec((rank, cols), lambda i: (0, 0)),
        ],
        out_specs=[
            pl.BlockSpec((block, cols), lambda i: (i, 0)),
            pl.BlockSpec((rank, block), lambda i: (0, i)),
        ],
        out_shape=[
            jax.ShapeDtypeStruct((rows, cols), BF16),
            jax.ShapeDtypeStruct((rank, rows), F32),
        ],
        compiler_params=params(24),
        cost_estimate=pl.CostEstimate(flops=4_000_000_000, bytes_accessed=8_000_000, transcendentals=0),
        name="merge",
    )(*[pltpu.with_memory_space_constraint(x, pltpu.HBM) for x in (acts, kv, err, vt)])


def pack_kernel(hidden_hbm, gram_hbm, *refs):
    load_refs, (hidden_ref, gram_ref, all_ref, sems) = refs[:-4], refs[-4:]
    n_exp, units = all_ref.shape[:2]
    terms = gram_ref.shape[0]
    copies = [
        pltpu.make_async_copy(hidden_hbm, hidden_ref, sems.at[0]),
        pltpu.make_async_copy(gram_hbm, gram_ref, sems.at[1]),
    ]
    for copy in copies:
        copy.start()
    for copy in copies:
        copy.wait()
    all_ref[...] = hidden_ref[0].T.reshape(all_ref.shape)
    place = lax.axis_index("exp")
    for k, ref in enumerate(load_refs):
        ref[0:terms] = gram_ref[...]
        ref[terms : terms + units] = all_ref[lax.rem(place + k, n_exp)]


def pack(hidden, gram, n_exp):
    _, tokens, units = hidden.shape
    slab = (units // n_exp, tokens)
    load = (gram.shape[0] + slab[0], tokens)
    return pl.pallas_call(
        pack_kernel,
        in_specs=[HBM] * 2,
        out_shape=[pltpu.HBM(load, BF16)] + [jax.ShapeDtypeStruct(load, BF16)] * (n_exp - 1),
        scratch_shapes=[
            pltpu.VMEM(hidden.shape, BF16),
            pltpu.VMEM(gram.shape, BF16),
            pltpu.VMEM((n_exp,) + slab, BF16),
            pltpu.SemaphoreType.DMA((2,)),
        ],
        compiler_params=params(8),
        cost_estimate=SMALL,
        name="pack",
    )(*in_hbm(hidden, gram))


def right_kernel(n_parts, *refs):
    part_refs, merged_ref = refs[:n_parts], refs[n_parts]
    lt_ref, gram_ref, chunk_ref = refs[n_parts + 1 :]
    parts = [ref[...].astype(F32) for ref in part_refs]
    while len(parts) > 1:
        parts = [a + b for a, b in zip(parts[0::2], parts[1::2])]
    lt = parts[0]
    rank = lt.shape[0]
    lt_ref[...] = lt.astype(BF16)
    gram = lax.dot_general(lt, lt, COLS_LAST, precision=HIGHEST, preferred_element_type=F32)
    half = rank // 2
    packed = jnp.concatenate([gram[:half], gram[half:]], axis=1)
    high = packed.astype(BF16)
    rest = packed - high.astype(F32)
    middle = rest.astype(BF16)
    low = (rest - middle.astype(F32)).astype(BF16)
    gram_ref[0:half] = high
    gram_ref[half : 2 * half] = middle
    gram_ref[2 * half : 3 * half] = low
    product = left_times(lt, merged_ref[...], (((1,), (0,)), ((), ()))).astype(BF16)
    across = product.shape[1] // TILE_C
    for a in range(rank // TILE_R):
        for b in range(across):
            chunk_ref[a * across + b] = product[
                a * TILE_R : (a + 1) * TILE_R, b * TILE_C : (b + 1) * TILE_C
            ]


def right_product(parts, merged):
    rank, rows = parts[0].shape
    cols = merged.shape[1]
    chunks = rank * cols // (TILE_R * TILE_C)
    return pl.pallas_call(
        functools.partial(right_kernel, len(parts)),
        out_shape=[
            pltpu.HBM((rank, rows), BF16),
            pltpu.HBM((3 * (rank // 2), 2 * rank), BF16),
            jax.ShapeDtypeStruct((chunks, TILE_R, TILE_C), BF16),
        ],
        compiler_params=params(16),
        cost_estimate=SMALL,
        name="right_product",
    )(*parts, merged)


def sum_kernel(share_ref, out_ref):
    total = share_ref[0].astype(F32)
    for i in range(1, share_ref.shape[0]):
        total = total + share_ref[i].astype(F32)
    out_ref[...] = total.astype(BF16)


def replica_sum(shares):
    return pl.pallas_call(
        sum_kernel,
        out_shape=jax.ShapeDtypeStruct(shares.shape[1:], BF16),
        compiler_params=params(4),
        cost_estimate=SMALL,
        name="replica_sum",
    )(shares)


def line_kernel(*refs):
    load_refs, out_ref, parts_ref = refs[:-2], refs[-2], refs[-1]
    n_exp = len(load_refs)
    for k in range(n_exp):
        parts_ref[k] = load_refs[k][...].astype(F32)
    place = lax.axis_index("exp")
    total = None
    for j in range(n_exp):
        part = parts_ref[lax.rem(place + n_exp - j, n_exp)]
        total = part if total is None else total + part
    total = total.astype(BF16)
    for i in range(out_ref.shape[0]):
        out_ref[i] = total


def line_sum(loads, n_rep):
    return pl.pallas_call(
        line_kernel,
        out_shape=jax.ShapeDtypeStruct((n_rep,) + loads[0].shape, BF16),
        scratch_shapes=[pltpu.VMEM((len(loads),) + loads[0].shape, F32)],
        compiler_params=params(4),
        cost_estimate=SMALL,
        name="line_sum",
    )(*loads)


def inverse_of_factor(gram, wide_ref):
    rank = gram.shape[0]
    row = lax.broadcasted_iota(jnp.int32, (rank, rank), 0)
    col = lax.broadcasted_iota(jnp.int32, (rank, rank), 1)
    a = jnp.concatenate([gram, jnp.where(row == col, 1.0, 0.0).astype(F32)], axis=1)
    group = 4
    for k in range(0, rank, group):
        cols = [jnp.broadcast_to(a[:, k + j : k + j + 1], a.shape) for j in range(group)]
        rows = [a[k + j : k + j + 1, :] for j in range(group)]
        for j in range(group):
            pivot = cols[j][k + j : k + j + 1, :]
            wide_ref[k + j : k + j + 1, :] = rows[j] * lax.rsqrt(pivot)
            factor = cols[j] * (1.0 / pivot)
            for m in range(j + 1, group):
                cols[m] = cols[m] - factor * cols[m][k + j : k + j + 1, :]
                rows[m] = rows[m] - factor[k + m : k + m + 1, :] * rows[j]
            a = a - factor * rows[j]
    return wide_ref[:, rank:]


def inverse_kernel(n_exp, *refs):
    load_hbms, lt_hbm = refs[:n_exp], refs[n_exp]
    w_ref, basis_ref, terms_ref, lt_ref, wide_ref, sems = refs[n_exp + 1 :]
    rank = lt_ref.shape[0]
    half = rank // 2
    copies = [
        pltpu.make_async_copy(load_hbms[k].at[0 : 3 * half], terms_ref.at[k], sems.at[k])
        for k in range(n_exp)
    ]
    lt_copy = pltpu.make_async_copy(lt_hbm, lt_ref, sems.at[n_exp])
    for copy in copies:
        copy.start()
    lt_copy.start()
    for copy in copies:
        copy.wait()
    place = lax.axis_index("exp")
    packed = None
    for j in range(n_exp):
        terms = terms_ref[lax.rem(place + n_exp - j, n_exp)].astype(F32)
        part = terms[:half] + terms[half : 2 * half] + terms[2 * half :]
        packed = part if packed is None else packed + part
    w = inverse_of_factor(jnp.concatenate([packed[:, :rank], packed[:, rank:]], axis=0), wide_ref)
    w_ref[...] = w
    lt_copy.wait()
    basis_ref[...] = left_times(w, lt_ref[...], (((1,), (0,)), ((), ()))).T.astype(BF16)


def inverse_factor(loads, lt):
    rank, rows = lt.shape
    n_exp = len(loads)
    return pl.pallas_call(
        functools.partial(inverse_kernel, n_exp),
        in_specs=[HBM] + [ANY] * (n_exp - 1) + [HBM],
        out_shape=[pltpu.HBM((rank, rank), F32), pltpu.HBM((rows, rank), BF16)],
        scratch_shapes=[
            pltpu.VMEM((n_exp, 3 * (rank // 2), 2 * rank), BF16),
            pltpu.VMEM((rank, rows), BF16),
            pltpu.VMEM((rank, 2 * rank), F32),
            pltpu.SemaphoreType.DMA((n_exp + 1,)),
        ],
        compiler_params=params(8),
        cost_estimate=pl.CostEstimate(flops=4_000_000_000, bytes_accessed=1000, transcendentals=0),
        name="inverse_factor",
    )(*in_hbm(loads[0]), *loads[1:], *in_hbm(lt))


def finish_kernel(
    replicas, w_any, chunk_ref, basis_any, merged_ref, right_hbm, err_hbm, w_ref, basis_ref, right_ref, err_ref, sems
):
    rank, cols = right_ref.shape
    rows, block = err_ref.shape[0], 128
    w_copy = pltpu.make_async_copy(w_any, w_ref, sems.at[rows // block + 1])
    w_copy.start()
    basis_copy = pltpu.make_async_copy(basis_any, basis_ref, sems.at[rows // block + 2])
    basis_copy.start()
    across = cols // TILE_C
    pieces = []
    for a in range(rank // TILE_R):
        pieces.append(jnp.concatenate([chunk_ref[a * across + b] for b in range(across)], axis=1))
    product = jnp.concatenate(pieces, axis=0)
    w_copy.wait()
    new_right = left_times(w_ref[...], product, (((1,), (0,)), ((), ()))) * (1.0 / replicas)
    right_ref[...] = new_right
    copies = [pltpu.make_async_copy(right_ref, right_hbm, sems.at[0])]
    copies[0].start()
    rounded = new_right.astype(BF16)
    basis_copy.wait()
    for i in range(rows // block):
        here = slice(i * block, (i + 1) * block)
        approx = jnp.dot(basis_ref[here, :], rounded, preferred_element_type=F32)
        err_ref[here, :] = (merged_ref[here, :].astype(F32) - approx).astype(BF16)
        copies.append(
            pltpu.make_async_copy(err_ref.at[here, :], err_hbm.at[0, here, :], sems.at[i + 1])
        )
        copies[-1].start()
    for copy in copies:
        copy.wait()


def finish(replicas, w, chunks, basis, merged):
    rows, rank = basis.shape
    cols = merged.shape[1]
    return pl.pallas_call(
        functools.partial(finish_kernel, replicas),
        in_specs=[HBM, VMEM, HBM, VMEM],
        out_specs=[HBM] * 2,
        out_shape=[
            jax.ShapeDtypeStruct((rank, cols), F32),
            jax.ShapeDtypeStruct((1, rows, cols), BF16),
        ],
        scratch_shapes=[
            pltpu.VMEM((rank, rank), F32),
            pltpu.VMEM((rows, rank), BF16),
            pltpu.VMEM((rank, cols), F32),
            pltpu.VMEM((rows, cols), BF16),
            pltpu.SemaphoreType.DMA((rows // 128 + 3,)),
        ],
        compiler_params=params(16),
        cost_estimate=SMALL,
        name="finish",
    )(*in_hbm(w), chunks, *in_hbm(basis), merged)


def expert_kernel(n_exp, n_grad, chunk, *refs):
    load_hbms, grad_hbms = refs[:n_exp], refs[n_exp : n_exp + n_grad]
    one_hbm, two_hbm, first_hbm, second_hbm, step_hbm = refs[n_exp + n_grad : n_exp + n_grad + 5]
    hid, rows, one, two, first, second, step, in_sems, out_sems = refs[n_exp + n_grad + 5 :]
    units, width = one.shape
    count = width // chunk
    terms = load_hbms[0].shape[0] - units

    slabs = [
        pltpu.make_async_copy(load_hbms[k].at[terms : terms + units], hid.at[k], in_sems.at[count, k])
        for k in range(n_exp)
    ]

    def loads(c):
        here = slice(c * chunk, (c + 1) * chunk)
        pairs, at = [], 0
        for grad_hbm in grad_hbms:
            end = at + grad_hbm.shape[1]
            pairs.append((grad_hbm.at[0, :, here], rows.at[at:end, here]))
            at = end
        pairs += [(one_hbm.at[0, :, here], one.at[:, here]), (two_hbm.at[0, :, here], two.at[:, here])]
        return [pltpu.make_async_copy(a, b, in_sems.at[c, i]) for i, (a, b) in enumerate(pairs)]

    def stores(c):
        here = slice(c * chunk, (c + 1) * chunk)
        pairs = [(first, first_hbm), (second, second_hbm), (step, step_hbm)]
        return [
            pltpu.make_async_copy(a.at[:, here], b.at[0, :, here], out_sems.at[c, i])
            for i, (a, b) in enumerate(pairs)
        ]

    for copy in slabs:
        copy.start()
    for c in range(count):
        for copy in loads(c):
            copy.start()
    for copy in slabs:
        copy.wait()
    left = jnp.concatenate([hid[k] for k in range(n_exp)], axis=1)
    for c in range(count):
        here = slice(c * chunk, (c + 1) * chunk)
        for copy in loads(c):
            copy.wait()
        grad = jnp.dot(left, rows[:, here], preferred_element_type=F32)
        first_new = beta_one * one[:, here] + (1.0 - beta_one) * grad
        second_new = beta_two * two[:, here] + (1.0 - beta_two) * grad * grad
        first[:, here] = first_new
        second[:, here] = second_new
        scaled = second_new * (1.0 / correction_two)
        bottom = scaled * lax.rsqrt(scaled) + epsilon
        step[:, here] = (
            first_new * (1.0 / correction_one) * pl.reciprocal(bottom, approx=True)
        ).astype(BF16)
        for copy in stores(c):
            copy.start()
    for c in range(count):
        for copy in stores(c):
            copy.wait()


def expert_step(slabs, grads, moment_one, moment_two):
    _, units, width = moment_one.shape
    chunk = 512
    n_exp, n_grad = len(slabs), len(grads)
    tokens = slabs[0].shape[1]
    return pl.pallas_call(
        functools.partial(expert_kernel, n_exp, n_grad, chunk),
        in_specs=[HBM] + [ANY] * (n_exp - 1) + [HBM] + [ANY] * (n_grad - 1) + [HBM] * 2,
        out_specs=[HBM] * 3,
        out_shape=[
            jax.ShapeDtypeStruct((1, units, width), F32),
            jax.ShapeDtypeStruct((1, units, width), F32),
            jax.ShapeDtypeStruct((1, units, width), BF16),
        ],
        scratch_shapes=[
            pltpu.VMEM((n_exp, units, tokens), BF16),
            pltpu.VMEM((n_exp * tokens, width), BF16),
            pltpu.VMEM((units, width), F32),
            pltpu.VMEM((units, width), F32),
            pltpu.VMEM((units, width), F32),
            pltpu.VMEM((units, width), F32),
            pltpu.VMEM((units, width), BF16),
            pltpu.SemaphoreType.DMA((width // chunk + 1, n_grad + 2)),
            pltpu.SemaphoreType.DMA((width // chunk, 3)),
        ],
        compiler_params=params(24),
        cost_estimate=SMALL,
        name="expert_step",
    )(
        *in_hbm(slabs[0]), *slabs[1:], *in_hbm(grads[0]), *grads[1:], *in_hbm(moment_one, moment_two)
    )


def swap(x, axis, size, mask):
    return lax.ppermute(x, axis, [(i, i ^ mask) for i in range(size)])


def shift(x, size, k):
    return lax.ppermute(x, "exp", [(i, (i + k) % size) for i in range(size)])


def after(x, y):
    return lax.optimization_barrier((x, y))[0]


def body(n_rep, n_exp, activations, kv_grad, errors, right_factor, hidden, out_grad, moment_one, moment_two):
    grads = {0: out_grad, 1: shift(out_grad, n_exp, 1)}
    if n_exp > 2:
        grads[n_exp - 1] = shift(out_grad, n_exp, -1)
    merged, lt = merge(activations, kv_grad, errors, right_factor.T)

    lt = (lt + swap(lt, "rep", n_rep, 1)).astype(BF16)
    bit = 2
    parts = [lt]
    while bit < n_rep:
        while len(parts) > 1:
            parts = [a.astype(F32) + b.astype(F32) for a, b in zip(parts[0::2], parts[1::2])]
        own = parts[0].astype(BF16)
        masks = [bit] if 2 * bit >= n_rep else [bit, 2 * bit, 3 * bit]
        parts = [own] + [swap(own, "rep", n_rep, m) for m in masks]
        bit *= len(parts)
    lt, gram, chunks = right_product(parts, merged)

    slabs = pack(hidden, gram, n_exp)
    slabs = [slabs[0]] + [shift(slabs[k], n_exp, k) for k in range(1, n_exp)]

    rows = chunks.shape[0] * TILE_R // n_rep
    load = replica_sum(lax.all_to_all(chunks.reshape(n_rep, rows, TILE_C), "rep", 0, 0, tiled=True))
    loads = [load] + [shift(load, n_exp, k) for k in range(1, n_exp)]
    w, basis = inverse_factor(slabs, lt)
    loads, grads = lax.optimization_barrier((loads, grads))
    share = line_sum(loads, n_rep)
    share, w, basis = lax.optimization_barrier((share, w, basis))
    chunks = lax.all_to_all(share, "rep", 0, 0, tiled=True).reshape(chunks.shape)

    left, right = 1, n_exp - 1
    while right - left > 1:
        if left <= n_exp - right:
            grads[left + 1] = shift(after(grads[left], share), n_exp, 1)
            left += 1
        else:
            grads[right - 1] = shift(after(grads[right], share), n_exp, -1)
            right -= 1

    new_right, new_error = finish(n_rep, w, chunks, basis, merged)
    first_new, second_new, step = expert_step(
        slabs, [grads[k] for k in range(n_exp)], moment_one, moment_two
    )
    return new_error, new_right.T, first_new, second_new, step


def solution(mesh):
    placed = (
        P("rep", "exp"),
        P("rep", None),
        P("rep", "exp", None),
        P(),
        P("rep", "exp", None),
        P("rep", "exp", None),
        P("rep", "exp", None),
        P("rep", "exp", None),
    )
    return jax.shard_map(
        functools.partial(body, mesh.shape["rep"], mesh.shape["exp"]),
        mesh=mesh,
        in_specs=placed,
        out_specs=(
            P("rep", "exp", None),
            P(),
            P("rep", "exp", None),
            P("rep", "exp", None),
            P("rep", "exp", None),
        ),
        check_vma=False,
    )
```

```python
import functools

import jax
import jax.numpy as jnp
from jax import lax
from jax.experimental import pallas as pl
from jax.experimental.pallas import tpu as pltpu
from jax.sharding import PartitionSpec as P

HIGHEST = lax.Precision.HIGHEST
F32 = jnp.float32
BF16 = jnp.bfloat16
beta_one = 0.9
beta_two = 0.99
correction_one = 1.0 - 0.9**10
correction_two = 1.0 - 0.99**10
epsilon = 1e-08

ROWS_FIRST = (((0,), (0,)), ((), ()))
COLS_LAST = (((1,), (1,)), ((), ()))
TILE_R, TILE_C = 16, 128
HBM = pl.BlockSpec(memory_space=pltpu.HBM)
ANY = pl.BlockSpec(memory_space=pl.ANY)
VMEM = pl.BlockSpec(memory_space=pltpu.VMEM)


def params(mebibytes):
    return pltpu.CompilerParams(vmem_limit_bytes=mebibytes * 1024 * 1024)


def in_hbm(*arrays):
    return [pltpu.with_memory_space_constraint(x, pltpu.HBM) for x in arrays]


SMALL = pl.CostEstimate(flops=1000, bytes_accessed=1000, transcendentals=0)


def split_two(x):
    hi = x.astype(BF16)
    return hi, (x - hi.astype(F32)).astype(BF16)


def left_times(left, right_bf16, dims):
    rows = left.shape[0]
    hi, lo = split_two(left)
    both = jnp.concatenate([hi, lo], axis=0)
    out = lax.dot_general(both, right_bf16, dims, preferred_element_type=F32)
    return out[:rows] + out[rows:]


def merge_kernel(acts_ref, kv_ref, err_ref, vt_ref, merged_ref, lt_ref):
    merged = lax.dot_general(acts_ref[...], kv_ref[...], ROWS_FIRST, preferred_element_type=F32)
    merged = (merged + err_ref[0].astype(F32)).astype(BF16)
    merged_ref[...] = merged
    lt_ref[...] = left_times(vt_ref[...], merged, COLS_LAST)


def merge(acts, kv, err, vt):
    tokens, rows = acts.shape
    cols = kv.shape[1]
    rank = vt.shape[0]
    block = 256
    return pl.pallas_call(
        merge_kernel,
        grid=(rows // block,),
        in_specs=[
            pl.BlockSpec((tokens, block), lambda i: (0, i)),
            pl.BlockSpec((tokens, cols), lambda i: (0, 0)),
            pl.BlockSpec((1, block, cols), lambda i: (0, i, 0)),
            pl.BlockSpec((rank, cols), lambda i: (0, 0)),
        ],
        out_specs=[
            pl.BlockSpec((block, cols), lambda i: (i, 0)),
            pl.BlockSpec((rank, block), lambda i: (0, i)),
        ],
        out_shape=[
            jax.ShapeDtypeStruct((rows, cols), BF16),
            jax.ShapeDtypeStruct((rank, rows), F32),
        ],
        compiler_params=params(24),
        cost_estimate=pl.CostEstimate(flops=4_000_000_000, bytes_accessed=8_000_000, transcendentals=0),
        name="merge",
    )(*[pltpu.with_memory_space_constraint(x, pltpu.HBM) for x in (acts, kv, err, vt)])


def slab_kernel(hidden_ref, own_ref, *refs):
    send_refs, all_ref = refs[:-1], refs[-1]
    n_exp = all_ref.shape[0]
    all_ref[...] = hidden_ref[0].T.reshape(all_ref.shape)
    place = lax.axis_index("exp")
    for k, ref in enumerate((own_ref,) + tuple(send_refs)):
        ref[...] = all_ref[lax.rem(place + k, n_exp)]


def unit_slabs(hidden, n_exp):
    _, tokens, units = hidden.shape
    slab = (units // n_exp, tokens)
    return pl.pallas_call(
        slab_kernel,
        out_shape=[pltpu.HBM(slab, BF16)] * n_exp,
        scratch_shapes=[pltpu.VMEM((n_exp,) + slab, BF16)],
        compiler_params=params(8),
        cost_estimate=SMALL,
        name="unit_slabs",
    )(hidden)


def right_kernel(n_parts, *refs):
    part_refs, merged_ref = refs[:n_parts], refs[n_parts]
    lt_ref, gram_ref, chunk_ref = refs[n_parts + 1 :]
    parts = [ref[...].astype(F32) for ref in part_refs]
    while len(parts) > 1:
        parts = [a + b for a, b in zip(parts[0::2], parts[1::2])]
    lt = parts[0]
    rank = lt.shape[0]
    lt_ref[...] = lt.astype(BF16)
    gram = lax.dot_general(lt, lt, COLS_LAST, precision=HIGHEST, preferred_element_type=F32)
    half = rank // 2
    packed = jnp.concatenate([gram[:half], gram[half:]], axis=1)
    high = packed.astype(BF16)
    rest = packed - high.astype(F32)
    middle = rest.astype(BF16)
    low = (rest - middle.astype(F32)).astype(BF16)
    gram_ref[0:half] = high
    gram_ref[half : 2 * half] = middle
    gram_ref[2 * half : 3 * half] = low
    product = left_times(lt, merged_ref[...], (((1,), (0,)), ((), ()))).astype(BF16)
    across = product.shape[1] // TILE_C
    for a in range(rank // TILE_R):
        for b in range(across):
            chunk_ref[a * across + b] = product[
                a * TILE_R : (a + 1) * TILE_R, b * TILE_C : (b + 1) * TILE_C
            ]


def right_product(parts, merged):
    rank, rows = parts[0].shape
    cols = merged.shape[1]
    chunks = rank * cols // (TILE_R * TILE_C)
    return pl.pallas_call(
        functools.partial(right_kernel, len(parts)),
        out_shape=[
            pltpu.HBM((rank, rows), BF16),
            pltpu.HBM((3 * (rank // 2), 2 * rank), BF16),
            jax.ShapeDtypeStruct((chunks, TILE_R, TILE_C), BF16),
        ],
        compiler_params=params(16),
        cost_estimate=SMALL,
        name="right_product",
    )(*parts, merged)


def load_kernel(share_ref, gram_hbm, load_ref, gram_ref, sem):
    terms = gram_ref.shape[0]
    copy = pltpu.make_async_copy(gram_hbm, gram_ref, sem)
    copy.start()
    total = share_ref[0].astype(F32)
    for i in range(1, share_ref.shape[0]):
        total = total + share_ref[i].astype(F32)
    load_ref[terms:] = total.astype(BF16)
    copy.wait()
    load_ref[0:terms] = gram_ref[...]


def line_load(shares, gram):
    return pl.pallas_call(
        load_kernel,
        in_specs=[VMEM, HBM],
        out_shape=jax.ShapeDtypeStruct((gram.shape[0] + shares.shape[1], TILE_C), BF16),
        scratch_shapes=[pltpu.VMEM(gram.shape, BF16), pltpu.SemaphoreType.DMA],
        compiler_params=params(4),
        cost_estimate=SMALL,
        name="line_load",
    )(shares, *in_hbm(gram))


def line_kernel(terms, *refs):
    load_refs, (out_ref, gram_ref, parts_ref) = refs[:-3], refs[-3:]
    n_exp = len(load_refs)
    for k in range(n_exp):
        parts_ref[k] = load_refs[k][...].astype(F32)
    place = lax.axis_index("exp")
    half = terms // 3
    total = packed = None
    for j in range(n_exp):
        which = lax.rem(place + n_exp - j, n_exp)
        part = parts_ref[which, terms:]
        total = part if total is None else total + part
        gram = parts_ref[which, 0:half] + parts_ref[which, half : 2 * half]
        gram = gram + parts_ref[which, 2 * half : terms]
        packed = gram if packed is None else packed + gram
    total = total.astype(BF16)
    for i in range(out_ref.shape[0]):
        out_ref[i] = total
    gram_ref[0:half] = packed[:, : gram_ref.shape[1]]
    gram_ref[half:] = packed[:, gram_ref.shape[1] :]


def line_sum(loads, terms, n_rep):
    rows = loads[0].shape[0] - terms
    rank = 2 * (terms // 3)
    return pl.pallas_call(
        functools.partial(line_kernel, terms),
        out_shape=[
            jax.ShapeDtypeStruct((n_rep, rows, TILE_C), BF16),
            pltpu.HBM((rank, rank), F32),
        ],
        scratch_shapes=[pltpu.VMEM((len(loads),) + loads[0].shape, F32)],
        compiler_params=params(4),
        cost_estimate=SMALL,
        name="line_sum",
    )(*loads)


def inverse_of_factor(gram, wide_ref):
    rank = gram.shape[0]
    row = lax.broadcasted_iota(jnp.int32, (rank, rank), 0)
    col = lax.broadcasted_iota(jnp.int32, (rank, rank), 1)
    a = jnp.concatenate([gram, jnp.where(row == col, 1.0, 0.0).astype(F32)], axis=1)
    group = 4
    for k in range(0, rank, group):
        cols = [jnp.broadcast_to(a[:, k + j : k + j + 1], a.shape) for j in range(group)]
        rows = [a[k + j : k + j + 1, :] for j in range(group)]
        for j in range(group):
            pivot = cols[j][k + j : k + j + 1, :]
            wide_ref[k + j : k + j + 1, :] = rows[j] * lax.rsqrt(pivot)
            factor = cols[j] * (1.0 / pivot)
            for m in range(j + 1, group):
                cols[m] = cols[m] - factor * cols[m][k + j : k + j + 1, :]
                rows[m] = rows[m] - factor[k + m : k + m + 1, :] * rows[j]
            a = a - factor * rows[j]
    return wide_ref[:, rank:]


def inverse_kernel(gram_any, lt_any, w_ref, basis_ref, gram_ref, lt_ref, wide_ref, sems):
    gram_copy = pltpu.make_async_copy(gram_any, gram_ref, sems.at[0])
    gram_copy.start()
    lt_copy = pltpu.make_async_copy(lt_any, lt_ref, sems.at[1])
    lt_copy.start()
    gram_copy.wait()
    w = inverse_of_factor(gram_ref[...], wide_ref)
    w_ref[...] = w
    lt_copy.wait()
    basis_ref[...] = left_times(w, lt_ref[...], (((1,), (0,)), ((), ()))).T.astype(BF16)


def inverse_factor(gram, lt):
    rank, rows = lt.shape
    return pl.pallas_call(
        inverse_kernel,
        in_specs=[ANY] * 2,
        out_shape=[pltpu.HBM((rank, rank), F32), pltpu.HBM((rows, rank), BF16)],
        scratch_shapes=[
            pltpu.VMEM((rank, rank), F32),
            pltpu.VMEM((rank, rows), BF16),
            pltpu.VMEM((rank, 2 * rank), F32),
            pltpu.SemaphoreType.DMA((2,)),
        ],
        compiler_params=params(8),
        cost_estimate=pl.CostEstimate(flops=4_000_000_000, bytes_accessed=1000, transcendentals=0),
        name="inverse_factor",
    )(*in_hbm(gram, lt))


def finish_kernel(
    replicas, w_any, chunk_ref, basis_any, merged_ref, right_hbm, err_hbm, w_ref, basis_ref, right_ref, err_ref, sems
):
    rank, cols = right_ref.shape
    rows, block = err_ref.shape[0], 128
    w_copy = pltpu.make_async_copy(w_any, w_ref, sems.at[rows // block + 1])
    w_copy.start()
    basis_copy = pltpu.make_async_copy(basis_any, basis_ref, sems.at[rows // block + 2])
    basis_copy.start()
    across = cols // TILE_C
    pieces = []
    for a in range(rank // TILE_R):
        pieces.append(jnp.concatenate([chunk_ref[a * across + b] for b in range(across)], axis=1))
    product = jnp.concatenate(pieces, axis=0)
    w_copy.wait()
    new_right = left_times(w_ref[...], product, (((1,), (0,)), ((), ()))) * (1.0 / replicas)
    right_ref[...] = new_right
    copies = [pltpu.make_async_copy(right_ref, right_hbm, sems.at[0])]
    copies[0].start()
    rounded = new_right.astype(BF16)
    basis_copy.wait()
    for i in range(rows // block):
        here = slice(i * block, (i + 1) * block)
        approx = jnp.dot(basis_ref[here, :], rounded, preferred_element_type=F32)
        err_ref[here, :] = (merged_ref[here, :].astype(F32) - approx).astype(BF16)
        copies.append(
            pltpu.make_async_copy(err_ref.at[here, :], err_hbm.at[0, here, :], sems.at[i + 1])
        )
        copies[-1].start()
    for copy in copies:
        copy.wait()


def finish(replicas, w, chunks, basis, merged):
    rows, rank = basis.shape
    cols = merged.shape[1]
    return pl.pallas_call(
        functools.partial(finish_kernel, replicas),
        in_specs=[HBM, VMEM, HBM, VMEM],
        out_specs=[HBM] * 2,
        out_shape=[
            jax.ShapeDtypeStruct((rank, cols), F32),
            jax.ShapeDtypeStruct((1, rows, cols), BF16),
        ],
        scratch_shapes=[
            pltpu.VMEM((rank, rank), F32),
            pltpu.VMEM((rows, rank), BF16),
            pltpu.VMEM((rank, cols), F32),
            pltpu.VMEM((rows, cols), BF16),
            pltpu.SemaphoreType.DMA((rows // 128 + 3,)),
        ],
        compiler_params=params(16),
        cost_estimate=SMALL,
        name="finish",
    )(*in_hbm(w), chunks, *in_hbm(basis), merged)


def expert_kernel(n_exp, n_grad, chunk, *refs):
    load_hbms, grad_hbms = refs[:n_exp], refs[n_exp : n_exp + n_grad]
    one_hbm, two_hbm, first_hbm, second_hbm, step_hbm = refs[n_exp + n_grad : n_exp + n_grad + 5]
    hid, rows, one, two, first, second, step, in_sems, out_sems = refs[n_exp + n_grad + 5 :]
    units, width = one.shape
    count = width // chunk

    slabs = [
        pltpu.make_async_copy(load_hbms[k], hid.at[k], in_sems.at[count, k])
        for k in range(n_exp)
    ]

    def loads(c):
        here = slice(c * chunk, (c + 1) * chunk)
        pairs, at = [], 0
        for grad_hbm in grad_hbms:
            end = at + grad_hbm.shape[1]
            pairs.append((grad_hbm.at[0, :, here], rows.at[at:end, here]))
            at = end
        pairs += [(one_hbm.at[0, :, here], one.at[:, here]), (two_hbm.at[0, :, here], two.at[:, here])]
        return [pltpu.make_async_copy(a, b, in_sems.at[c, i]) for i, (a, b) in enumerate(pairs)]

    def stores(c):
        here = slice(c * chunk, (c + 1) * chunk)
        pairs = [(first, first_hbm), (second, second_hbm), (step, step_hbm)]
        return [
            pltpu.make_async_copy(a.at[:, here], b.at[0, :, here], out_sems.at[c, i])
            for i, (a, b) in enumerate(pairs)
        ]

    for copy in slabs:
        copy.start()
    for c in range(count):
        for copy in loads(c):
            copy.start()
    for copy in slabs:
        copy.wait()
    left = jnp.concatenate([hid[k] for k in range(n_exp)], axis=1)
    for c in range(count):
        here = slice(c * chunk, (c + 1) * chunk)
        for copy in loads(c):
            copy.wait()
        grad = jnp.dot(left, rows[:, here], preferred_element_type=F32)
        first_new = beta_one * one[:, here] + (1.0 - beta_one) * grad
        second_new = beta_two * two[:, here] + (1.0 - beta_two) * grad * grad
        first[:, here] = first_new
        second[:, here] = second_new
        scaled = second_new * (1.0 / correction_two)
        bottom = scaled * lax.rsqrt(scaled) + epsilon
        step[:, here] = (
            first_new * (1.0 / correction_one) * pl.reciprocal(bottom, approx=True)
        ).astype(BF16)
        for copy in stores(c):
            copy.start()
    for c in range(count):
        for copy in stores(c):
            copy.wait()


def expert_step(slabs, grads, moment_one, moment_two):
    _, units, width = moment_one.shape
    chunk = 512
    n_exp, n_grad = len(slabs), len(grads)
    tokens = slabs[0].shape[1]
    return pl.pallas_call(
        functools.partial(expert_kernel, n_exp, n_grad, chunk),
        in_specs=[ANY] * n_exp + [HBM] + [ANY] * (n_grad - 1) + [HBM] * 2,
        out_specs=[HBM] * 3,
        out_shape=[
            jax.ShapeDtypeStruct((1, units, width), F32),
            jax.ShapeDtypeStruct((1, units, width), F32),
            jax.ShapeDtypeStruct((1, units, width), BF16),
        ],
        scratch_shapes=[
            pltpu.VMEM((n_exp, units, tokens), BF16),
            pltpu.VMEM((n_exp * tokens, width), BF16),
            pltpu.VMEM((units, width), F32),
            pltpu.VMEM((units, width), F32),
            pltpu.VMEM((units, width), F32),
            pltpu.VMEM((units, width), F32),
            pltpu.VMEM((units, width), BF16),
            pltpu.SemaphoreType.DMA((width // chunk + 1, n_grad + 2)),
            pltpu.SemaphoreType.DMA((width // chunk, 3)),
        ],
        compiler_params=params(24),
        cost_estimate=SMALL,
        name="expert_step",
    )(
        *slabs, *in_hbm(grads[0]), *grads[1:], *in_hbm(moment_one, moment_two)
    )


def swap(x, axis, size, mask):
    return lax.ppermute(x, axis, [(i, i ^ mask) for i in range(size)])


def shift(x, size, k):
    return lax.ppermute(x, "exp", [(i, (i + k) % size) for i in range(size)])


def after(x, y):
    return lax.optimization_barrier((x, y))[0]


def body(n_rep, n_exp, activations, kv_grad, errors, right_factor, hidden, out_grad, moment_one, moment_two):
    grads = {0: out_grad, 1: shift(out_grad, n_exp, 1)}
    if n_exp > 2:
        grads[n_exp - 1] = shift(out_grad, n_exp, -1)
    merged, lt = merge(activations, kv_grad, errors, right_factor.T)

    lt = (lt + swap(lt, "rep", n_rep, 1)).astype(BF16)
    slabs = unit_slabs(after(hidden, lt), n_exp)
    bit = 2
    parts = [lt]
    while bit < n_rep:
        while len(parts) > 1:
            parts = [a.astype(F32) + b.astype(F32) for a, b in zip(parts[0::2], parts[1::2])]
        own = parts[0].astype(BF16)
        masks = [bit] if 2 * bit >= n_rep else [bit, 2 * bit, 3 * bit]
        parts = [own] + [swap(own, "rep", n_rep, m) for m in masks]
        bit *= len(parts)
    lt, gram, chunks = right_product(parts, merged)

    slabs = [slabs[0]] + [shift(after(slabs[k], lt), n_exp, k) for k in range(1, n_exp)]
    rows = chunks.shape[0] * TILE_R // n_rep
    shares = lax.all_to_all(chunks.reshape(n_rep, rows, TILE_C), "rep", 0, 0, tiled=True)

    load = line_load(shares, gram)
    loads = [load] + [shift(load, n_exp, k) for k in range(1, n_exp)]
    loads, slabs, grads = lax.optimization_barrier((loads, slabs, grads))
    share, gram = line_sum(loads, gram.shape[0], n_rep)
    w, basis = inverse_factor(gram, lt)
    chunks = lax.all_to_all(share, "rep", 0, 0, tiled=True).reshape(chunks.shape)

    left, right = 1, n_exp - 1
    while right - left > 1:
        if left <= n_exp - right:
            grads[left + 1] = shift(after(grads[left], share), n_exp, 1)
            left += 1
        else:
            grads[right - 1] = shift(after(grads[right], share), n_exp, -1)
            right -= 1

    new_right, new_error = finish(n_rep, w, chunks, basis, merged)
    first_new, second_new, step = expert_step(
        slabs, [grads[k] for k in range(n_exp)], moment_one, moment_two
    )
    return new_error, new_right.T, first_new, second_new, step


def solution(mesh):
    placed = (
        P("rep", "exp"),
        P("rep", None),
        P("rep", "exp", None),
        P(),
        P("rep", "exp", None),
        P("rep", "exp", None),
        P("rep", "exp", None),
        P("rep", "exp", None),
    )
    return jax.shard_map(
        functools.partial(body, mesh.shape["rep"], mesh.shape["exp"]),
        mesh=mesh,
        in_specs=placed,
        out_specs=(
            P("rep", "exp", None),
            P(),
            P("rep", "exp", None),
            P("rep", "exp", None),
            P("rep", "exp", None),
        ),
        check_vma=False,
    )
```

```python
import functools

import jax
import jax.numpy as jnp
from jax import lax
from jax.experimental import pallas as pl
from jax.experimental.pallas import tpu as pltpu
from jax.sharding import PartitionSpec as P

HIGHEST = lax.Precision.HIGHEST
F32 = jnp.float32
BF16 = jnp.bfloat16
beta_one = 0.9
beta_two = 0.99
correction_one = 1.0 - 0.9**10
correction_two = 1.0 - 0.99**10
epsilon = 1e-08

ROWS_FIRST = (((0,), (0,)), ((), ()))
COLS_LAST = (((1,), (1,)), ((), ()))
TILE_R, TILE_C = 16, 128
HBM = pl.BlockSpec(memory_space=pltpu.HBM)
ANY = pl.BlockSpec(memory_space=pl.ANY)
VMEM = pl.BlockSpec(memory_space=pltpu.VMEM)


def params(mebibytes):
    return pltpu.CompilerParams(vmem_limit_bytes=mebibytes * 1024 * 1024)


def in_hbm(*arrays):
    return [pltpu.with_memory_space_constraint(x, pltpu.HBM) for x in arrays]


SMALL = pl.CostEstimate(flops=1000, bytes_accessed=1000, transcendentals=0)


def split_two(x):
    hi = x.astype(BF16)
    return hi, (x - hi.astype(F32)).astype(BF16)


def left_times(left, right_bf16, dims):
    rows = left.shape[0]
    hi, lo = split_two(left)
    both = jnp.concatenate([hi, lo], axis=0)
    out = lax.dot_general(both, right_bf16, dims, preferred_element_type=F32)
    return out[:rows] + out[rows:]


def merge_kernel(acts_ref, kv_ref, err_ref, vt_ref, merged_ref, lt_ref):
    merged = lax.dot_general(acts_ref[...], kv_ref[...], ROWS_FIRST, preferred_element_type=F32)
    merged = (merged + err_ref[0].astype(F32)).astype(BF16)
    merged_ref[...] = merged
    lt_ref[...] = left_times(vt_ref[...], merged, COLS_LAST)


def merge(acts, kv, err, vt):
    tokens, rows = acts.shape
    cols = kv.shape[1]
    rank = vt.shape[0]
    block = 256
    return pl.pallas_call(
        merge_kernel,
        grid=(rows // block,),
        in_specs=[
            pl.BlockSpec((tokens, block), lambda i: (0, i)),
            pl.BlockSpec((tokens, cols), lambda i: (0, 0)),
            pl.BlockSpec((1, block, cols), lambda i: (0, i, 0)),
            pl.BlockSpec((rank, cols), lambda i: (0, 0)),
        ],
        out_specs=[
            pl.BlockSpec((block, cols), lambda i: (i, 0)),
            pl.BlockSpec((rank, block), lambda i: (0, i)),
        ],
        out_shape=[
            jax.ShapeDtypeStruct((rows, cols), BF16),
            jax.ShapeDtypeStruct((rank, rows), F32),
        ],
        compiler_params=params(24),
        cost_estimate=pl.CostEstimate(flops=4_000_000_000, bytes_accessed=8_000_000, transcendentals=0),
        name="merge",
    )(*[pltpu.with_memory_space_constraint(x, pltpu.HBM) for x in (acts, kv, err, vt)])


def slab_kernel(hidden_ref, own_ref, *refs):
    send_refs, all_ref = refs[:-1], refs[-1]
    n_exp = all_ref.shape[0]
    all_ref[...] = hidden_ref[0].T.reshape(all_ref.shape)
    place = lax.axis_index("exp")
    for k, ref in enumerate((own_ref,) + tuple(send_refs)):
        ref[...] = all_ref[lax.rem(place + k, n_exp)]


def unit_slabs(hidden, n_exp):
    _, tokens, units = hidden.shape
    slab = (units // n_exp, tokens)
    return pl.pallas_call(
        slab_kernel,
        out_shape=[pltpu.HBM(slab, BF16)] * n_exp,
        scratch_shapes=[pltpu.VMEM((n_exp,) + slab, BF16)],
        compiler_params=params(8),
        cost_estimate=SMALL,
        name="unit_slabs",
    )(hidden)


def right_kernel(n_parts, *refs):
    part_refs, merged_ref = refs[:n_parts], refs[n_parts]
    lt_ref, gram_ref, chunk_ref = refs[n_parts + 1 :]
    parts = [ref[...].astype(F32) for ref in part_refs]
    while len(parts) > 1:
        parts = [a + b for a, b in zip(parts[0::2], parts[1::2])]
    lt = parts[0]
    rank = lt.shape[0]
    lt_ref[...] = lt.astype(BF16)
    gram = lax.dot_general(lt, lt, COLS_LAST, precision=HIGHEST, preferred_element_type=F32)
    half = rank // 2
    packed = jnp.concatenate([gram[:half], gram[half:]], axis=1)
    high = packed.astype(BF16)
    rest = packed - high.astype(F32)
    middle = rest.astype(BF16)
    low = (rest - middle.astype(F32)).astype(BF16)
    gram_ref[0:half] = high
    gram_ref[half : 2 * half] = middle
    gram_ref[2 * half : 3 * half] = low
    product = left_times(lt, merged_ref[...], (((1,), (0,)), ((), ()))).astype(BF16)
    across = product.shape[1] // TILE_C
    for a in range(rank // TILE_R):
        for b in range(across):
            chunk_ref[a * across + b] = product[
                a * TILE_R : (a + 1) * TILE_R, b * TILE_C : (b + 1) * TILE_C
            ]


def right_product(parts, merged):
    rank, rows = parts[0].shape
    cols = merged.shape[1]
    chunks = rank * cols // (TILE_R * TILE_C)
    return pl.pallas_call(
        functools.partial(right_kernel, len(parts)),
        out_shape=[
            pltpu.HBM((rank, rows), BF16),
            pltpu.HBM((3 * (rank // 2), 2 * rank), BF16),
            jax.ShapeDtypeStruct((chunks, TILE_R, TILE_C), BF16),
        ],
        compiler_params=params(16),
        cost_estimate=SMALL,
        name="right_product",
    )(*parts, merged)


def load_kernel(share_ref, gram_hbm, load_ref, gram_ref, sem):
    terms = gram_ref.shape[0]
    copy = pltpu.make_async_copy(gram_hbm, gram_ref, sem)
    copy.start()
    total = share_ref[0].astype(F32)
    for i in range(1, share_ref.shape[0]):
        total = total + share_ref[i].astype(F32)
    load_ref[terms:] = total.astype(BF16)
    copy.wait()
    load_ref[0:terms] = gram_ref[...]


def line_load(shares, gram):
    return pl.pallas_call(
        load_kernel,
        in_specs=[VMEM, HBM],
        out_shape=jax.ShapeDtypeStruct((gram.shape[0] + shares.shape[1], TILE_C), BF16),
        scratch_shapes=[pltpu.VMEM(gram.shape, BF16), pltpu.SemaphoreType.DMA],
        compiler_params=params(4),
        cost_estimate=SMALL,
        name="line_load",
    )(shares, *in_hbm(gram))


def line_kernel(terms, *refs):
    load_refs, (out_ref, gram_ref, parts_ref) = refs[:-3], refs[-3:]
    n_exp = len(load_refs)
    for k in range(n_exp):
        parts_ref[k] = load_refs[k][...].astype(F32)
    place = lax.axis_index("exp")
    half = terms // 3
    total = packed = None
    for j in range(n_exp):
        which = lax.rem(place + n_exp - j, n_exp)
        part = parts_ref[which, terms:]
        total = part if total is None else total + part
        gram = parts_ref[which, 0:half] + parts_ref[which, half : 2 * half]
        gram = gram + parts_ref[which, 2 * half : terms]
        packed = gram if packed is None else packed + gram
    total = total.astype(BF16)
    for i in range(out_ref.shape[0]):
        out_ref[i] = total
    gram_ref[0:half] = packed[:, : gram_ref.shape[1]]
    gram_ref[half:] = packed[:, gram_ref.shape[1] :]


def line_sum(loads, terms, n_rep):
    rows = loads[0].shape[0] - terms
    rank = 2 * (terms // 3)
    return pl.pallas_call(
        functools.partial(line_kernel, terms),
        out_shape=[
            jax.ShapeDtypeStruct((n_rep, rows, TILE_C), BF16),
            pltpu.HBM((rank, rank), F32),
        ],
        scratch_shapes=[pltpu.VMEM((len(loads),) + loads[0].shape, F32)],
        compiler_params=params(4),
        cost_estimate=SMALL,
        name="line_sum",
    )(*loads)


def inverse_of_factor(gram, wide_ref):
    rank = gram.shape[0]
    row = lax.broadcasted_iota(jnp.int32, (rank, rank), 0)
    col = lax.broadcasted_iota(jnp.int32, (rank, rank), 1)
    a = jnp.concatenate([gram, jnp.where(row == col, 1.0, 0.0).astype(F32)], axis=1)
    group = 4
    for k in range(0, rank, group):
        cols = [jnp.broadcast_to(a[:, k + j : k + j + 1], a.shape) for j in range(group)]
        rows = [a[k + j : k + j + 1, :] for j in range(group)]
        for j in range(group):
            pivot = cols[j][k + j : k + j + 1, :]
            wide_ref[k + j : k + j + 1, :] = rows[j] * lax.rsqrt(pivot)
            factor = cols[j] * (1.0 / pivot)
            for m in range(j + 1, group):
                cols[m] = cols[m] - factor * cols[m][k + j : k + j + 1, :]
                rows[m] = rows[m] - factor[k + m : k + m + 1, :] * rows[j]
            a = a - factor * rows[j]
    return wide_ref[:, rank:]


def inverse_kernel(gram_any, lt_any, w_ref, basis_ref, gram_ref, lt_ref, wide_ref, sems):
    gram_copy = pltpu.make_async_copy(gram_any, gram_ref, sems.at[0])
    gram_copy.start()
    lt_copy = pltpu.make_async_copy(lt_any, lt_ref, sems.at[1])
    lt_copy.start()
    gram_copy.wait()
    w = inverse_of_factor(gram_ref[...], wide_ref)
    w_ref[...] = w
    lt_copy.wait()
    basis_ref[...] = left_times(w, lt_ref[...], (((1,), (0,)), ((), ()))).T.astype(BF16)


def inverse_factor(gram, lt):
    rank, rows = lt.shape
    return pl.pallas_call(
        inverse_kernel,
        in_specs=[ANY] * 2,
        out_shape=[pltpu.HBM((rank, rank), F32), pltpu.HBM((rows, rank), BF16)],
        scratch_shapes=[
            pltpu.VMEM((rank, rank), F32),
            pltpu.VMEM((rank, rows), BF16),
            pltpu.VMEM((rank, 2 * rank), F32),
            pltpu.SemaphoreType.DMA((2,)),
        ],
        compiler_params=params(8),
        cost_estimate=pl.CostEstimate(flops=4_000_000_000, bytes_accessed=1000, transcendentals=0),
        name="inverse_factor",
    )(*in_hbm(gram, lt))


def finish_kernel(
    replicas, w_any, chunk_ref, basis_any, merged_ref, right_hbm, err_hbm, w_ref, basis_ref, right_ref, err_ref, sems
):
    rank, cols = right_ref.shape
    rows, block = err_ref.shape[0], 128
    w_copy = pltpu.make_async_copy(w_any, w_ref, sems.at[rows // block + 1])
    w_copy.start()
    basis_copy = pltpu.make_async_copy(basis_any, basis_ref, sems.at[rows // block + 2])
    basis_copy.start()
    across = cols // TILE_C
    pieces = []
    for a in range(rank // TILE_R):
        pieces.append(jnp.concatenate([chunk_ref[a * across + b] for b in range(across)], axis=1))
    product = jnp.concatenate(pieces, axis=0)
    w_copy.wait()
    new_right = left_times(w_ref[...], product, (((1,), (0,)), ((), ()))) * (1.0 / replicas)
    right_ref[...] = new_right
    copies = [pltpu.make_async_copy(right_ref, right_hbm, sems.at[0])]
    copies[0].start()
    rounded = new_right.astype(BF16)
    basis_copy.wait()
    for i in range(rows // block):
        here = slice(i * block, (i + 1) * block)
        approx = jnp.dot(basis_ref[here, :], rounded, preferred_element_type=F32)
        err_ref[here, :] = (merged_ref[here, :].astype(F32) - approx).astype(BF16)
        copies.append(
            pltpu.make_async_copy(err_ref.at[here, :], err_hbm.at[0, here, :], sems.at[i + 1])
        )
        copies[-1].start()
    for copy in copies:
        copy.wait()


def finish(replicas, w, chunks, basis, merged):
    rows, rank = basis.shape
    cols = merged.shape[1]
    return pl.pallas_call(
        functools.partial(finish_kernel, replicas),
        in_specs=[HBM, VMEM, HBM, VMEM],
        out_specs=[HBM] * 2,
        out_shape=[
            jax.ShapeDtypeStruct((rank, cols), F32),
            jax.ShapeDtypeStruct((1, rows, cols), BF16),
        ],
        scratch_shapes=[
            pltpu.VMEM((rank, rank), F32),
            pltpu.VMEM((rows, rank), BF16),
            pltpu.VMEM((rank, cols), F32),
            pltpu.VMEM((rows, cols), BF16),
            pltpu.SemaphoreType.DMA((rows // 128 + 3,)),
        ],
        compiler_params=params(16),
        cost_estimate=SMALL,
        name="finish",
    )(*in_hbm(w), chunks, *in_hbm(basis), merged)


def expert_kernel(n_exp, n_grad, chunk, *refs):
    load_hbms, grad_hbms = refs[:n_exp], refs[n_exp : n_exp + n_grad]
    one_hbm, two_hbm, first_hbm, second_hbm, step_hbm = refs[n_exp + n_grad : n_exp + n_grad + 5]
    hid, rows, one, two, first, second, step, in_sems, out_sems = refs[n_exp + n_grad + 5 :]
    units, width = one.shape
    count = width // chunk

    slabs = [
        pltpu.make_async_copy(load_hbms[k], hid.at[k], in_sems.at[count, k])
        for k in range(n_exp)
    ]

    def loads(c):
        here = slice(c * chunk, (c + 1) * chunk)
        pairs, at = [], 0
        for grad_hbm in grad_hbms:
            end = at + grad_hbm.shape[1]
            pairs.append((grad_hbm.at[0, :, here], rows.at[at:end, here]))
            at = end
        pairs += [(one_hbm.at[0, :, here], one.at[:, here]), (two_hbm.at[0, :, here], two.at[:, here])]
        return [pltpu.make_async_copy(a, b, in_sems.at[c, i]) for i, (a, b) in enumerate(pairs)]

    def stores(c):
        here = slice(c * chunk, (c + 1) * chunk)
        pairs = [(first, first_hbm), (second, second_hbm), (step, step_hbm)]
        return [
            pltpu.make_async_copy(a.at[:, here], b.at[0, :, here], out_sems.at[c, i])
            for i, (a, b) in enumerate(pairs)
        ]

    for copy in slabs:
        copy.start()
    for c in range(count):
        for copy in loads(c):
            copy.start()
    for copy in slabs:
        copy.wait()
    left = jnp.concatenate([hid[k] for k in range(n_exp)], axis=1)
    for c in range(count):
        here = slice(c * chunk, (c + 1) * chunk)
        for copy in loads(c):
            copy.wait()
        grad = jnp.dot(left, rows[:, here], preferred_element_type=F32)
        first_new = beta_one * one[:, here] + (1.0 - beta_one) * grad
        second_new = beta_two * two[:, here] + (1.0 - beta_two) * grad * grad
        first[:, here] = first_new
        second[:, here] = second_new
        scaled = second_new * (1.0 / correction_two)
        bottom = scaled * lax.rsqrt(scaled) + epsilon
        step[:, here] = (
            first_new * (1.0 / correction_one) * pl.reciprocal(bottom, approx=True)
        ).astype(BF16)
        for copy in stores(c):
            copy.start()
    for c in range(count):
        for copy in stores(c):
            copy.wait()


def expert_step(slabs, grads, moment_one, moment_two):
    _, units, width = moment_one.shape
    chunk = 512
    n_exp, n_grad = len(slabs), len(grads)
    tokens = slabs[0].shape[1]
    return pl.pallas_call(
        functools.partial(expert_kernel, n_exp, n_grad, chunk),
        in_specs=[ANY] * n_exp + [HBM] + [ANY] * (n_grad - 1) + [HBM] * 2,
        out_specs=[HBM] * 3,
        out_shape=[
            jax.ShapeDtypeStruct((1, units, width), F32),
            jax.ShapeDtypeStruct((1, units, width), F32),
            jax.ShapeDtypeStruct((1, units, width), BF16),
        ],
        scratch_shapes=[
            pltpu.VMEM((n_exp, units, tokens), BF16),
            pltpu.VMEM((n_exp * tokens, width), BF16),
            pltpu.VMEM((units, width), F32),
            pltpu.VMEM((units, width), F32),
            pltpu.VMEM((units, width), F32),
            pltpu.VMEM((units, width), F32),
            pltpu.VMEM((units, width), BF16),
            pltpu.SemaphoreType.DMA((width // chunk + 1, n_grad + 2)),
            pltpu.SemaphoreType.DMA((width // chunk, 3)),
        ],
        compiler_params=params(24),
        cost_estimate=SMALL,
        name="expert_step",
    )(
        *slabs, *in_hbm(grads[0]), *grads[1:], *in_hbm(moment_one, moment_two)
    )


def swap(x, axis, size, mask):
    return lax.ppermute(x, axis, [(i, i ^ mask) for i in range(size)])


def shift(x, size, k):
    return lax.ppermute(x, "exp", [(i, (i + k) % size) for i in range(size)])


def after(x, y):
    return lax.optimization_barrier((x, y))[0]


def body(n_rep, n_exp, activations, kv_grad, errors, right_factor, hidden, out_grad, moment_one, moment_two):
    grads = {0: out_grad, 1: shift(out_grad, n_exp, 1)}
    if n_exp > 2:
        grads[n_exp - 1] = shift(out_grad, n_exp, -1)
    merged, lt = merge(activations, kv_grad, errors, right_factor.T)

    lt = (lt + swap(lt, "rep", n_rep, 1)).astype(BF16)
    slabs = unit_slabs(after(hidden, lt), n_exp)
    bit = 2
    parts = [lt]
    while bit < n_rep:
        while len(parts) > 1:
            parts = [a.astype(F32) + b.astype(F32) for a, b in zip(parts[0::2], parts[1::2])]
        own = parts[0].astype(BF16)
        masks = [bit] if 2 * bit >= n_rep else [bit, 2 * bit, 3 * bit]
        parts = [own] + [swap(own, "rep", n_rep, m) for m in masks]
        bit *= len(parts)
    lt, gram, chunks = right_product(parts, merged)

    slabs = [slabs[0]] + [shift(after(slabs[k], lt), n_exp, k) for k in range(1, n_exp)]
    rows = chunks.shape[0] * TILE_R // n_rep
    shares = lax.all_to_all(chunks.reshape(n_rep, rows, TILE_C), "rep", 0, 0, tiled=True)

    load = line_load(shares, gram)
    loads = [load] + [shift(load, n_exp, k) for k in range(1, n_exp)]
    loads, grads = lax.optimization_barrier((loads, grads))
    share, gram = line_sum(loads, gram.shape[0], n_rep)
    share, slabs = lax.optimization_barrier((share, slabs))
    w, basis = inverse_factor(gram, lt)
    chunks = lax.all_to_all(share, "rep", 0, 0, tiled=True).reshape(chunks.shape)

    left, right = 1, n_exp - 1
    while right - left > 1:
        if left <= n_exp - right:
            grads[left + 1] = shift(after(grads[left], share), n_exp, 1)
            left += 1
        else:
            grads[right - 1] = shift(after(grads[right], share), n_exp, -1)
            right -= 1

    new_right, new_error = finish(n_rep, w, chunks, basis, merged)
    first_new, second_new, step = expert_step(
        slabs, [grads[k] for k in range(n_exp)], moment_one, moment_two
    )
    return new_error, new_right.T, first_new, second_new, step


def solution(mesh):
    placed = (
        P("rep", "exp"),
        P("rep", None),
        P("rep", "exp", None),
        P(),
        P("rep", "exp", None),
        P("rep", "exp", None),
        P("rep", "exp", None),
        P("rep", "exp", None),
    )
    return jax.shard_map(
        functools.partial(body, mesh.shape["rep"], mesh.shape["exp"]),
        mesh=mesh,
        in_specs=placed,
        out_specs=(
            P("rep", "exp", None),
            P(),
            P("rep", "exp", None),
            P("rep", "exp", None),
            P("rep", "exp", None),
        ),
        check_vma=False,
    )
```

```python
import functools

import jax
import jax.numpy as jnp
from jax import lax
from jax.experimental import pallas as pl
from jax.experimental.pallas import tpu as pltpu
from jax.sharding import PartitionSpec as P

HIGHEST = lax.Precision.HIGHEST
F32 = jnp.float32
BF16 = jnp.bfloat16
beta_one = 0.9
beta_two = 0.99
correction_one = 1.0 - 0.9**10
correction_two = 1.0 - 0.99**10
epsilon = 1e-08

ROWS_FIRST = (((0,), (0,)), ((), ()))
COLS_LAST = (((1,), (1,)), ((), ()))
TILE_R, TILE_C = 16, 128
HBM = pl.BlockSpec(memory_space=pltpu.HBM)
ANY = pl.BlockSpec(memory_space=pl.ANY)
VMEM = pl.BlockSpec(memory_space=pltpu.VMEM)


def params(mebibytes):
    return pltpu.CompilerParams(vmem_limit_bytes=mebibytes * 1024 * 1024)


def in_hbm(*arrays):
    return [pltpu.with_memory_space_constraint(x, pltpu.HBM) for x in arrays]


SMALL = pl.CostEstimate(flops=1000, bytes_accessed=1000, transcendentals=0)


def split_two(x):
    hi = x.astype(BF16)
    return hi, (x - hi.astype(F32)).astype(BF16)


def left_times(left, right_bf16, dims):
    rows = left.shape[0]
    hi, lo = split_two(left)
    both = jnp.concatenate([hi, lo], axis=0)
    out = lax.dot_general(both, right_bf16, dims, preferred_element_type=F32)
    return out[:rows] + out[rows:]


def merge_kernel(acts_ref, kv_ref, err_ref, vt_ref, merged_ref, lt_ref):
    merged = lax.dot_general(acts_ref[...], kv_ref[...], ROWS_FIRST, preferred_element_type=F32)
    merged = (merged + err_ref[0].astype(F32)).astype(BF16)
    merged_ref[...] = merged
    lt_ref[...] = left_times(vt_ref[...], merged, COLS_LAST)


def merge(acts, kv, err, vt):
    tokens, rows = acts.shape
    cols = kv.shape[1]
    rank = vt.shape[0]
    block = 256
    return pl.pallas_call(
        merge_kernel,
        grid=(rows // block,),
        in_specs=[
            pl.BlockSpec((tokens, block), lambda i: (0, i)),
            pl.BlockSpec((tokens, cols), lambda i: (0, 0)),
            pl.BlockSpec((1, block, cols), lambda i: (0, i, 0)),
            pl.BlockSpec((rank, cols), lambda i: (0, 0)),
        ],
        out_specs=[
            pl.BlockSpec((block, cols), lambda i: (i, 0)),
            pl.BlockSpec((rank, block), lambda i: (0, i)),
        ],
        out_shape=[
            jax.ShapeDtypeStruct((rows, cols), BF16),
            jax.ShapeDtypeStruct((rank, rows), F32),
        ],
        compiler_params=params(24),
        cost_estimate=pl.CostEstimate(flops=4_000_000_000, bytes_accessed=8_000_000, transcendentals=0),
        name="merge",
    )(*[pltpu.with_memory_space_constraint(x, pltpu.HBM) for x in (acts, kv, err, vt)])


def slab_kernel(hidden_ref, own_ref, *refs):
    send_refs, all_ref = refs[:-1], refs[-1]
    n_exp = all_ref.shape[0]
    all_ref[...] = hidden_ref[0].T.reshape(all_ref.shape)
    place = lax.axis_index("exp")
    for k, ref in enumerate((own_ref,) + tuple(send_refs)):
        ref[...] = all_ref[lax.rem(place + k, n_exp)]


def unit_slabs(hidden, n_exp):
    _, tokens, units = hidden.shape
    slab = (units // n_exp, tokens)
    return pl.pallas_call(
        slab_kernel,
        out_shape=[pltpu.HBM(slab, BF16)] * n_exp,
        scratch_shapes=[pltpu.VMEM((n_exp,) + slab, BF16)],
        compiler_params=params(8),
        cost_estimate=SMALL,
        name="unit_slabs",
    )(hidden)


def right_kernel(n_parts, *refs):
    part_refs, merged_ref = refs[:n_parts], refs[n_parts]
    lt_ref, gram_ref, chunk_ref = refs[n_parts + 1 :]
    parts = [ref[...].astype(F32) for ref in part_refs]
    while len(parts) > 1:
        parts = [a + b for a, b in zip(parts[0::2], parts[1::2])]
    lt = parts[0]
    rank = lt.shape[0]
    lt_ref[...] = lt.astype(BF16)
    gram = lax.dot_general(lt, lt, COLS_LAST, precision=HIGHEST, preferred_element_type=F32)
    half = rank // 2
    packed = jnp.concatenate([gram[:half], gram[half:]], axis=1)
    high = packed.astype(BF16)
    rest = packed - high.astype(F32)
    middle = rest.astype(BF16)
    low = (rest - middle.astype(F32)).astype(BF16)
    gram_ref[0:half] = high
    gram_ref[half : 2 * half] = middle
    gram_ref[2 * half : 3 * half] = low
    product = left_times(lt, merged_ref[...], (((1,), (0,)), ((), ()))).astype(BF16)
    across = product.shape[1] // TILE_C
    for a in range(rank // TILE_R):
        for b in range(across):
            chunk_ref[a * across + b] = product[
                a * TILE_R : (a + 1) * TILE_R, b * TILE_C : (b + 1) * TILE_C
            ]


def right_product(parts, merged):
    rank, rows = parts[0].shape
    cols = merged.shape[1]
    chunks = rank * cols // (TILE_R * TILE_C)
    return pl.pallas_call(
        functools.partial(right_kernel, len(parts)),
        out_shape=[
            pltpu.HBM((rank, rows), BF16),
            pltpu.HBM((3 * (rank // 2), 2 * rank), BF16),
            jax.ShapeDtypeStruct((chunks, TILE_R, TILE_C), BF16),
        ],
        compiler_params=params(16),
        cost_estimate=SMALL,
        name="right_product",
    )(*parts, merged)


def load_kernel(share_ref, gram_hbm, load_ref, gram_ref, sem):
    terms = gram_ref.shape[0]
    copy = pltpu.make_async_copy(gram_hbm, gram_ref, sem)
    copy.start()
    total = share_ref[0].astype(F32)
    for i in range(1, share_ref.shape[0]):
        total = total + share_ref[i].astype(F32)
    load_ref[terms:] = total.astype(BF16)
    copy.wait()
    load_ref[0:terms] = gram_ref[...]


def line_load(shares, gram):
    return pl.pallas_call(
        load_kernel,
        in_specs=[VMEM, HBM],
        out_shape=jax.ShapeDtypeStruct((gram.shape[0] + shares.shape[1], TILE_C), BF16),
        scratch_shapes=[pltpu.VMEM(gram.shape, BF16), pltpu.SemaphoreType.DMA],
        compiler_params=params(4),
        cost_estimate=SMALL,
        name="line_load",
    )(shares, *in_hbm(gram))


def line_kernel(terms, *refs):
    load_refs, (out_ref, gram_ref, parts_ref) = refs[:-3], refs[-3:]
    n_exp = len(load_refs)
    for k in range(n_exp):
        parts_ref[k] = load_refs[k][...].astype(F32)
    place = lax.axis_index("exp")
    half = terms // 3
    total = packed = None
    for j in range(n_exp):
        which = lax.rem(place + n_exp - j, n_exp)
        part = parts_ref[which, terms:]
        total = part if total is None else total + part
        gram = parts_ref[which, 0:half] + parts_ref[which, half : 2 * half]
        gram = gram + parts_ref[which, 2 * half : terms]
        packed = gram if packed is None else packed + gram
    total = total.astype(BF16)
    for i in range(out_ref.shape[0]):
        out_ref[i] = total
    gram_ref[0:half] = packed[:, : gram_ref.shape[1]]
    gram_ref[half:] = packed[:, gram_ref.shape[1] :]


def line_sum(loads, terms, n_rep):
    rows = loads[0].shape[0] - terms
    rank = 2 * (terms // 3)
    return pl.pallas_call(
        functools.partial(line_kernel, terms),
        out_shape=[
            jax.ShapeDtypeStruct((n_rep, rows, TILE_C), BF16),
            pltpu.HBM((rank, rank), F32),
        ],
        scratch_shapes=[pltpu.VMEM((len(loads),) + loads[0].shape, F32)],
        compiler_params=params(4),
        cost_estimate=SMALL,
        name="line_sum",
    )(*loads)


def inverse_of_factor(gram, wide_ref):
    rank = gram.shape[0]
    row = lax.broadcasted_iota(jnp.int32, (rank, rank), 0)
    col = lax.broadcasted_iota(jnp.int32, (rank, rank), 1)
    a = jnp.concatenate([gram, jnp.where(row == col, 1.0, 0.0).astype(F32)], axis=1)
    group = 4
    for k in range(0, rank, group):
        cols = [jnp.broadcast_to(a[:, k + j : k + j + 1], a.shape) for j in range(group)]
        rows = [a[k + j : k + j + 1, :] for j in range(group)]
        for j in range(group):
            pivot = cols[j][k + j : k + j + 1, :]
            wide_ref[k + j : k + j + 1, :] = rows[j] * lax.rsqrt(pivot)
            factor = cols[j] * (1.0 / pivot)
            for m in range(j + 1, group):
                cols[m] = cols[m] - factor * cols[m][k + j : k + j + 1, :]
                rows[m] = rows[m] - factor[k + m : k + m + 1, :] * rows[j]
            a = a - factor * rows[j]
    return wide_ref[:, rank:]


def inverse_kernel(gram_any, lt_any, w_ref, basis_ref, gram_ref, lt_ref, wide_ref, sems):
    gram_copy = pltpu.make_async_copy(gram_any, gram_ref, sems.at[0])
    gram_copy.start()
    lt_copy = pltpu.make_async_copy(lt_any, lt_ref, sems.at[1])
    lt_copy.start()
    gram_copy.wait()
    w = inverse_of_factor(gram_ref[...], wide_ref)
    w_ref[...] = w
    lt_copy.wait()
    basis_ref[...] = left_times(w, lt_ref[...], (((1,), (0,)), ((), ()))).T.astype(BF16)


def inverse_factor(gram, lt):
    rank, rows = lt.shape
    return pl.pallas_call(
        inverse_kernel,
        in_specs=[ANY] * 2,
        out_shape=[pltpu.HBM((rank, rank), F32), pltpu.HBM((rows, rank), BF16)],
        scratch_shapes=[
            pltpu.VMEM((rank, rank), F32),
            pltpu.VMEM((rank, rows), BF16),
            pltpu.VMEM((rank, 2 * rank), F32),
            pltpu.SemaphoreType.DMA((2,)),
        ],
        compiler_params=params(8),
        cost_estimate=pl.CostEstimate(flops=4_000_000_000, bytes_accessed=1000, transcendentals=0),
        name="inverse_factor",
    )(*in_hbm(gram, lt))


def finish_kernel(
    replicas, w_any, chunk_ref, basis_any, merged_ref, right_hbm, err_hbm, w_ref, basis_ref, right_ref, err_ref, sems
):
    rank, cols = right_ref.shape
    rows, block = err_ref.shape[0], 128
    w_copy = pltpu.make_async_copy(w_any, w_ref, sems.at[rows // block + 1])
    w_copy.start()
    basis_copy = pltpu.make_async_copy(basis_any, basis_ref, sems.at[rows // block + 2])
    basis_copy.start()
    across = cols // TILE_C
    pieces = []
    for a in range(rank // TILE_R):
        pieces.append(jnp.concatenate([chunk_ref[a * across + b] for b in range(across)], axis=1))
    product = jnp.concatenate(pieces, axis=0)
    w_copy.wait()
    new_right = left_times(w_ref[...], product, (((1,), (0,)), ((), ()))) * (1.0 / replicas)
    right_ref[...] = new_right
    copies = [pltpu.make_async_copy(right_ref, right_hbm, sems.at[0])]
    copies[0].start()
    rounded = new_right.astype(BF16)
    basis_copy.wait()
    for i in range(rows // block):
        here = slice(i * block, (i + 1) * block)
        approx = jnp.dot(basis_ref[here, :], rounded, preferred_element_type=F32)
        err_ref[here, :] = (merged_ref[here, :].astype(F32) - approx).astype(BF16)
        copies.append(
            pltpu.make_async_copy(err_ref.at[here, :], err_hbm.at[0, here, :], sems.at[i + 1])
        )
        copies[-1].start()
    for copy in copies:
        copy.wait()


def finish(replicas, w, chunks, basis, merged):
    rows, rank = basis.shape
    cols = merged.shape[1]
    return pl.pallas_call(
        functools.partial(finish_kernel, replicas),
        in_specs=[HBM, VMEM, HBM, VMEM],
        out_specs=[HBM] * 2,
        out_shape=[
            jax.ShapeDtypeStruct((rank, cols), F32),
            jax.ShapeDtypeStruct((1, rows, cols), BF16),
        ],
        scratch_shapes=[
            pltpu.VMEM((rank, rank), F32),
            pltpu.VMEM((rows, rank), BF16),
            pltpu.VMEM((rank, cols), F32),
            pltpu.VMEM((rows, cols), BF16),
            pltpu.SemaphoreType.DMA((rows // 128 + 3,)),
        ],
        compiler_params=params(16),
        cost_estimate=SMALL,
        name="finish",
    )(*in_hbm(w), chunks, *in_hbm(basis), merged)


def expert_kernel(n_exp, n_grad, chunk, *refs):
    load_hbms, grad_hbms = refs[:n_exp], refs[n_exp : n_exp + n_grad]
    one_hbm, two_hbm, first_hbm, second_hbm, step_hbm = refs[n_exp + n_grad : n_exp + n_grad + 5]
    hid, rows, one, two, first, second, step, in_sems, out_sems = refs[n_exp + n_grad + 5 :]
    units, width = one.shape
    count = width // chunk

    slabs = [
        pltpu.make_async_copy(load_hbms[k], hid.at[k], in_sems.at[count, k])
        for k in range(n_exp)
    ]

    def loads(c):
        here = slice(c * chunk, (c + 1) * chunk)
        pairs, at = [], 0
        for grad_hbm in grad_hbms:
            end = at + grad_hbm.shape[1]
            pairs.append((grad_hbm.at[0, :, here], rows.at[at:end, here]))
            at = end
        pairs += [(one_hbm.at[0, :, here], one.at[:, here]), (two_hbm.at[0, :, here], two.at[:, here])]
        return [pltpu.make_async_copy(a, b, in_sems.at[c, i]) for i, (a, b) in enumerate(pairs)]

    def stores(c):
        here = slice(c * chunk, (c + 1) * chunk)
        pairs = [(first, first_hbm), (second, second_hbm), (step, step_hbm)]
        return [
            pltpu.make_async_copy(a.at[:, here], b.at[0, :, here], out_sems.at[c, i])
            for i, (a, b) in enumerate(pairs)
        ]

    for copy in slabs:
        copy.start()
    for c in range(count):
        for copy in loads(c):
            copy.start()
    for copy in slabs:
        copy.wait()
    left = jnp.concatenate([hid[k] for k in range(n_exp)], axis=1)
    for c in range(count):
        here = slice(c * chunk, (c + 1) * chunk)
        for copy in loads(c):
            copy.wait()
        grad = jnp.dot(left, rows[:, here], preferred_element_type=F32)
        first_new = beta_one * one[:, here] + (1.0 - beta_one) * grad
        second_new = beta_two * two[:, here] + (1.0 - beta_two) * grad * grad
        first[:, here] = first_new
        second[:, here] = second_new
        scaled = second_new * (1.0 / correction_two)
        bottom = scaled * lax.rsqrt(scaled) + epsilon
        step[:, here] = (
            first_new * (1.0 / correction_one) * pl.reciprocal(bottom, approx=True)
        ).astype(BF16)
        for copy in stores(c):
            copy.start()
    for c in range(count):
        for copy in stores(c):
            copy.wait()


def expert_step(slabs, grads, moment_one, moment_two):
    _, units, width = moment_one.shape
    chunk = 512
    n_exp, n_grad = len(slabs), len(grads)
    tokens = slabs[0].shape[1]
    return pl.pallas_call(
        functools.partial(expert_kernel, n_exp, n_grad, chunk),
        in_specs=[ANY] * n_exp + [HBM] + [ANY] * (n_grad - 1) + [HBM] * 2,
        out_specs=[HBM] * 3,
        out_shape=[
            jax.ShapeDtypeStruct((1, units, width), F32),
            jax.ShapeDtypeStruct((1, units, width), F32),
            jax.ShapeDtypeStruct((1, units, width), BF16),
        ],
        scratch_shapes=[
            pltpu.VMEM((n_exp, units, tokens), BF16),
            pltpu.VMEM((n_exp * tokens, width), BF16),
            pltpu.VMEM((units, width), F32),
            pltpu.VMEM((units, width), F32),
            pltpu.VMEM((units, width), F32),
            pltpu.VMEM((units, width), F32),
            pltpu.VMEM((units, width), BF16),
            pltpu.SemaphoreType.DMA((width // chunk + 1, n_grad + 2)),
            pltpu.SemaphoreType.DMA((width // chunk, 3)),
        ],
        compiler_params=params(24),
        cost_estimate=SMALL,
        name="expert_step",
    )(
        *slabs, *in_hbm(grads[0]), *grads[1:], *in_hbm(moment_one, moment_two)
    )


def swap(x, axis, size, mask):
    return lax.ppermute(x, axis, [(i, i ^ mask) for i in range(size)])


def shift(x, size, k):
    return lax.ppermute(x, "exp", [(i, (i + k) % size) for i in range(size)])


def after(x, y):
    return lax.optimization_barrier((x, y))[0]


def body(n_rep, n_exp, activations, kv_grad, errors, right_factor, hidden, out_grad, moment_one, moment_two):
    grads = {0: out_grad, 1: shift(out_grad, n_exp, 1)}
    if n_exp > 2:
        grads[n_exp - 1] = shift(out_grad, n_exp, -1)
    merged, lt = merge(activations, kv_grad, errors, right_factor.T)

    lt = (lt + swap(lt, "rep", n_rep, 1)).astype(BF16)
    slabs = unit_slabs(after(hidden, lt), n_exp)
    bit = 2
    parts = [lt]
    while bit < n_rep:
        while len(parts) > 1:
            parts = [a.astype(F32) + b.astype(F32) for a, b in zip(parts[0::2], parts[1::2])]
        own = parts[0].astype(BF16)
        masks = [bit] if 2 * bit >= n_rep else [bit, 2 * bit, 3 * bit]
        parts = [own] + [swap(own, "rep", n_rep, m) for m in masks]
        bit *= len(parts)
    lt, gram, chunks = right_product(parts, merged)

    rows = chunks.shape[0] * TILE_R // n_rep
    shares = lax.all_to_all(chunks.reshape(n_rep, rows, TILE_C), "rep", 0, 0, tiled=True)

    load = line_load(shares, gram)
    loads = [load] + [shift(load, n_exp, k) for k in range(1, n_exp)]
    loads, grads = lax.optimization_barrier((loads, grads))
    share, gram = line_sum(loads, gram.shape[0], n_rep)
    slabs = [slabs[0]] + [shift(after(slabs[k], share), n_exp, k) for k in range(1, n_exp)]
    w, basis = inverse_factor(gram, lt)
    chunks = lax.all_to_all(share, "rep", 0, 0, tiled=True).reshape(chunks.shape)

    left, right = 1, n_exp - 1
    while right - left > 1:
        if left <= n_exp - right:
            grads[left + 1] = shift(after(grads[left], share), n_exp, 1)
            left += 1
        else:
            grads[right - 1] = shift(after(grads[right], share), n_exp, -1)
            right -= 1

    new_right, new_error = finish(n_rep, w, chunks, basis, merged)
    first_new, second_new, step = expert_step(
        slabs, [grads[k] for k in range(n_exp)], moment_one, moment_two
    )
    return new_error, new_right.T, first_new, second_new, step


def solution(mesh):
    placed = (
        P("rep", "exp"),
        P("rep", None),
        P("rep", "exp", None),
        P(),
        P("rep", "exp", None),
        P("rep", "exp", None),
        P("rep", "exp", None),
        P("rep", "exp", None),
    )
    return jax.shard_map(
        functools.partial(body, mesh.shape["rep"], mesh.shape["exp"]),
        mesh=mesh,
        in_specs=placed,
        out_specs=(
            P("rep", "exp", None),
            P(),
            P("rep", "exp", None),
            P("rep", "exp", None),
            P("rep", "exp", None),
        ),
        check_vma=False,
    )
```
